32 devices in a mesh: group: 4 (over y, core), vocab: 8 (over z, x).
Axes of the slice: x: 2, y: 2, z: 4, core: 2. Of those that a mesh axis runs over, the one named last changes fastest.
Arguments:
- hidden: bfloat16 [2, 2048, 2304], P(None, ('group', 'vocab')), may hold values from -120 to 120
- head: bfloat16 [32768, 2304], P('vocab'), may hold values from -0.125 to 0.125
- factor_u: bfloat16 [32768, 64], P(('group', 'vocab')), may hold values from -0.29882812 to 0.29882812
- factor_v: bfloat16 [2304, 64], P('vocab'), may hold values from -0.125 to 0.125
- sampled: int32 [2, 2048], P(None, 'group'), may hold values from 0 to 32767
Outputs:
- logprob: float32 [2, 2048], P(None, 'group')
- log_total: float32 [2, 2048], P(None, 'group')
The draws below stay inside these ranges and needn't reach their ends.
All inputs are finite; a program needn't handle non-finite values.
Results may differ from the reference program's by a relative error of at most 0.00044.
Values may be sent and summed in bfloat16 or wider, within the bound.
No kernel may reach another device: no remote copies, remote signals or barrier semaphores. Data moves between devices by JAX's collectives and lax.ppermute only.
A program may use at most 128 MiB of HBM per device.

```python
import jax
import jax.numpy as jnp

D = 2304
RANK = 64
STEPS = 2
VOCAB = 32768
ROWS_ALL = 2048


def draw_hidden(key, part):
    key = jax.random.fold_in(key, 7)
    value_key = jax.random.fold_in(key, 1)
    values = 3.0 * jnp.clip(jax.random.normal(value_key, (STEPS, ROWS_ALL, D)), -8.0, 8.0)
    return values.astype(jnp.float32).astype(jnp.bfloat16)


def touch_ends(values, key, low, top_value):
    longest = values.shape.index(max(values.shape))
    spots = []
    for shift in (0, 1):
        where = [jax.random.randint(jax.random.fold_in(key, axis), (), 0, length) for axis, length in enumerate(values.shape)]
        where[longest] = (where[longest] + shift) % values.shape[longest]
        spots.append(tuple(where))
    return values.at[spots[0]].set(low).at[spots[1]].set(top_value)


def steps_of(key, dims, shards, smallest, high):
    gain, own = 1.0, jax.random.fold_in(key, 6)
    for dim, blocks in shards:
        heights = jnp.exp(jax.random.uniform(jax.random.fold_in(own, dim), (blocks,), jnp.float32, smallest / len(shards), high / len(shards)))
        gain = gain * jnp.repeat(heights, dims[dim] // blocks).reshape([-1 if axis == dim else 1 for axis in range(len(dims))])
    return gain


def noise(key, dims, scale, bound, shards=(), held_as=jnp.bfloat16):
    values = scale * jax.random.normal(key, dims, jnp.float32)
    if shards:
        values = values * steps_of(key, dims, shards, -0.22, 0.18)
    return jnp.clip(values, -bound, bound).astype(held_as)


def setup_inputs(seed: int = 0) -> dict:
    streams_of = jax.random.split(jax.random.key(seed), 6)
    hidden = draw_hidden(jax.random.fold_in(streams_of[5], 71), 0)
    head = noise(streams_of[1], (VOCAB, D), D ** -0.5, 0.125, ((0, 8),))
    factor_u = noise(streams_of[2], (VOCAB, RANK), 0.05, 0.29882812, ((0, 32),))
    factor_v = noise(streams_of[3], (D, RANK), D ** -0.5, 0.125, ((0, 8),))
    sampled = touch_ends(jax.random.randint(streams_of[4], (STEPS, ROWS_ALL), 0, VOCAB), jax.random.fold_in(streams_of[4], 1), 0, VOCAB - 1).astype(jnp.int32)
    return dict(hidden=hidden, head=head, factor_u=factor_u, factor_v=factor_v, sampled=sampled)


def reference(hidden, head, factor_u, factor_v, sampled):
    logprobs = []
    totals = []
    for step in range(STEPS):
        rows = hidden[step]
        base = jnp.dot(rows, head.T, preferred_element_type=jnp.float32)
        projected = jnp.dot(rows, factor_v, preferred_element_type=jnp.float32).astype(jnp.bfloat16)
        logits = base + jnp.dot(projected, factor_u.T, preferred_element_type=jnp.float32)
        top = jnp.max(logits, axis=1)
        total = jnp.sum(jnp.exp(logits - top[:, None]), axis=1)
        log_total = top + jnp.log(total)
        picked = jnp.take_along_axis(logits, sampled[step][:, None].astype(jnp.int32), axis=1)[:, 0]
        logprobs.append(picked - log_total)
        totals.append(log_total)
    return jnp.stack(logprobs), jnp.stack(totals)
```

```python
import jax
import jax.numpy as jnp
from jax import lax
from jax.experimental import pallas as pl
from jax.experimental.pallas import tpu as pltpu
from jax.sharding import PartitionSpec as P

VMEM_LIMIT = 40 * 1024 * 1024
NT = (((1,), (1,)), ((), ()))


def ring_order(n):
    if n % 2:
        return list(range(n))
    return [2 * i for i in range(n // 2)] + [2 * i + 1 for i in reversed(range(n // 2))]


def tile_rows(entries):
    for rows in (512, 256, 128, 64, 32, 16):
        if entries % rows == 0:
            return rows
    return entries


def make_assemble(n_u, n_v, u_rows, v_rows, rank):
    def kernel(place_ref, *refs):
        u_in = refs[:n_u]
        v_in = refs[n_u : n_u + n_v]
        u_out, v_out, v_wide = refs[n_u + n_v :]
        for k in range(n_u):
            start = pl.multiple_of(place_ref[k] * u_rows, u_rows)
            u_out[pl.ds(start, u_rows), :] = u_in[k][...]
        for k in range(n_v):
            v_wide[place_ref[n_u + k]] = v_in[k][...].astype(jnp.float32)
        v_out[...] = v_wide[...].reshape(n_v * v_rows, rank).astype(jnp.bfloat16)

    return pl.pallas_call(
        kernel,
        out_shape=(
            jax.ShapeDtypeStruct((n_u * u_rows, rank), jnp.bfloat16),
            jax.ShapeDtypeStruct((n_v * v_rows, rank), jnp.bfloat16),
        ),
        in_specs=[pl.BlockSpec(memory_space=pltpu.SMEM)]
        + [pl.BlockSpec(memory_space=pltpu.VMEM)] * (n_u + n_v),
        out_specs=(pl.BlockSpec(memory_space=pltpu.VMEM),) * 2,
        scratch_shapes=[pltpu.VMEM((n_v, v_rows, rank), jnp.float32)],
        compiler_params=pltpu.CompilerParams(vmem_limit_bytes=VMEM_LIMIT),
        name="assemble",
    )


def make_chunk(pieces, r, depth, entries, rank, n_voc):
    tile = tile_rows(entries)
    sub = min(tile, 256)
    steps = entries // tile
    n = pieces * r

    def kernel(src_ref, *refs):
        piece = refs[:pieces]
        head_ref, u_ref, v_ref, want_ref, out_ref, rows, proj, top, total, pick = refs[pieces:]
        i = pl.program_id(0)

        @pl.when(i == 0)
        def _():
            for k in range(pieces):
                rows[k * r : (k + 1) * r, :] = piece[k][...]
            proj[...] = jnp.dot(
                rows[...], v_ref[...], preferred_element_type=jnp.float32
            ).astype(jnp.bfloat16)
            top[...] = jnp.full(top.shape, -jnp.inf, jnp.float32)
            total[...] = jnp.zeros(total.shape, jnp.float32)
            pick[...] = jnp.zeros(pick.shape, jnp.float32)

        want = jnp.concatenate([want_ref[src_ref[0]], want_ref[src_ref[1]]], axis=1) - i * tile
        for j in range(tile // sub):
            span = slice(j * sub, (j + 1) * sub)
            x = lax.dot_general(head_ref[span, :], rows[...], NT, preferred_element_type=jnp.float32)
            x = x + lax.dot_general(u_ref[span, :], proj[...], NT, preferred_element_type=jnp.float32)
            entry = lax.broadcasted_iota(jnp.int32, (sub, n), 0) + j * sub
            hit = jnp.where(entry == want, x, 0.0)
            x3 = x.reshape(sub // 8, 8, n)
            new = jnp.maximum(top[...], jnp.max(x3, axis=0))
            total[...] = total[...] * jnp.exp(top[...] - new) + jnp.sum(jnp.exp(x3 - new[None]), axis=0)
            pick[...] = pick[...] + jnp.sum(hit.reshape(sub // 8, 8, n), axis=0)
            top[...] = new

        @pl.when(i == steps - 1)
        def _():
            best = jnp.max(top[...], axis=0, keepdims=True)
            out_ref[0:1, :] = best
            out_ref[1:2, :] = jnp.sum(total[...] * jnp.exp(top[...] - best), axis=0, keepdims=True)
            out_ref[2:3, :] = jnp.sum(pick[...], axis=0, keepdims=True)

    whole = pl.BlockSpec(memory_space=pltpu.VMEM)
    return pl.pallas_call(
        kernel,
        grid=(steps,),
        out_shape=jax.ShapeDtypeStruct((3, n), jnp.float32),
        in_specs=[pl.BlockSpec(memory_space=pltpu.SMEM)]
        + [whole] * pieces
        + [
            pl.BlockSpec((tile, depth), lambda i: (i, 0)),
            pl.BlockSpec((tile, rank), lambda i: (i, 0)),
            whole,
            whole,
        ],
        out_specs=whole,
        scratch_shapes=[
            pltpu.VMEM((n, depth), jnp.bfloat16),
            pltpu.VMEM((n, rank), jnp.bfloat16),
            pltpu.VMEM((8, n), jnp.float32),
            pltpu.VMEM((8, n), jnp.float32),
            pltpu.VMEM((8, n), jnp.float32),
        ],
        compiler_params=pltpu.CompilerParams(vmem_limit_bytes=VMEM_LIMIT),
        cost_estimate=pl.CostEstimate(
            flops=2 * n * entries * (depth + 256),
            bytes_accessed=2 * entries * (depth + 128),
            transcendentals=n * entries,
        ),
        name="chunk",
    )


def make_place(n_chunks, r, n_voc):
    def kernel(src_ref, *refs):
        out_ref = refs[-1]
        for c in range(n_chunks):
            for half in range(2):
                value = refs[c][:, half * 2 * r : (half + 1) * 2 * r]
                for q in range(3):
                    out_ref[q, pl.ds(src_ref[2 * c + half], 1), :] = value[q : q + 1]

    return pl.pallas_call(
        kernel,
        out_shape=jax.ShapeDtypeStruct((3, n_voc, 2 * r), jnp.float32),
        in_specs=[pl.BlockSpec(memory_space=pltpu.SMEM)]
        + [pl.BlockSpec(memory_space=pltpu.VMEM)] * n_chunks,
        out_specs=pl.BlockSpec(memory_space=pltpu.VMEM),
        name="place",
    )


def make_finish(r, n_voc):
    def kernel(src_ref, *refs):
        stats = refs[:n_voc]
        prob_ref, log_ref, held = refs[n_voc:]
        for k in range(n_voc):
            held[src_ref[k]] = stats[k][...]
        top = held[0, 0]
        for k in range(1, n_voc):
            top = jnp.maximum(top, held[k, 0])
        total = jnp.zeros_like(top)
        pick = jnp.zeros_like(top)
        for k in range(n_voc):
            total = total + held[k, 1] * jnp.exp(held[k, 0] - top)
            pick = pick + held[k, 2]
        log_total = top + jnp.log(total)
        prob = pick - log_total
        for k in range(n_voc):
            for s in range(2):
                log_ref[s : s + 1, k * r : (k + 1) * r] = log_total[k : k + 1, s * r : (s + 1) * r]
                prob_ref[s : s + 1, k * r : (k + 1) * r] = prob[k : k + 1, s * r : (s + 1) * r]

    shape = jax.ShapeDtypeStruct((2, n_voc * r), jnp.float32)
    return pl.pallas_call(
        kernel,
        out_shape=(shape, shape),
        in_specs=[pl.BlockSpec(memory_space=pltpu.SMEM)]
        + [pl.BlockSpec(memory_space=pltpu.VMEM)] * n_voc,
        out_specs=(pl.BlockSpec(memory_space=pltpu.VMEM),) * 2,
        scratch_shapes=[pltpu.VMEM((n_voc, 3, n_voc, 2 * r), jnp.float32)],
        name="finish",
    )


def body(hidden, head, factor_u, factor_v, sampled):
    n_group = lax.axis_size("group")
    n_voc = lax.axis_size("vocab")
    group = lax.axis_index("group")
    voc = lax.axis_index("vocab")
    _, r, depth = hidden.shape
    entries = head.shape[0]
    rank = factor_u.shape[1]

    order = ring_order(n_voc)
    ahead = [(order[i], order[(i + 1) % n_voc]) for i in range(n_voc)]
    behind = [(b, a) for a, b in ahead]
    ring = jnp.array(order, jnp.int32)
    position = jnp.array([order.index(v) for v in range(n_voc)], jnp.int32)[voc]

    half = n_voc // 2
    own = [hidden[0], hidden[1]]
    up = {0: own}
    down = {0: own}
    for hop in range(1, half):
        up[hop] = [lax.ppermute(x, "vocab", ahead) for x in up[hop - 1]]
        down[hop] = [lax.ppermute(x, "vocab", behind) for x in down[hop - 1]]
    last = [
        lax.ppermute(up[half - 1][0], "vocab", ahead),
        lax.ppermute(down[half - 1][1], "vocab", behind),
    ]

    moves = [
        (v * n_group + g, g * n_voc + v) for v in range(n_voc) for g in range(n_group)
    ]
    mine = lax.ppermute(factor_u, ("group", "vocab"), moves)
    u_parts = [mine]
    for k in range(1, n_group):
        u_parts.append(
            lax.ppermute(mine, "group", [((g + k) % n_group, g) for g in range(n_group)])
        )
    v_parts = [factor_v]
    for k in range(1, n_voc):
        v_parts.append(
            lax.ppermute(factor_v, "vocab", [((v + k) % n_voc, v) for v in range(n_voc)])
        )
    place = jnp.concatenate(
        [
            (group + jnp.arange(n_group, dtype=jnp.int32)) % n_group,
            (voc + jnp.arange(n_voc, dtype=jnp.int32)) % n_voc,
        ]
    )
    full_u, full_v = make_assemble(n_group, n_voc, mine.shape[0], factor_v.shape[0], rank)(
        place, *u_parts, *v_parts
    )

    want = sampled - voc * entries
    want = want.reshape(2, n_voc, r).transpose(1, 0, 2).reshape(n_voc, 1, 2 * r)
    chunk = make_chunk(4, r, depth, entries, rank, n_voc)
    stats = []
    sources = []
    for hop in range(1, half + 1):
        if hop < half:
            rows = up[hop] + down[hop]
            src = ring[jnp.stack([(position - hop) % n_voc, (position + hop) % n_voc])]
        else:
            rows = own + last
            src = ring[jnp.stack([position, (position + half) % n_voc])]
        stats.append(chunk(src, *rows, head, full_u, full_v, want))
        sources.append(src)
    part = make_place(half, r, n_voc)(jnp.concatenate(sources), *stats)
    parts = [part]
    for k in range(1, n_voc):
        parts.append(
            lax.ppermute(part, "vocab", [((v + k) % n_voc, v) for v in range(n_voc)])
        )
    from_whom = (voc + jnp.arange(n_voc, dtype=jnp.int32)) % n_voc
    return make_finish(r, n_voc)(from_whom, *parts)


def solution(mesh):
    in_specs = (
        P(None, ("group", "vocab"), None),
        P("vocab", None),
        P(("group", "vocab"), None),
        P("vocab", None),
        P(None, "group"),
    )
    out_specs = (P(None, "group"), P(None, "group"))
    return jax.shard_map(body, mesh=mesh, in_specs=in_specs, out_specs=out_specs, check_vma=False)
```

```python
import jax
import jax.numpy as jnp
from jax import lax
from jax.experimental import pallas as pl
from jax.experimental.pallas import tpu as pltpu
from jax.sharding import PartitionSpec as P

VMEM_LIMIT = 48 * 1024 * 1024
LANES = 128
WHOLE = pl.BlockSpec(memory_space=pltpu.VMEM)


def ring_order(n):
    return [2 * i for i in range(n // 2)] + [2 * i + 1 for i in reversed(range(n // 2))]


def ring_position(device, n):
    return jnp.where(device % 2 == 0, device // 2, n - 1 - device // 2)


def ring_device(position, n):
    position = lax.rem(position + n, n)
    return jnp.where(position < n // 2, 2 * position, 2 * (n - 1 - position) + 1)


def tile_rows(entries):
    for rows in (512, 256, 128, 64, 32, 16):
        if entries % (2 * rows) == 0:
            return rows
    raise ValueError(entries)


def padded(size):
    return -(-size // LANES) * LANES


def make_assemble(n_group, n_voc, u_rows, v_rows, rank, r, entries):
    per = n_voc // n_group
    wide = padded(v_rows)

    def kernel(sampled_ref, *refs):
        packs = refs[:n_group]
        u_out, v_out, want_out, v_wide = refs[n_group:]
        group = lax.axis_index("group")
        voc = lax.axis_index("vocab")
        for k in range(n_group):
            member = group ^ k
            start = pl.multiple_of(member * u_rows, u_rows)
            u_out[pl.ds(start, u_rows), :] = packs[k][:, :u_rows].T
            for t in range(per):
                shard = member * per + lax.rem(t + voc // n_group, per)
                at = u_rows + t * wide
                block = packs[k][:, at : at + wide].astype(jnp.float32).T
                v_wide[pl.ds(pl.multiple_of(shard * v_rows, 8), v_rows), :] = block[:v_rows]
        v_out[...] = v_wide[...].T.astype(jnp.bfloat16)
        for k in range(n_voc):
            for s in range(2):
                want_out[k, :, s * r : (s + 1) * r] = (
                    sampled_ref[s : s + 1, k * r : (k + 1) * r] - voc * entries
                )

    return pl.pallas_call(
        kernel,
        out_shape=(
            jax.ShapeDtypeStruct((n_group * u_rows, rank), jnp.bfloat16),
            jax.ShapeDtypeStruct((rank, n_voc * v_rows), jnp.bfloat16),
            jax.ShapeDtypeStruct((n_voc, 1, 2 * r), jnp.int32),
        ),
        in_specs=[WHOLE] * (1 + n_group),
        out_specs=(WHOLE,) * 3,
        scratch_shapes=[pltpu.VMEM((n_voc * v_rows, rank), jnp.float32)],
        compiler_params=pltpu.CompilerParams(vmem_limit_bytes=VMEM_LIMIT),
        name="assemble",
    )


def sources_of(hop, n_voc):
    position = ring_position(lax.axis_index("vocab"), n_voc)
    if hop < n_voc // 2:
        return ring_device(position - hop, n_voc), ring_device(position + hop, n_voc)
    return ring_device(position, n_voc), ring_device(position + hop, n_voc)


def make_chunk(hop, pieces, r, depth, entries, rank, n_voc):
    tile = tile_rows(entries)
    tiles = entries // tile
    n = 4 * r
    last = hop == n_voc // 2
    earlier = hop - 1 if last else 0

    def kernel(*refs):
        piece = refs[:pieces]
        head_ref, u_ref, v_ref, want_ref = refs[pieces : pieces + 4]
        before = refs[pieces + 4 : pieces + 4 + earlier]
        out_ref, held, rows, proj, first, second, top, total, pick, sems = refs[
            pieces + 4 + earlier :
        ]

        def fetch(t, slot):
            return pltpu.make_async_copy(
                head_ref.at[pl.ds(pl.multiple_of(t * tile, tile), tile), :],
                held.at[slot],
                sems.at[slot],
            )

        for t in range(min(4, tiles)):
            fetch(t, t).start()
        at = 0
        for ref in piece:
            block = ref[...].reshape(-1, depth)
            rows[:, at : at + block.shape[0]] = block.T
            at += block.shape[0]
        proj[...] = jnp.dot(v_ref[...], rows[...], preferred_element_type=jnp.float32).astype(
            jnp.bfloat16
        )
        top[...] = jnp.full(top.shape, -1e30, jnp.float32)
        second[...] = jnp.full(second.shape, -1e30, jnp.float32)
        total[...] = jnp.zeros(total.shape, jnp.float32)
        pick[...] = jnp.zeros(pick.shape, jnp.float32)
        left, right = sources_of(hop, n_voc)
        want = jnp.concatenate([want_ref[left], want_ref[right]], axis=1)

        def multiply(t, slot, into):
            u_tile = u_ref[pl.ds(pl.multiple_of(t * tile, tile), tile), :]
            into[...] = jnp.dot(
                held[slot], rows[...], preferred_element_type=jnp.float32
            ) + jnp.dot(u_tile, proj[...], preferred_element_type=jnp.float32)

        def reduce(start, values):
            x = values[...]
            entry = lax.broadcasted_iota(jnp.int32, (tile, n), 0)
            hit = jnp.where(entry == want - start, x, 0.0)
            x3 = x.reshape(tile // 8, 8, n)
            new = jnp.maximum(top[...], jnp.max(x3, axis=0))
            total[...] = total[...] * jnp.exp(top[...] - new) + jnp.sum(
                jnp.exp(x3 - new[None]), axis=0
            )
            pick[...] = pick[...] + jnp.sum(hit.reshape(tile // 8, 8, n), axis=0)
            top[...] = new

        @pl.loop(0, tiles // 2)
        def _(i):
            slot = 2 * lax.rem(i, 2)
            fetch(2 * i, slot).wait()
            multiply(2 * i, slot, first)
            reduce(jnp.where(i == 0, 1 << 29, (2 * i - 1) * tile), second)
            fetch(2 * i + 1, slot + 1).wait()
            multiply(2 * i + 1, slot + 1, second)
            reduce(2 * i * tile, first)

            @pl.when(2 * i + 4 < tiles)
            def _():
                fetch(2 * i + 4, slot).start()
                fetch(2 * i + 5, slot + 1).start()

        reduce(entries - tile, second)
        best = jnp.max(top[...], axis=0, keepdims=True)
        sums = jnp.sum(total[...] * jnp.exp(top[...] - best), axis=0, keepdims=True)
        picked = jnp.sum(pick[...], axis=0, keepdims=True)
        if not last:
            for q, value in enumerate((best, sums, picked)):
                out_ref[q : q + 1, :] = value
            return
        for q, value in enumerate((best, sums, picked)):
            out_ref[q, pl.ds(left, 1), :] = value[:, : 2 * r]
            out_ref[q, pl.ds(right, 1), :] = value[:, 2 * r :]
            for k in range(1, hop):
                a, b = sources_of(k, n_voc)
                out_ref[q, pl.ds(a, 1), :] = before[k - 1][q : q + 1, : 2 * r]
                out_ref[q, pl.ds(b, 1), :] = before[k - 1][q : q + 1, 2 * r :]

    return pl.pallas_call(
        kernel,
        out_shape=jax.ShapeDtypeStruct((3, n_voc, 2 * r) if last else (3, n), jnp.float32),
        in_specs=[WHOLE] * pieces
        + [pl.BlockSpec(memory_space=pl.ANY)]
        + [WHOLE] * (3 + earlier),
        out_specs=WHOLE,
        scratch_shapes=[
            pltpu.VMEM((4, tile, depth), jnp.bfloat16),
            pltpu.VMEM((depth, n), jnp.bfloat16),
            pltpu.VMEM((rank, n), jnp.bfloat16),
            pltpu.VMEM((tile, n), jnp.float32),
            pltpu.VMEM((tile, n), jnp.float32),
            pltpu.VMEM((8, n), jnp.float32),
            pltpu.VMEM((8, n), jnp.float32),
            pltpu.VMEM((8, n), jnp.float32),
            pltpu.SemaphoreType.DMA((4,)),
        ],
        compiler_params=pltpu.CompilerParams(vmem_limit_bytes=VMEM_LIMIT),
        cost_estimate=pl.CostEstimate(
            flops=2 * n * entries * (depth + 256),
            bytes_accessed=2 * entries * (depth + LANES),
            transcendentals=n * entries,
        ),
        name="chunk",
    )


def make_combine(bit, r, n_voc, finish):
    def kernel(mine_ref, other_ref, *outs):
        high = (lax.axis_index("vocab") & bit) != 0
        low = [jnp.where(high, other_ref[q], mine_ref[q]) for q in range(3)]
        up = [jnp.where(high, mine_ref[q], other_ref[q]) for q in range(3)]
        top = jnp.maximum(low[0], up[0])
        total = low[1] * jnp.exp(low[0] - top) + up[1] * jnp.exp(up[0] - top)
        pick = low[2] + up[2]
        if not finish:
            for q, value in enumerate((top, total, pick)):
                outs[0][q] = value
            return
        log_total = top + jnp.log(total)
        for ref, value in zip(outs, (pick - log_total, log_total)):
            for k in range(n_voc):
                for s in range(2):
                    ref[s : s + 1, k * r : (k + 1) * r] = value[k : k + 1, s * r : (s + 1) * r]

    if finish:
        shape = (jax.ShapeDtypeStruct((2, n_voc * r), jnp.float32),) * 2
        specs = (WHOLE, WHOLE)
    else:
        shape, specs = jax.ShapeDtypeStruct((3, n_voc, 2 * r), jnp.float32), WHOLE
    return pl.pallas_call(
        kernel, out_shape=shape, in_specs=[WHOLE, WHOLE], out_specs=specs, name="combine"
    )


def body(hidden, head, factor_u, factor_v, sampled):
    n_group = lax.axis_size("group")
    n_voc = lax.axis_size("vocab")
    _, r, depth = hidden.shape
    entries = head.shape[0]
    rank = factor_u.shape[1]
    per = n_voc // n_group
    half = n_voc // 2

    order = ring_order(n_voc)
    ahead = [(order[i], order[(i + 1) % n_voc]) for i in range(n_voc)]
    behind = [(b, a) for a, b in ahead]

    def trade(x, axis, size, bit):
        return lax.ppermute(x, axis, [(i, i ^ bit) for i in range(size)])

    up, down = [hidden], [hidden]
    for hop in range(1, half):
        up.append(lax.ppermute(up[-1], "vocab", ahead))
        down.append(lax.ppermute(down[-1], "vocab", behind))
    ends = [
        lax.ppermute(up[-1][0], "vocab", ahead),
        lax.ppermute(down[-1][1], "vocab", behind),
    ]

    moves = [(v * n_group + g, g * n_voc + v) for v in range(n_voc) for g in range(n_group)]
    pack = [lax.ppermute(factor_u.T, ("group", "vocab"), moves)]
    for t in range(per):
        moves = [
            (
                (v % n_group) * n_voc + g * per + (t + v // n_group) % per,
                g * n_voc + v,
            )
            for v in range(n_voc)
            for g in range(n_group)
        ]
        shard = lax.ppermute(factor_v.T, ("group", "vocab"), moves)
        pack.append(jnp.pad(shard, ((0, 0), (0, padded(shard.shape[1]) - shard.shape[1]))))
    packs = {0: jnp.concatenate(pack, axis=1)}
    bit = n_group // 2
    while bit:
        for k in list(packs):
            packs[k ^ bit] = trade(packs[k], "group", n_group, bit)
        bit //= 2
    full_u, full_v, want = make_assemble(
        n_group, n_voc, factor_u.shape[0], factor_v.shape[0], rank, r, entries
    )(sampled, *[packs[k] for k in range(n_group)])

    stats = []
    for hop in range(1, half + 1):
        pieces = [up[hop], down[hop]] if hop < half else [hidden] + ends
        chunk = make_chunk(hop, len(pieces), r, depth, entries, rank, n_voc)
        before = stats if hop == half else []
        stats.append(chunk(*pieces, head, full_u, full_v, want, *before))
    part = stats[-1]
    bit = 1
    while bit < n_voc:
        other = trade(part, "vocab", n_voc, bit)
        part = make_combine(bit, r, n_voc, 2 * bit == n_voc)(part, other)
        bit *= 2
    return part


def solution(mesh):
    in_specs = (
        P(None, ("group", "vocab"), None),
        P("vocab", None),
        P(("group", "vocab"), None),
        P("vocab", None),
        P(None, "group"),
    )
    out_specs = (P(None, "group"), P(None, "group"))
    return jax.shard_map(body, mesh=mesh, in_specs=in_specs, out_specs=out_specs, check_vma=False)
```

```python
import jax
import jax.numpy as jnp
from jax import lax
from jax.experimental import pallas as pl
from jax.experimental.pallas import tpu as pltpu
from jax.sharding import PartitionSpec as P

VMEM_LIMIT = 30 * 1024 * 1024
LANES = 128
WHOLE = pl.BlockSpec(memory_space=pltpu.VMEM)


def ring_order(n):
    return [2 * i for i in range(n // 2)] + [2 * i + 1 for i in reversed(range(n // 2))]


def ring_position(device, n):
    return jnp.where(device % 2 == 0, device // 2, n - 1 - device // 2)


def ring_device(position, n):
    position = lax.rem(position + n, n)
    return jnp.where(position < n // 2, 2 * position, 2 * (n - 1 - position) + 1)


def tile_rows(entries):
    for rows in (512, 256, 128, 64, 32, 16):
        if entries % (2 * rows) == 0:
            return rows
    raise ValueError(entries)


def padded(size):
    return -(-size // LANES) * LANES


def make_assemble(n_group, n_voc, u_rows, v_rows, rank, r, entries):
    per = n_voc // n_group
    wide = padded(v_rows)

    def kernel(sampled_ref, *refs):
        packs = refs[:n_group]
        u_out, v_out, want_out, v_wide = refs[n_group:]
        group = lax.axis_index("group")
        voc = lax.axis_index("vocab")
        for k in range(n_group):
            member = group ^ k
            start = pl.multiple_of(member * u_rows, u_rows)
            u_out[pl.ds(start, u_rows), :] = packs[k][:, :u_rows].T
            for t in range(per):
                shard = member * per + lax.rem(t + voc // n_group, per)
                at = u_rows + t * wide
                block = packs[k][:, at : at + wide].astype(jnp.float32).T
                v_wide[pl.ds(pl.multiple_of(shard * v_rows, 8), v_rows), :] = block[:v_rows]
        v_out[...] = v_wide[...].T.astype(jnp.bfloat16)
        for k in range(n_voc):
            for s in range(2):
                want_out[k, :, s * r : (s + 1) * r] = (
                    sampled_ref[s : s + 1, k * r : (k + 1) * r] - voc * entries
                )

    return pl.pallas_call(
        kernel,
        out_shape=(
            jax.ShapeDtypeStruct((n_group * u_rows, rank), jnp.bfloat16),
            jax.ShapeDtypeStruct((rank, n_voc * v_rows), jnp.bfloat16),
            jax.ShapeDtypeStruct((n_voc, 1, 2 * r), jnp.int32),
        ),
        in_specs=[WHOLE] * (1 + n_group),
        out_specs=(WHOLE,) * 3,
        scratch_shapes=[pltpu.VMEM((n_voc * v_rows, rank), jnp.float32)],
        compiler_params=pltpu.CompilerParams(vmem_limit_bytes=VMEM_LIMIT),
        name="assemble",
    )


def sources_of(hop, n_voc):
    position = ring_position(lax.axis_index("vocab"), n_voc)
    if hop < n_voc // 2:
        return ring_device(position - hop, n_voc), ring_device(position + hop, n_voc)
    return ring_device(position, n_voc), ring_device(position + hop, n_voc)


def make_chunk(hop, pieces, r, depth, entries, rank, n_voc):
    tile = tile_rows(entries)
    tiles = entries // tile
    n = 4 * r
    last = hop == n_voc // 2
    earlier = hop - 1 if last else 0

    def kernel(*refs):
        piece = refs[:pieces]
        head_ref, u_ref, v_ref, want_ref = refs[pieces : pieces + 4]
        before = refs[pieces + 4 : pieces + 4 + earlier]
        out_ref, rows, proj, first, second, top, total, pick = refs[
            pieces + 4 + earlier :
        ]

        at = 0
        for ref in piece:
            block = ref[...].reshape(-1, depth)
            rows[:, at : at + block.shape[0]] = block.T
            at += block.shape[0]
        proj[...] = jnp.dot(v_ref[...], rows[...], preferred_element_type=jnp.float32).astype(
            jnp.bfloat16
        )
        top[...] = jnp.full(top.shape, -1e30, jnp.float32)
        second[...] = jnp.full(second.shape, -1e30, jnp.float32)
        total[...] = jnp.zeros(total.shape, jnp.float32)
        pick[...] = jnp.zeros(pick.shape, jnp.float32)
        left, right = sources_of(hop, n_voc)
        want = jnp.concatenate([want_ref[left], want_ref[right]], axis=1)

        def multiply(t, into):
            span = pl.ds(pl.multiple_of(t * tile, tile), tile)
            into[...] = jnp.dot(
                head_ref[span, :], rows[...], preferred_element_type=jnp.float32
            ) + jnp.dot(u_ref[span, :], proj[...], preferred_element_type=jnp.float32)

        def reduce(start, values):
            x = values[...]
            entry = lax.broadcasted_iota(jnp.int32, (tile, n), 0)
            hit = jnp.where(entry == want - start, x, 0.0)
            x3 = x.reshape(tile // 8, 8, n)
            new = jnp.maximum(top[...], jnp.max(x3, axis=0))
            total[...] = total[...] * jnp.exp(top[...] - new) + jnp.sum(
                jnp.exp(x3 - new[None]), axis=0
            )
            pick[...] = pick[...] + jnp.sum(hit.reshape(tile // 8, 8, n), axis=0)
            top[...] = new

        @pl.loop(0, tiles // 2)
        def _(i):
            multiply(2 * i, first)
            reduce(jnp.where(i == 0, 1 << 29, (2 * i - 1) * tile), second)
            multiply(2 * i + 1, second)
            reduce(2 * i * tile, first)

        reduce(entries - tile, second)
        best = jnp.max(top[...], axis=0, keepdims=True)
        sums = jnp.sum(total[...] * jnp.exp(top[...] - best), axis=0, keepdims=True)
        picked = jnp.sum(pick[...], axis=0, keepdims=True)
        if not last:
            for q, value in enumerate((best, sums, picked)):
                out_ref[q : q + 1, :] = value
            return
        for q, value in enumerate((best, sums, picked)):
            out_ref[q, pl.ds(left, 1), :] = value[:, : 2 * r]
            out_ref[q, pl.ds(right, 1), :] = value[:, 2 * r :]
            for k in range(1, hop):
                a, b = sources_of(k, n_voc)
                out_ref[q, pl.ds(a, 1), :] = before[k - 1][q : q + 1, : 2 * r]
                out_ref[q, pl.ds(b, 1), :] = before[k - 1][q : q + 1, 2 * r :]

    return pl.pallas_call(
        kernel,
        out_shape=jax.ShapeDtypeStruct((3, n_voc, 2 * r) if last else (3, n), jnp.float32),
        in_specs=[WHOLE] * (pieces + 4 + earlier),
        out_specs=WHOLE,
        scratch_shapes=[
            pltpu.VMEM((depth, n), jnp.bfloat16),
            pltpu.VMEM((rank, n), jnp.bfloat16),
            pltpu.VMEM((tile, n), jnp.float32),
            pltpu.VMEM((tile, n), jnp.float32),
            pltpu.VMEM((8, n), jnp.float32),
            pltpu.VMEM((8, n), jnp.float32),
            pltpu.VMEM((8, n), jnp.float32),
        ],
        compiler_params=pltpu.CompilerParams(vmem_limit_bytes=VMEM_LIMIT),
        cost_estimate=pl.CostEstimate(
            flops=2 * n * entries * (depth + 256),
            bytes_accessed=2 * entries * (depth + LANES),
            transcendentals=n * entries,
        ),
        name="chunk",
    )


def make_combine(bit, r, n_voc, finish):
    def kernel(mine_ref, other_ref, *outs):
        high = (lax.axis_index("vocab") & bit) != 0
        low = [jnp.where(high, other_ref[q], mine_ref[q]) for q in range(3)]
        up = [jnp.where(high, mine_ref[q], other_ref[q]) for q in range(3)]
        top = jnp.maximum(low[0], up[0])
        total = low[1] * jnp.exp(low[0] - top) + up[1] * jnp.exp(up[0] - top)
        pick = low[2] + up[2]
        if not finish:
            for q, value in enumerate((top, total, pick)):
                outs[0][q] = value
            return
        log_total = top + jnp.log(total)
        for ref, value in zip(outs, (pick - log_total, log_total)):
            for k in range(n_voc):
                for s in range(2):
                    ref[s : s + 1, k * r : (k + 1) * r] = value[k : k + 1, s * r : (s + 1) * r]

    if finish:
        shape = (jax.ShapeDtypeStruct((2, n_voc * r), jnp.float32),) * 2
        specs = (WHOLE, WHOLE)
    else:
        shape, specs = jax.ShapeDtypeStruct((3, n_voc, 2 * r), jnp.float32), WHOLE
    return pl.pallas_call(
        kernel, out_shape=shape, in_specs=[WHOLE, WHOLE], out_specs=specs, name="combine"
    )


def body(hidden, head, factor_u, factor_v, sampled):
    n_group = lax.axis_size("group")
    n_voc = lax.axis_size("vocab")
    _, r, depth = hidden.shape
    entries = head.shape[0]
    rank = factor_u.shape[1]
    per = n_voc // n_group
    half = n_voc // 2

    order = ring_order(n_voc)
    ahead = [(order[i], order[(i + 1) % n_voc]) for i in range(n_voc)]
    behind = [(b, a) for a, b in ahead]

    def trade(x, axis, size, bit):
        return lax.ppermute(x, axis, [(i, i ^ bit) for i in range(size)])

    up, down = [hidden], [hidden]
    for hop in range(1, half):
        up.append(lax.ppermute(up[-1], "vocab", ahead))
        down.append(lax.ppermute(down[-1], "vocab", behind))
    ends = [
        lax.ppermute(up[-1][0], "vocab", ahead),
        lax.ppermute(down[-1][1], "vocab", behind),
    ]

    moves = [(v * n_group + g, g * n_voc + v) for v in range(n_voc) for g in range(n_group)]
    pack = [lax.ppermute(factor_u.T, ("group", "vocab"), moves)]
    for t in range(per):
        moves = [
            (
                (v % n_group) * n_voc + g * per + (t + v // n_group) % per,
                g * n_voc + v,
            )
            for v in range(n_voc)
            for g in range(n_group)
        ]
        shard = lax.ppermute(factor_v.T, ("group", "vocab"), moves)
        pack.append(jnp.pad(shard, ((0, 0), (0, padded(shard.shape[1]) - shard.shape[1]))))
    packs = {0: jnp.concatenate(pack, axis=1)}
    bit = n_group // 2
    while bit:
        for k in list(packs):
            packs[k ^ bit] = trade(packs[k], "group", n_group, bit)
        bit //= 2
    full_u, full_v, want = make_assemble(
        n_group, n_voc, factor_u.shape[0], factor_v.shape[0], rank, r, entries
    )(sampled, *[packs[k] for k in range(n_group)])

    stats = []
    for hop in range(1, half + 1):
        pieces = [up[hop], down[hop]] if hop < half else [hidden] + ends
        chunk = make_chunk(hop, len(pieces), r, depth, entries, rank, n_voc)
        before = stats if hop == half else []
        stats.append(chunk(*pieces, head, full_u, full_v, want, *before))
    part = stats[-1]
    bit = 1
    while bit < n_voc:
        other = trade(part, "vocab", n_voc, bit)
        part = make_combine(bit, r, n_voc, 2 * bit == n_voc)(part, other)
        bit *= 2
    return part


def solution(mesh):
    in_specs = (
        P(None, ("group", "vocab"), None),
        P("vocab", None),
        P(("group", "vocab"), None),
        P("vocab", None),
        P(None, "group"),
    )
    out_specs = (P(None, "group"), P(None, "group"))
    return jax.shard_map(body, mesh=mesh, in_specs=in_specs, out_specs=out_specs, check_vma=False)
```

```python
import jax
import jax.numpy as jnp
from jax import lax
from jax.experimental import pallas as pl
from jax.experimental.pallas import tpu as pltpu
from jax.sharding import PartitionSpec as P

MIB = 1024 * 1024
LANES = 128
WHOLE = pl.BlockSpec(memory_space=pltpu.VMEM)


def ring_order(n):
    return [2 * i for i in range(n // 2)] + [2 * i + 1 for i in reversed(range(n // 2))]


def ring_position(device, n):
    return jnp.where(device % 2 == 0, device // 2, n - 1 - device // 2)


def ring_device(position, n):
    position = lax.rem(position + n, n)
    return jnp.where(position < n // 2, 2 * position, 2 * (n - 1 - position) + 1)


def tile_rows(entries):
    for rows in (512, 256, 128, 64, 32, 16):
        if entries % (2 * rows) == 0:
            return rows
    raise ValueError(entries)


def padded(size):
    return -(-size // LANES) * LANES


def make_assemble(n_group, n_voc, u_rows, v_rows, rank, r, entries):
    per = n_voc // n_group
    wide = padded(v_rows)

    def kernel(sampled_ref, *refs):
        packs = refs[:n_group]
        u_out, v_out, want_out, v_wide = refs[n_group:]
        group = lax.axis_index("group")
        voc = lax.axis_index("vocab")
        for k in range(n_group):
            member = group ^ k
            start = pl.multiple_of(member * u_rows, u_rows)
            u_out[pl.ds(start, u_rows), :] = packs[k][:, :u_rows].T
            for t in range(per):
                shard = n_group * (lax.rem(voc, per) ^ t) + member
                at = u_rows + t * wide
                block = packs[k][:, at : at + wide].astype(jnp.float32).T
                v_wide[pl.ds(pl.multiple_of(shard * v_rows, 8), v_rows), :] = block[:v_rows]
        v_out[...] = v_wide[...].T.astype(jnp.bfloat16)
        for k in range(n_voc):
            for s in range(2):
                want_out[k, :, s * r : (s + 1) * r] = (
                    sampled_ref[s : s + 1, k * r : (k + 1) * r] - voc * entries
                )

    return pl.pallas_call(
        kernel,
        out_shape=(
            jax.ShapeDtypeStruct((n_group * u_rows, rank), jnp.bfloat16),
            jax.ShapeDtypeStruct((rank, n_voc * v_rows), jnp.bfloat16),
            jax.ShapeDtypeStruct((n_voc, 1, 2 * r), jnp.int32),
        ),
        in_specs=[WHOLE] * (1 + n_group),
        out_specs=(WHOLE,) * 3,
        scratch_shapes=[pltpu.VMEM((n_voc * v_rows, rank), jnp.float32)],
        compiler_params=pltpu.CompilerParams(vmem_limit_bytes=4 * MIB),
        name="assemble",
    )


def sources_of(hop, n_voc):
    position = ring_position(lax.axis_index("vocab"), n_voc)
    if hop < n_voc // 2:
        return ring_device(position - hop, n_voc), ring_device(position + hop, n_voc)
    return ring_device(position, n_voc), ring_device(position + hop, n_voc)


def make_chunk(hop, pieces, r, depth, entries, rank, n_voc):
    tile = tile_rows(entries)
    tiles = entries // tile
    n = 4 * r
    first, last = hop == 1, hop == n_voc // 2
    earlier = hop - 1 if last else 0
    parts = 16 if entries % 4096 == 0 else tiles
    part = entries // parts

    def kernel(*refs):
        piece = refs[:pieces]
        head_ref, u_ref, v_ref, want_ref = refs[pieces : pieces + 4]
        before = refs[pieces + 4 : pieces + 4 + earlier]
        out_ref, *rest = refs[pieces + 4 + earlier :]
        held = head_ref
        if first:
            held, *rest, sems = rest
        rows, proj, even, odd, top, total, pick = rest

        def fetch(t):
            span = pl.ds(pl.multiple_of(t * part, part), part)
            return pltpu.make_async_copy(head_ref.at[span, :], held.at[span, :], sems.at[t])

        if first:
            for t in range(parts):
                fetch(t).start()

        at = 0
        for ref in piece:
            block = ref[...].reshape(-1, depth)
            rows[:, at : at + block.shape[0]] = block.T
            at += block.shape[0]
        proj[...] = jnp.dot(v_ref[...], rows[...], preferred_element_type=jnp.float32).astype(
            jnp.bfloat16
        )
        top[...] = jnp.full(top.shape, -1e30, jnp.float32)
        odd[...] = jnp.full(odd.shape, -1e30, jnp.float32)
        total[...] = jnp.zeros(total.shape, jnp.float32)
        pick[...] = jnp.zeros(pick.shape, jnp.float32)
        left, right = sources_of(hop, n_voc)
        want = jnp.concatenate([want_ref[left], want_ref[right]], axis=1)

        def multiply(t, into):
            if first:
                for k in range(parts // tiles):
                    fetch(t * (parts // tiles) + k).wait()
            span = pl.ds(pl.multiple_of(t * tile, tile), tile)
            into[...] = jnp.dot(
                held[span, :], rows[...], preferred_element_type=jnp.float32
            ) + jnp.dot(u_ref[span, :], proj[...], preferred_element_type=jnp.float32)

        def reduce(start, values):
            x = values[...]
            entry = lax.broadcasted_iota(jnp.int32, (tile, n), 0)
            hit = jnp.where(entry == want - start, x, 0.0)
            x3 = x.reshape(tile // 8, 8, n)
            new = jnp.maximum(top[...], jnp.max(x3, axis=0))
            total[...] = total[...] * jnp.exp(top[...] - new) + jnp.sum(
                jnp.exp(x3 - new[None]), axis=0
            )
            pick[...] = pick[...] + jnp.sum(hit.reshape(tile // 8, 8, n), axis=0)
            top[...] = new

        @pl.loop(0, tiles // 2)
        def _(i):
            multiply(2 * i, even)
            reduce(jnp.where(i == 0, 1 << 29, (2 * i - 1) * tile), odd)
            multiply(2 * i + 1, odd)
            reduce(2 * i * tile, even)

        reduce(entries - tile, odd)
        best = jnp.max(top[...], axis=0, keepdims=True)
        sums = jnp.sum(total[...] * jnp.exp(top[...] - best), axis=0, keepdims=True)
        picked = jnp.sum(pick[...], axis=0, keepdims=True)
        if not last:
            for q, value in enumerate((best, sums, picked)):
                out_ref[q : q + 1, :] = value
            return
        for q, value in enumerate((best, sums, picked)):
            out_ref[q, pl.ds(left, 1), :] = value[:, : 2 * r]
            out_ref[q, pl.ds(right, 1), :] = value[:, 2 * r :]
            for k in range(1, hop):
                a, b = sources_of(k, n_voc)
                out_ref[q, pl.ds(a, 1), :] = before[k - 1][q : q + 1, : 2 * r]
                out_ref[q, pl.ds(b, 1), :] = before[k - 1][q : q + 1, 2 * r :]

    out_shape = jax.ShapeDtypeStruct((3, n_voc, 2 * r) if last else (3, n), jnp.float32)
    out_specs = WHOLE
    scratch = [
        pltpu.VMEM((depth, n), jnp.bfloat16),
        pltpu.VMEM((rank, n), jnp.bfloat16),
        pltpu.VMEM((tile, n), jnp.float32),
        pltpu.VMEM((tile, n), jnp.float32),
        pltpu.VMEM((8, n), jnp.float32),
        pltpu.VMEM((8, n), jnp.float32),
        pltpu.VMEM((8, n), jnp.float32),
    ]
    if first:
        out_shape = (out_shape, jax.ShapeDtypeStruct((entries, depth), jnp.bfloat16))
        out_specs = (WHOLE, WHOLE)
        scratch.append(pltpu.SemaphoreType.DMA((parts,)))
    return pl.pallas_call(
        kernel,
        out_shape=out_shape,
        in_specs=[WHOLE] * pieces
        + [pl.BlockSpec(memory_space=pltpu.HBM) if first else WHOLE]
        + [WHOLE] * (3 + earlier),
        out_specs=out_specs,
        scratch_shapes=scratch,
        compiler_params=pltpu.CompilerParams(vmem_limit_bytes=8 * MIB),
        cost_estimate=pl.CostEstimate(
            flops=2 * n * entries * (depth + 256),
            bytes_accessed=2 * entries * (depth + LANES),
            transcendentals=n * entries,
        ),
        name="chunk",
    )


def make_combine(bit, r, n_voc, finish):
    def kernel(mine_ref, other_ref, *outs):
        high = (lax.axis_index("vocab") & bit) != 0
        low = [jnp.where(high, other_ref[q], mine_ref[q]) for q in range(3)]
        up = [jnp.where(high, mine_ref[q], other_ref[q]) for q in range(3)]
        top = jnp.maximum(low[0], up[0])
        total = low[1] * jnp.exp(low[0] - top) + up[1] * jnp.exp(up[0] - top)
        pick = low[2] + up[2]
        if not finish:
            for q, value in enumerate((top, total, pick)):
                outs[0][q] = value
            return
        log_total = top + jnp.log(total)
        for ref, value in zip(outs, (pick - log_total, log_total)):
            for k in range(n_voc):
                for s in range(2):
                    ref[s : s + 1, k * r : (k + 1) * r] = value[k : k + 1, s * r : (s + 1) * r]

    if finish:
        shape = (jax.ShapeDtypeStruct((2, n_voc * r), jnp.float32),) * 2
        specs = (WHOLE, WHOLE)
    else:
        shape, specs = jax.ShapeDtypeStruct((3, n_voc, 2 * r), jnp.float32), WHOLE
    return pl.pallas_call(
        kernel,
        out_shape=shape,
        in_specs=[WHOLE, WHOLE],
        out_specs=specs,
        compiler_params=pltpu.CompilerParams(vmem_limit_bytes=MIB),
        name="combine",
    )


def body(hidden, head, factor_u, factor_v, sampled):
    n_group = lax.axis_size("group")
    n_voc = lax.axis_size("vocab")
    _, r, depth = hidden.shape
    entries = head.shape[0]
    rank = factor_u.shape[1]
    per = n_voc // n_group
    half = n_voc // 2

    order = ring_order(n_voc)
    ahead = [(order[i], order[(i + 1) % n_voc]) for i in range(n_voc)]
    behind = [(b, a) for a, b in ahead]

    def trade(x, axis, size, bit):
        return lax.ppermute(x, axis, [(i, i ^ bit) for i in range(size)])

    up, down = [hidden], [hidden]
    for hop in range(1, half):
        up.append(lax.ppermute(up[-1], "vocab", ahead))
        down.append(lax.ppermute(down[-1], "vocab", behind))
    ends = [
        lax.ppermute(up[-1][0], "vocab", ahead),
        lax.ppermute(down[-1][1], "vocab", behind),
    ]

    u_rows, v_rows = factor_u.shape[0], factor_v.shape[0]
    moves = [(v * n_group + g, g * n_voc + v) for v in range(n_voc) for g in range(n_group)]
    shard = jnp.pad(factor_v.T, ((0, 0), (0, padded(v_rows) - v_rows)))
    pack = jnp.concatenate([factor_u.T, shard], axis=1)
    pack = lax.ppermute(pack, ("group", "vocab"), moves)
    bit = 1
    while bit < per:
        other = trade(pack[:, u_rows:], "vocab", n_voc, bit)
        pack = jnp.concatenate([pack, other], axis=1)
        bit *= 2
    packs = {0: pack}
    bit = n_group // 2
    while bit:
        for k in list(packs):
            packs[k ^ bit] = trade(packs[k], "group", n_group, bit)
        bit //= 2
    full_u, full_v, want = make_assemble(
        n_group, n_voc, u_rows, v_rows, rank, r, entries
    )(sampled, *[packs[k] for k in range(n_group)])

    stats = []
    for hop in range(1, half + 1):
        pieces = [up[hop], down[hop]] if hop < half else [hidden] + ends
        chunk = make_chunk(hop, len(pieces), r, depth, entries, rank, n_voc)
        before = stats if hop == half else []
        out = chunk(*pieces, head, full_u, full_v, want, *before)
        if hop == 1:
            out, head = out
        stats.append(out)
    part = stats[-1]
    bit = 1
    while bit < n_voc:
        other = trade(part, "vocab", n_voc, bit)
        part = make_combine(bit, r, n_voc, 2 * bit == n_voc)(part, other)
        bit *= 2
    return part


def solution(mesh):
    in_specs = (
        P(None, ("group", "vocab"), None),
        P("vocab", None),
        P(("group", "vocab"), None),
        P("vocab", None),
        P(None, "group"),
    )
    out_specs = (P(None, "group"), P(None, "group"))
    return jax.shard_map(body, mesh=mesh, in_specs=in_specs, out_specs=out_specs, check_vma=False)
```

```python
import jax
import jax.numpy as jnp
from jax import lax
from jax.experimental import pallas as pl
from jax.experimental.pallas import tpu as pltpu
from jax.sharding import PartitionSpec as P

MIB = 1024 * 1024
LANES = 128
WHOLE = pl.BlockSpec(memory_space=pltpu.VMEM)


def ring_order(n):
    return [2 * i for i in range(n // 2)] + [2 * i + 1 for i in reversed(range(n // 2))]


def ring_position(device, n):
    return jnp.where(device % 2 == 0, device // 2, n - 1 - device // 2)


def ring_device(position, n):
    position = lax.rem(position + n, n)
    return jnp.where(position < n // 2, 2 * position, 2 * (n - 1 - position) + 1)


def tile_rows(entries):
    for rows in (512, 256, 128, 64, 32, 16):
        if entries % (2 * rows) == 0:
            return rows
    raise ValueError(entries)


def padded(size):
    return -(-size // LANES) * LANES


def make_assemble(n_group, n_voc, u_rows, v_rows, rank, r, entries):
    per = n_voc // n_group
    wide = padded(v_rows)

    def kernel(sampled_ref, *refs):
        packs = refs[:n_group]
        u_out, v_out, want_out, v_wide = refs[n_group:]
        group = lax.axis_index("group")
        voc = lax.axis_index("vocab")
        for k in range(n_group):
            member = group ^ k
            start = pl.multiple_of(member * u_rows, u_rows)
            u_out[pl.ds(start, u_rows), :] = packs[k][:, :u_rows].T
            for t in range(per):
                shard = n_group * (lax.rem(voc, per) ^ t) + member
                at = u_rows + t * wide
                block = packs[k][:, at : at + wide].astype(jnp.float32).T
                v_wide[pl.ds(pl.multiple_of(shard * v_rows, 8), v_rows), :] = block[:v_rows]
        v_out[...] = v_wide[...].T.astype(jnp.bfloat16)
        for k in range(n_voc):
            for s in range(2):
                want_out[k, :, s * r : (s + 1) * r] = (
                    sampled_ref[s : s + 1, k * r : (k + 1) * r] - voc * entries
                )

    return pl.pallas_call(
        kernel,
        out_shape=(
            jax.ShapeDtypeStruct((n_group * u_rows, rank), jnp.bfloat16),
            jax.ShapeDtypeStruct((rank, n_voc * v_rows), jnp.bfloat16),
            jax.ShapeDtypeStruct((n_voc, 1, 2 * r), jnp.int32),
        ),
        in_specs=[WHOLE] * (1 + n_group),
        out_specs=(WHOLE,) * 3,
        scratch_shapes=[pltpu.VMEM((n_voc * v_rows, rank), jnp.float32)],
        compiler_params=pltpu.CompilerParams(vmem_limit_bytes=4 * MIB),
        name="assemble",
    )


def sources_of(hop, n_voc):
    position = ring_position(lax.axis_index("vocab"), n_voc)
    if hop < n_voc // 2:
        return ring_device(position - hop, n_voc), ring_device(position + hop, n_voc)
    return ring_device(position, n_voc), ring_device(position + hop, n_voc)


def make_chunk(hop, pieces, r, depth, entries, rank, n_voc):
    tile = tile_rows(entries)
    tiles = entries // tile
    n = 4 * r
    first, last = hop == 1, hop == n_voc // 2
    earlier = hop - 1 if last else 0
    parts = 16 if entries % 4096 == 0 else tiles
    part = entries // parts

    def kernel(*refs):
        piece = refs[:pieces]
        head_ref, u_ref, v_ref, want_ref = refs[pieces : pieces + 4]
        before = refs[pieces + 4 : pieces + 4 + earlier]
        out_ref, *rest = refs[pieces + 4 + earlier :]
        held = head_ref
        if first:
            held, *rest, sems = rest
        rows, proj, even, odd, top, total, pick = rest

        def fetch(t):
            span = pl.ds(pl.multiple_of(t * part, part), part)
            return pltpu.make_async_copy(head_ref.at[span, :], held.at[span, :], sems.at[t])

        if first:
            for t in range(parts):
                fetch(t).start()

        at = 0
        for ref in piece:
            block = ref[...].reshape(-1, depth)
            rows[:, at : at + block.shape[0]] = block.T
            at += block.shape[0]
        proj[...] = jnp.dot(v_ref[...], rows[...], preferred_element_type=jnp.float32).astype(
            jnp.bfloat16
        )
        top[...] = jnp.full(top.shape, -1e30, jnp.float32)
        odd[...] = jnp.full(odd.shape, -1e30, jnp.float32)
        total[...] = jnp.zeros(total.shape, jnp.float32)
        pick[...] = jnp.zeros(pick.shape, jnp.float32)
        left, right = sources_of(hop, n_voc)
        want = jnp.concatenate([want_ref[left], want_ref[right]], axis=1)

        def multiply(t, into):
            if first:
                for k in range(parts // tiles):
                    fetch(t * (parts // tiles) + k).wait()
            span = pl.ds(pl.multiple_of(t * tile, tile), tile)
            into[...] = jnp.dot(
                held[span, :], rows[...], preferred_element_type=jnp.float32
            ) + jnp.dot(u_ref[span, :], proj[...], preferred_element_type=jnp.float32)

        def reduce(start, values):
            x = values[...]
            entry = lax.broadcasted_iota(jnp.int32, (tile, n), 0)
            hit = jnp.where(entry == want - start, x, 0.0)
            x3 = x.reshape(tile // 8, 8, n)
            new = jnp.maximum(top[...], jnp.max(x3, axis=0))
            total[...] = total[...] * jnp.exp(top[...] - new) + jnp.sum(
                jnp.exp(x3 - new[None]), axis=0
            )
            pick[...] = pick[...] + jnp.sum(hit.reshape(tile // 8, 8, n), axis=0)
            top[...] = new

        @pl.loop(0, tiles // 2)
        def _(i):
            multiply(2 * i, even)
            reduce(jnp.where(i == 0, 1 << 29, (2 * i - 1) * tile), odd)
            multiply(2 * i + 1, odd)
            reduce(2 * i * tile, even)

        reduce(entries - tile, odd)
        best = jnp.max(top[...], axis=0, keepdims=True)
        sums = jnp.sum(total[...] * jnp.exp(top[...] - best), axis=0, keepdims=True)
        picked = jnp.sum(pick[...], axis=0, keepdims=True)
        if not last:
            for q, value in enumerate((best, sums, picked)):
                out_ref[q : q + 1, :] = value
            return
        for q, value in enumerate((best, sums, picked)):
            out_ref[q, pl.ds(left, 1), :] = value[:, : 2 * r]
            out_ref[q, pl.ds(right, 1), :] = value[:, 2 * r :]
            for k in range(1, hop):
                a, b = sources_of(k, n_voc)
                out_ref[q, pl.ds(a, 1), :] = before[k - 1][q : q + 1, : 2 * r]
                out_ref[q, pl.ds(b, 1), :] = before[k - 1][q : q + 1, 2 * r :]

    out_shape = jax.ShapeDtypeStruct((3, n_voc, 2 * r) if last else (3, n), jnp.float32)
    out_specs = WHOLE
    scratch = [
        pltpu.VMEM((depth, n), jnp.bfloat16),
        pltpu.VMEM((rank, n), jnp.bfloat16),
        pltpu.VMEM((tile, n), jnp.float32),
        pltpu.VMEM((tile, n), jnp.float32),
        pltpu.VMEM((8, n), jnp.float32),
        pltpu.VMEM((8, n), jnp.float32),
        pltpu.VMEM((8, n), jnp.float32),
    ]
    if first:
        out_shape = (out_shape, jax.ShapeDtypeStruct((entries, depth), jnp.bfloat16))
        out_specs = (WHOLE, WHOLE)
        scratch.append(pltpu.SemaphoreType.DMA((parts,)))
    return pl.pallas_call(
        kernel,
        out_shape=out_shape,
        in_specs=[WHOLE] * pieces
        + [pl.BlockSpec(memory_space=pltpu.HBM) if first else WHOLE]
        + [WHOLE] * (3 + earlier),
        out_specs=out_specs,
        scratch_shapes=scratch,
        compiler_params=pltpu.CompilerParams(vmem_limit_bytes=(30 if first else 8) * MIB),
        cost_estimate=pl.CostEstimate(
            flops=2 * n * entries * (depth + 256),
            bytes_accessed=2 * entries * (depth + LANES),
            transcendentals=n * entries,
        ),
        name="chunk",
    )


def make_combine(bit, r, n_voc, finish):
    def kernel(mine_ref, other_ref, *outs):
        high = (lax.axis_index("vocab") & bit) != 0
        low = [jnp.where(high, other_ref[q], mine_ref[q]) for q in range(3)]
        up = [jnp.where(high, mine_ref[q], other_ref[q]) for q in range(3)]
        top = jnp.maximum(low[0], up[0])
        total = low[1] * jnp.exp(low[0] - top) + up[1] * jnp.exp(up[0] - top)
        pick = low[2] + up[2]
        if not finish:
            for q, value in enumerate((top, total, pick)):
                outs[0][q] = value
            return
        log_total = top + jnp.log(total)
        for ref, value in zip(outs, (pick - log_total, log_total)):
            for k in range(n_voc):
                for s in range(2):
                    ref[s : s + 1, k * r : (k + 1) * r] = value[k : k + 1, s * r : (s + 1) * r]

    if finish:
        shape = (jax.ShapeDtypeStruct((2, n_voc * r), jnp.float32),) * 2
        specs = (WHOLE, WHOLE)
    else:
        shape, specs = jax.ShapeDtypeStruct((3, n_voc, 2 * r), jnp.float32), WHOLE
    return pl.pallas_call(
        kernel,
        out_shape=shape,
        in_specs=[WHOLE, WHOLE],
        out_specs=specs,
        compiler_params=pltpu.CompilerParams(vmem_limit_bytes=MIB),
        name="combine",
    )


def body(hidden, head, factor_u, factor_v, sampled):
    n_group = lax.axis_size("group")
    n_voc = lax.axis_size("vocab")
    _, r, depth = hidden.shape
    entries = head.shape[0]
    rank = factor_u.shape[1]
    per = n_voc // n_group
    half = n_voc // 2

    order = ring_order(n_voc)
    ahead = [(order[i], order[(i + 1) % n_voc]) for i in range(n_voc)]
    behind = [(b, a) for a, b in ahead]

    def trade(x, axis, size, bit):
        return lax.ppermute(x, axis, [(i, i ^ bit) for i in range(size)])

    u_rows, v_rows = factor_u.shape[0], factor_v.shape[0]
    shard = jnp.pad(factor_v.T, ((0, 0), (0, padded(v_rows) - v_rows)))
    taken = []
    for t in range(per):
        sent = shard if t else jnp.concatenate([factor_u.T, shard], axis=1)
        moves = [
            ((v ^ t) * n_group + g, g * n_voc + v) for v in range(n_voc) for g in range(n_group)
        ]
        taken.append(lax.ppermute(sent, ("group", "vocab"), moves))

    hidden, *taken = lax.optimization_barrier((hidden, *taken))
    up, down = [hidden], [hidden]
    for hop in range(1, half):
        up.append(lax.ppermute(up[-1], "vocab", ahead))
        down.append(lax.ppermute(down[-1], "vocab", behind))
    ends = [
        lax.ppermute(up[-1][0], "vocab", ahead),
        lax.ppermute(down[-1][1], "vocab", behind),
    ]
    pack = jnp.concatenate(taken, axis=1)
    packs = {0: pack}
    bit = n_group // 2
    while bit:
        for k in list(packs):
            packs[k ^ bit] = trade(packs[k], "group", n_group, bit)
        bit //= 2
    full_u, full_v, want = make_assemble(
        n_group, n_voc, u_rows, v_rows, rank, r, entries
    )(sampled, *[packs[k] for k in range(n_group)])

    stats = []
    for hop in range(1, half + 1):
        pieces = [up[hop], down[hop]] if hop < half else [hidden] + ends
        chunk = make_chunk(hop, len(pieces), r, depth, entries, rank, n_voc)
        before = stats if hop == half else []
        out = chunk(*pieces, head, full_u, full_v, want, *before)
        if hop == 1:
            out, head = out
        stats.append(out)
    part = stats[-1]
    bit = 1
    while bit < n_voc:
        other = trade(part, "vocab", n_voc, bit)
        part = make_combine(bit, r, n_voc, 2 * bit == n_voc)(part, other)
        bit *= 2
    return part


def solution(mesh):
    in_specs = (
        P(None, ("group", "vocab"), None),
        P("vocab", None),
        P(("group", "vocab"), None),
        P("vocab", None),
        P(None, "group"),
    )
    out_specs = (P(None, "group"), P(None, "group"))
    return jax.shard_map(body, mesh=mesh, in_specs=in_specs, out_specs=out_specs, check_vma=False)
```

```python
import jax
import jax.numpy as jnp
from jax import lax
from jax.experimental import pallas as pl
from jax.experimental.pallas import tpu as pltpu
from jax.sharding import PartitionSpec as P

MIB = 1024 * 1024
LANES = 128
WHOLE = pl.BlockSpec(memory_space=pltpu.VMEM)


def ring_order(n):
    return [2 * i for i in range(n // 2)] + [2 * i + 1 for i in reversed(range(n // 2))]


def ring_position(device, n):
    return jnp.where(device % 2 == 0, device // 2, n - 1 - device // 2)


def ring_device(position, n):
    position = lax.rem(position + n, n)
    return jnp.where(position < n // 2, 2 * position, 2 * (n - 1 - position) + 1)


def tile_rows(entries):
    for rows in (512, 256, 128, 64, 32, 16):
        if entries % (2 * rows) == 0:
            return rows
    raise ValueError(entries)


def padded(size):
    return -(-size // LANES) * LANES


def make_assemble(n_group, n_voc, u_rows, v_rows, rank, r, entries):
    per = n_voc // n_group
    wide = padded(v_rows)

    def kernel(sampled_ref, *refs):
        packs = refs[:n_group]
        u_out, v_out, want_out, v_wide = refs[n_group:]
        group = lax.axis_index("group")
        voc = lax.axis_index("vocab")
        for k in range(n_group):
            member = group ^ k ^ lax.rem(voc // per, n_group)
            start = pl.multiple_of(member * u_rows, u_rows)
            u_out[pl.ds(start, u_rows), :] = packs[k][:, :u_rows].T
            for t in range(per):
                shard = n_group * (lax.rem(voc, per) ^ t) + member
                at = u_rows + t * wide
                block = packs[k][:, at : at + wide].astype(jnp.float32).T
                v_wide[pl.ds(pl.multiple_of(shard * v_rows, 8), v_rows), :] = block[:v_rows]
        v_out[...] = v_wide[...].T.astype(jnp.bfloat16)
        for k in range(n_voc):
            for s in range(2):
                want_out[k, :, s * r : (s + 1) * r] = (
                    sampled_ref[s : s + 1, k * r : (k + 1) * r] - voc * entries
                )

    return pl.pallas_call(
        kernel,
        out_shape=(
            jax.ShapeDtypeStruct((n_group * u_rows, rank), jnp.bfloat16),
            jax.ShapeDtypeStruct((rank, n_voc * v_rows), jnp.bfloat16),
            jax.ShapeDtypeStruct((n_voc, 1, 2 * r), jnp.int32),
        ),
        in_specs=[WHOLE] * (1 + n_group),
        out_specs=(WHOLE,) * 3,
        scratch_shapes=[pltpu.VMEM((n_voc * v_rows, rank), jnp.float32)],
        compiler_params=pltpu.CompilerParams(vmem_limit_bytes=4 * MIB),
        name="assemble",
    )


def sources_of(hop, n_voc):
    position = ring_position(lax.axis_index("vocab"), n_voc)
    if hop < n_voc // 2:
        return ring_device(position - hop, n_voc), ring_device(position + hop, n_voc)
    return ring_device(position, n_voc), ring_device(position + hop, n_voc)


def load_rows(rows, pieces):
    at = 0
    for ref in pieces:
        block = ref[...].reshape(-1, ref.shape[-1])
        rows[:, at : at + block.shape[0]] = block.T
        at += block.shape[0]


def make_base(r, depth, entries):
    parts = 16 if entries % 4096 == 0 else 1
    part = entries // parts
    n = 4 * r

    def kernel(up_ref, down_ref, head_ref, base_ref, rows, held, sems):
        def fetch(t):
            span = pl.ds(pl.multiple_of(t * part, part), part)
            return pltpu.make_async_copy(head_ref.at[span, :], held.at[span, :], sems.at[t])

        for t in range(parts):
            fetch(t).start(priority=t % 2)
        load_rows(rows, (up_ref, down_ref))

        @pl.loop(0, parts // 2)
        def _(i):
            fetch(2 * i).wait()
            fetch(2 * i + 1).wait()
            span = pl.ds(pl.multiple_of(2 * i * part, 2 * part), 2 * part)
            base_ref[span, :] = jnp.dot(
                held[span, :], rows[...], preferred_element_type=jnp.float32
            )

    return pl.pallas_call(
        kernel,
        out_shape=(
            jax.ShapeDtypeStruct((entries, n), jnp.float32),
            jax.ShapeDtypeStruct((depth, n), jnp.bfloat16),
            jax.ShapeDtypeStruct((entries, depth), jnp.bfloat16),
        ),
        in_specs=[WHOLE, WHOLE, pl.BlockSpec(memory_space=pltpu.HBM)],
        out_specs=(WHOLE,) * 3,
        scratch_shapes=[pltpu.SemaphoreType.DMA((parts,))],
        compiler_params=pltpu.CompilerParams(vmem_limit_bytes=23 * MIB),
        cost_estimate=pl.CostEstimate(
            flops=2 * n * entries * depth,
            bytes_accessed=2 * entries * depth,
            transcendentals=0,
        ),
        name="base",
    )


def make_chunk(hop, pieces, r, depth, entries, rank, n_voc):
    tile = tile_rows(entries)
    tiles = entries // tile
    n = 4 * r
    carry, last = hop == 2, hop == n_voc // 2
    earlier = hop - 1 if last else 0

    def kernel(*refs):
        piece, refs = refs[:pieces], refs[pieces:]
        head_ref, u_ref, v_ref, want_ref, *refs = refs
        if carry:
            base_ref, base_rows, *refs = refs
        before, refs = refs[:earlier], refs[earlier:]
        out_ref, *refs = refs
        if carry:
            base_out, *refs = refs
        rows, even, odd, proj, top, total, pick, *refs = refs
        if carry:
            base_proj, base_top, base_total, base_pick = refs
            base_state = base_top, base_total, base_pick
        state = top, total, pick

        def project(source, into):
            into[...] = jnp.dot(
                v_ref[...], source[...], preferred_element_type=jnp.float32
            ).astype(jnp.bfloat16)

        def clear(top, total, pick):
            top[...] = jnp.full(top.shape, -1e30, jnp.float32)
            total[...] = jnp.zeros(total.shape, jnp.float32)
            pick[...] = jnp.zeros(pick.shape, jnp.float32)

        def wanted(k):
            left, right = sources_of(k, n_voc)
            return jnp.concatenate([want_ref[left], want_ref[right]], axis=1)

        load_rows(rows, piece)
        project(rows, proj)
        clear(*state)
        odd[...] = jnp.full(odd.shape, -1e30, jnp.float32)
        want = wanted(hop)
        if carry:
            project(base_rows, base_proj)
            clear(*base_state)
            base_want = wanted(1)

        def multiply(t, into):
            span = pl.ds(pl.multiple_of(t * tile, tile), tile)
            into[...] = jnp.dot(
                head_ref[span, :], rows[...], preferred_element_type=jnp.float32
            ) + jnp.dot(u_ref[span, :], proj[...], preferred_element_type=jnp.float32)

        def reduce(x, want, top, total, pick):
            entry = lax.broadcasted_iota(jnp.int32, (tile, n), 0)
            hit = jnp.where(entry == want, x, 0.0)
            x3 = x.reshape(tile // 8, 8, n)
            new = jnp.maximum(top[...], jnp.max(x3, axis=0))
            total[...] = total[...] * jnp.exp(top[...] - new) + jnp.sum(
                jnp.exp(x3 - new[None]), axis=0
            )
            pick[...] = pick[...] + jnp.sum(hit.reshape(tile // 8, 8, n), axis=0)
            top[...] = new

        def finish_base(t):
            if carry:
                span = pl.ds(pl.multiple_of(t * tile, tile), tile)
                x = base_ref[span, :] + jnp.dot(
                    u_ref[span, :], base_proj[...], preferred_element_type=jnp.float32
                )
                reduce(x, base_want - t * tile, *base_state)

        @pl.loop(0, tiles // 2)
        def _(i):
            multiply(2 * i, even)
            reduce(odd[...], want - jnp.where(i == 0, 1 << 29, (2 * i - 1) * tile), *state)
            finish_base(2 * i)
            multiply(2 * i + 1, odd)
            reduce(even[...], want - 2 * i * tile, *state)
            finish_base(2 * i + 1)

        reduce(odd[...], want - (entries - tile), *state)

        def results(top, total, pick):
            best = jnp.max(top[...], axis=0, keepdims=True)
            sums = jnp.sum(total[...] * jnp.exp(top[...] - best), axis=0, keepdims=True)
            return best, sums, jnp.sum(pick[...], axis=0, keepdims=True)

        if carry:
            for q, value in enumerate(results(*base_state)):
                base_out[q : q + 1, :] = value
        for q, value in enumerate(results(*state)):
            if not last:
                out_ref[q : q + 1, :] = value
                continue
            for k, lanes in [(hop, value)] + [
                (k, before[k - 1][q : q + 1, :]) for k in range(1, hop)
            ]:
                left, right = sources_of(k, n_voc)
                out_ref[q, pl.ds(left, 1), :] = lanes[:, : 2 * r]
                out_ref[q, pl.ds(right, 1), :] = lanes[:, 2 * r :]

    out_shape = jax.ShapeDtypeStruct((3, n_voc, 2 * r) if last else (3, n), jnp.float32)
    small = [pltpu.VMEM((rank, n), jnp.bfloat16)] + [pltpu.VMEM((8, n), jnp.float32)] * 3
    return pl.pallas_call(
        kernel,
        out_shape=(out_shape, out_shape) if carry else out_shape,
        in_specs=[WHOLE] * (pieces + 4 + 2 * carry + earlier),
        out_specs=(WHOLE, WHOLE) if carry else WHOLE,
        scratch_shapes=[
            pltpu.VMEM((depth, n), jnp.bfloat16),
            pltpu.VMEM((tile, n), jnp.float32),
            pltpu.VMEM((tile, n), jnp.float32),
        ]
        + small * (1 + carry),
        compiler_params=pltpu.CompilerParams(vmem_limit_bytes=8 * MIB),
        cost_estimate=pl.CostEstimate(
            flops=2 * n * entries * (depth + 256),
            bytes_accessed=2 * entries * (depth + LANES),
            transcendentals=n * entries,
        ),
        name="chunk",
    )


def make_combine(bit, r, n_voc, finish):
    def kernel(mine_ref, other_ref, *outs):
        high = (lax.axis_index("vocab") & bit) != 0
        low = [jnp.where(high, other_ref[q], mine_ref[q]) for q in range(3)]
        up = [jnp.where(high, mine_ref[q], other_ref[q]) for q in range(3)]
        top = jnp.maximum(low[0], up[0])
        total = low[1] * jnp.exp(low[0] - top) + up[1] * jnp.exp(up[0] - top)
        pick = low[2] + up[2]
        if not finish:
            for q, value in enumerate((top, total, pick)):
                outs[0][q] = value
            return
        log_total = top + jnp.log(total)
        for ref, value in zip(outs, (pick - log_total, log_total)):
            for k in range(n_voc):
                for s in range(2):
                    ref[s : s + 1, k * r : (k + 1) * r] = value[k : k + 1, s * r : (s + 1) * r]

    if finish:
        shape = (jax.ShapeDtypeStruct((2, n_voc * r), jnp.float32),) * 2
        specs = (WHOLE, WHOLE)
    else:
        shape, specs = jax.ShapeDtypeStruct((3, n_voc, 2 * r), jnp.float32), WHOLE
    return pl.pallas_call(
        kernel,
        out_shape=shape,
        in_specs=[WHOLE, WHOLE],
        out_specs=specs,
        compiler_params=pltpu.CompilerParams(vmem_limit_bytes=MIB),
        name="combine",
    )


def body(hidden, head, factor_u, factor_v, sampled):
    n_group = lax.axis_size("group")
    n_voc = lax.axis_size("vocab")
    _, r, depth = hidden.shape
    entries = head.shape[0]
    rank = factor_u.shape[1]
    per = n_voc // n_group
    half = n_voc // 2

    order = ring_order(n_voc)
    ahead = [(order[i], order[(i + 1) % n_voc]) for i in range(n_voc)]
    behind = [(b, a) for a, b in ahead]

    def trade(x, axis, size, bit):
        return lax.ppermute(x, axis, [(i, i ^ bit) for i in range(size)])

    u_rows, v_rows = factor_u.shape[0], factor_v.shape[0]
    shard = jnp.pad(factor_v.T, ((0, 0), (0, padded(v_rows) - v_rows)))
    taken = []
    for t in range(per):
        sent = shard if t else jnp.concatenate([factor_u.T, shard], axis=1)
        moves = [
            ((v ^ t) * n_group + (g ^ (v // per) % n_group), g * n_voc + v)
            for v in range(n_voc)
            for g in range(n_group)
        ]
        taken.append(lax.ppermute(sent, ("group", "vocab"), moves))

    up = [hidden, lax.ppermute(hidden, "vocab", ahead)]
    down = [hidden, lax.ppermute(hidden, "vocab", behind)]
    up[1], down[1], *taken = lax.optimization_barrier((up[1], down[1], *taken))
    base, base_rows, head = make_base(r, depth, entries)(up[1], down[1], head)
    for hop in range(2, half):
        up.append(lax.ppermute(up[-1], "vocab", ahead))
        down.append(lax.ppermute(down[-1], "vocab", behind))
        if hop == 2:
            up[2], down[2], base = lax.optimization_barrier((up[2], down[2], base))
    ends = [
        lax.ppermute(up[-1][0], "vocab", ahead),
        lax.ppermute(down[-1][1], "vocab", behind),
    ]
    packs = {0: jnp.concatenate(taken, axis=1)}
    bit = n_group // 2
    while bit:
        for k in list(packs):
            packs[k ^ bit] = trade(packs[k], "group", n_group, bit)
        bit //= 2
    full_u, full_v, want = make_assemble(
        n_group, n_voc, u_rows, v_rows, rank, r, entries
    )(sampled, *[packs[k] for k in range(n_group)])

    stats = []
    for hop in range(2, half + 1):
        pieces = [up[hop], down[hop]] if hop < half else [hidden] + ends
        extra = [base, base_rows] if hop == 2 else stats if hop == half else []
        chunk = make_chunk(hop, len(pieces), r, depth, entries, rank, n_voc)
        out = chunk(*pieces, head, full_u, full_v, want, *extra)
        stats += [out[1], out[0]] if hop == 2 else [out]
    part = stats[-1]
    bit = 1
    while bit < n_voc:
        other = trade(part, "vocab", n_voc, bit)
        part = make_combine(bit, r, n_voc, 2 * bit == n_voc)(part, other)
        bit *= 2
    return part


def solution(mesh):
    in_specs = (
        P(None, ("group", "vocab"), None),
        P("vocab", None),
        P(("group", "vocab"), None),
        P("vocab", None),
        P(None, "group"),
    )
    out_specs = (P(None, "group"), P(None, "group"))
    return jax.shard_map(body, mesh=mesh, in_specs=in_specs, out_specs=out_specs, check_vma=False)
```

```python
import jax
import jax.numpy as jnp
from jax import lax
from jax.experimental import pallas as pl
from jax.experimental.pallas import tpu as pltpu
from jax.sharding import PartitionSpec as P

MIB = 1024 * 1024
LANES = 128
WHOLE = pl.BlockSpec(memory_space=pltpu.VMEM)


def ring_order(n):
    return [2 * i for i in range(n // 2)] + [2 * i + 1 for i in reversed(range(n // 2))]


def ring_position(device, n):
    return jnp.where(device % 2 == 0, device // 2, n - 1 - device // 2)


def ring_device(position, n):
    position = lax.rem(position + n, n)
    return jnp.where(position < n // 2, 2 * position, 2 * (n - 1 - position) + 1)


def tile_rows(entries):
    for rows in (512, 256, 128, 64, 32, 16):
        if entries % (4 * rows) == 0:
            return rows
    raise ValueError(entries)


def padded(size):
    return -(-size // LANES) * LANES


def make_assemble(n_group, n_voc, u_rows, v_rows, rank, r, entries):
    per = n_voc // n_group
    wide = padded(v_rows)

    def kernel(sampled_ref, *refs):
        packs = refs[:n_group]
        u_out, v_out, want_out, v_wide = refs[n_group:]
        group = lax.axis_index("group")
        voc = lax.axis_index("vocab")
        for k in range(n_group):
            member = group ^ k ^ lax.rem(voc // per, n_group)
            start = pl.multiple_of(member * u_rows, u_rows)
            u_out[pl.ds(start, u_rows), :] = packs[k][:, :u_rows].T
            for t in range(per):
                shard = n_group * (lax.rem(voc, per) ^ t) + member
                at = u_rows + t * wide
                block = packs[k][:, at : at + wide].astype(jnp.float32).T
                v_wide[pl.ds(pl.multiple_of(shard * v_rows, 8), v_rows), :] = block[:v_rows]
        v_out[...] = v_wide[...].T.astype(jnp.bfloat16)
        for k in range(n_voc):
            for s in range(2):
                want_out[k, :, s * r : (s + 1) * r] = (
                    sampled_ref[s : s + 1, k * r : (k + 1) * r] - voc * entries
                )

    return pl.pallas_call(
        kernel,
        out_shape=(
            jax.ShapeDtypeStruct((n_group * u_rows, rank), jnp.bfloat16),
            jax.ShapeDtypeStruct((rank, n_voc * v_rows), jnp.bfloat16),
            jax.ShapeDtypeStruct((n_voc, 1, 2 * r), jnp.int32),
        ),
        in_specs=[WHOLE] * (1 + n_group),
        out_specs=(WHOLE,) * 3,
        scratch_shapes=[pltpu.VMEM((n_voc * v_rows, rank), jnp.float32)],
        compiler_params=pltpu.CompilerParams(vmem_limit_bytes=4 * MIB),
        name="assemble",
    )


def sources_of(hop, n_voc):
    position = ring_position(lax.axis_index("vocab"), n_voc)
    if hop < n_voc // 2:
        return ring_device(position - hop, n_voc), ring_device(position + hop, n_voc)
    return ring_device(position, n_voc), ring_device(position + hop, n_voc)


def load_rows(rows, pieces):
    at = 0
    for ref in pieces:
        block = ref[...].reshape(-1, ref.shape[-1])
        rows[:, at : at + block.shape[0]] = block.T
        at += block.shape[0]


def fetch_rows(head_ref, first, held, sems, parts=8):
    part = held.shape[0] // parts
    return [
        pltpu.make_async_copy(
            head_ref.at[pl.ds(first + t * part, part), :],
            held.at[pl.ds(t * part, part), :],
            sems.at[t],
        )
        for t in range(parts)
    ]


def make_load(depth, entries):
    def kernel(head_ref, held, sems):
        copies = fetch_rows(head_ref, 0, held, sems)
        for t, copy in enumerate(copies):
            copy.start(priority=t % 2)
        for copy in copies:
            copy.wait()

    return pl.pallas_call(
        kernel,
        out_shape=jax.ShapeDtypeStruct((entries // 2, depth), jnp.bfloat16),
        in_specs=[pl.BlockSpec(memory_space=pltpu.HBM)],
        out_specs=WHOLE,
        scratch_shapes=[pltpu.SemaphoreType.DMA((8,))],
        compiler_params=pltpu.CompilerParams(vmem_limit_bytes=40 * MIB),
        cost_estimate=pl.CostEstimate(
            flops=0, bytes_accessed=depth * entries, transcendentals=0
        ),
        name="load",
    )


def make_base(r, depth, entries):
    n = 4 * r
    half = entries // 2
    tile = 2 * half // 8

    def kernel(up_ref, down_ref, head_ref, low, base_ref, rows, high, sems):
        copies = fetch_rows(head_ref, half, high, sems)
        for t, copy in enumerate(copies):
            copy.start(priority=t % 2)
        load_rows(rows, (up_ref, down_ref))

        def multiply(i, held, first):
            span = pl.ds(pl.multiple_of(i * tile, tile), tile)
            at = pl.ds(pl.multiple_of(first + i * tile, tile), tile)
            base_ref[at, :] = jnp.dot(
                held[span, :], rows[...], preferred_element_type=jnp.float32
            )

        pl.loop(0, half // tile)(lambda i: multiply(i, low, 0))
        for i in range(half // tile):
            for copy in copies[2 * i : 2 * i + 2]:
                copy.wait()
            multiply(i, high, half)

    return pl.pallas_call(
        kernel,
        out_shape=(
            jax.ShapeDtypeStruct((entries, n), jnp.float32),
            jax.ShapeDtypeStruct((depth, n), jnp.bfloat16),
            jax.ShapeDtypeStruct((half, depth), jnp.bfloat16),
        ),
        in_specs=[WHOLE, WHOLE, pl.BlockSpec(memory_space=pltpu.HBM), WHOLE],
        out_specs=(WHOLE,) * 3,
        scratch_shapes=[pltpu.SemaphoreType.DMA((8,))],
        compiler_params=pltpu.CompilerParams(vmem_limit_bytes=24 * MIB),
        cost_estimate=pl.CostEstimate(
            flops=2 * n * entries * depth,
            bytes_accessed=2 * entries * depth,
            transcendentals=0,
        ),
        name="base",
    )


def make_chunk(hop, pieces, r, depth, entries, rank, n_voc):
    tile = tile_rows(entries)
    tiles = entries // tile
    n = 4 * r
    carry, last = hop == 2, hop == n_voc // 2
    earlier = hop - 1 if last else 0

    def kernel(*refs):
        piece, refs = refs[:pieces], refs[pieces:]
        low_ref, high_ref, u_ref, v_ref, want_ref, *refs = refs
        if carry:
            base_ref, base_rows, *refs = refs
        before, refs = refs[:earlier], refs[earlier:]
        out_ref, *refs = refs
        if carry:
            base_out, *refs = refs
        rows, even, odd, proj, top, total, pick, *refs = refs
        if carry:
            base_proj, base_top, base_total, base_pick = refs
            base_state = base_top, base_total, base_pick
        state = top, total, pick

        def project(source, into):
            into[...] = jnp.dot(
                v_ref[...], source[...], preferred_element_type=jnp.float32
            ).astype(jnp.bfloat16)

        def clear(top, total, pick):
            top[...] = jnp.full(top.shape, -1e30, jnp.float32)
            total[...] = jnp.zeros(total.shape, jnp.float32)
            pick[...] = jnp.zeros(pick.shape, jnp.float32)

        def wanted(k):
            left, right = sources_of(k, n_voc)
            return jnp.concatenate([want_ref[left], want_ref[right]], axis=1)

        load_rows(rows, piece)
        project(rows, proj)
        clear(*state)
        odd[...] = jnp.full(odd.shape, -1e30, jnp.float32)
        want = wanted(hop)
        if carry:
            project(base_rows, base_proj)
            clear(*base_state)
            base_want = wanted(1)

        def multiply(t, into, head_ref, first):
            span = pl.ds(pl.multiple_of(t * tile, tile), tile)
            at = pl.ds(pl.multiple_of((t - first) * tile, tile), tile)
            into[...] = jnp.dot(
                head_ref[at, :], rows[...], preferred_element_type=jnp.float32
            ) + jnp.dot(u_ref[span, :], proj[...], preferred_element_type=jnp.float32)

        def reduce(x, want, top, total, pick):
            entry = lax.broadcasted_iota(jnp.int32, (tile, n), 0)
            hit = jnp.where(entry == want, x, 0.0)
            x3 = x.reshape(tile // 8, 8, n)
            new = jnp.maximum(top[...], jnp.max(x3, axis=0))
            total[...] = total[...] * jnp.exp(top[...] - new) + jnp.sum(
                jnp.exp(x3 - new[None]), axis=0
            )
            pick[...] = pick[...] + jnp.sum(hit.reshape(tile // 8, 8, n), axis=0)
            top[...] = new

        def finish_base(t):
            if carry:
                span = pl.ds(pl.multiple_of(t * tile, tile), tile)
                x = base_ref[span, :] + jnp.dot(
                    u_ref[span, :], base_proj[...], preferred_element_type=jnp.float32
                )
                reduce(x, base_want - t * tile, *base_state)

        def step(i, head_ref, first):
            multiply(2 * i, even, head_ref, first)
            reduce(odd[...], want - jnp.where(i == 0, 1 << 29, (2 * i - 1) * tile), *state)
            finish_base(2 * i)
            multiply(2 * i + 1, odd, head_ref, first)
            reduce(even[...], want - 2 * i * tile, *state)
            finish_base(2 * i + 1)

        pl.loop(0, tiles // 4)(lambda i: step(i, low_ref, 0))
        pl.loop(tiles // 4, tiles // 2)(lambda i: step(i, high_ref, tiles // 2))

        reduce(odd[...], want - (entries - tile), *state)

        def results(top, total, pick):
            best = jnp.max(top[...], axis=0, keepdims=True)
            sums = jnp.sum(total[...] * jnp.exp(top[...] - best), axis=0, keepdims=True)
            return best, sums, jnp.sum(pick[...], axis=0, keepdims=True)

        if carry:
            for q, value in enumerate(results(*base_state)):
                base_out[q : q + 1, :] = value
        for q, value in enumerate(results(*state)):
            if not last:
                out_ref[q : q + 1, :] = value
                continue
            for k, lanes in [(hop, value)] + [
                (k, before[k - 1][q : q + 1, :]) for k in range(1, hop)
            ]:
                left, right = sources_of(k, n_voc)
                out_ref[q, pl.ds(left, 1), :] = lanes[:, : 2 * r]
                out_ref[q, pl.ds(right, 1), :] = lanes[:, 2 * r :]

    out_shape = jax.ShapeDtypeStruct((3, n_voc, 2 * r) if last else (3, n), jnp.float32)
    small = [pltpu.VMEM((rank, n), jnp.bfloat16)] + [pltpu.VMEM((8, n), jnp.float32)] * 3
    return pl.pallas_call(
        kernel,
        out_shape=(out_shape, out_shape) if carry else out_shape,
        in_specs=[WHOLE] * (pieces + 5 + 2 * carry + earlier),
        out_specs=(WHOLE, WHOLE) if carry else WHOLE,
        scratch_shapes=[
            pltpu.VMEM((depth, n), jnp.bfloat16),
            pltpu.VMEM((tile, n), jnp.float32),
            pltpu.VMEM((tile, n), jnp.float32),
        ]
        + small * (1 + carry),
        compiler_params=pltpu.CompilerParams(vmem_limit_bytes=8 * MIB),
        cost_estimate=pl.CostEstimate(
            flops=2 * n * entries * (depth + 256),
            bytes_accessed=2 * entries * (depth + LANES),
            transcendentals=n * entries,
        ),
        name="chunk",
    )


def make_combine(bits, r, n_voc, finish):
    low = bits & -bits
    count = bits // low + 1

    def kernel(*refs):
        parts, outs, held = refs[:count], refs[count:-1], refs[-1]
        slot = lax.rem(lax.axis_index("vocab") // low, count)
        for k in range(count):
            held[slot ^ k] = parts[k][...]
        top = held[0, 0]
        for k in range(1, count):
            top = jnp.maximum(top, held[k, 0])
        total = held[0, 1] * jnp.exp(held[0, 0] - top)
        pick = held[0, 2]
        for k in range(1, count):
            total = total + held[k, 1] * jnp.exp(held[k, 0] - top)
            pick = pick + held[k, 2]
        if not finish:
            for q, value in enumerate((top, total, pick)):
                outs[0][q] = value
            return
        log_total = top + jnp.log(total)
        for ref, value in zip(outs, (pick - log_total, log_total)):
            for k in range(n_voc):
                for s in range(2):
                    ref[s : s + 1, k * r : (k + 1) * r] = value[k : k + 1, s * r : (s + 1) * r]

    if finish:
        shape = (jax.ShapeDtypeStruct((2, n_voc * r), jnp.float32),) * 2
        specs = (WHOLE, WHOLE)
    else:
        shape, specs = jax.ShapeDtypeStruct((3, n_voc, 2 * r), jnp.float32), WHOLE
    return pl.pallas_call(
        kernel,
        out_shape=shape,
        in_specs=[WHOLE] * count,
        out_specs=specs,
        scratch_shapes=[pltpu.VMEM((count, 3, n_voc, 2 * r), jnp.float32)],
        compiler_params=pltpu.CompilerParams(vmem_limit_bytes=MIB),
        name="combine",
    )


def body(hidden, head, factor_u, factor_v, sampled):
    n_group = lax.axis_size("group")
    n_voc = lax.axis_size("vocab")
    _, r, depth = hidden.shape
    entries = head.shape[0]
    rank = factor_u.shape[1]
    per = n_voc // n_group
    half = n_voc // 2

    order = ring_order(n_voc)
    ahead = [(order[i], order[(i + 1) % n_voc]) for i in range(n_voc)]
    behind = [(b, a) for a, b in ahead]

    def trade(x, axis, size, bit):
        return lax.ppermute(x, axis, [(i, i ^ bit) for i in range(size)])

    u_rows, v_rows = factor_u.shape[0], factor_v.shape[0]
    shard = jnp.pad(factor_v.T, ((0, 0), (0, padded(v_rows) - v_rows)))
    taken = []
    for t in range(per):
        sent = shard if t else jnp.concatenate([factor_u.T, shard], axis=1)
        moves = [
            ((v ^ t) * n_group + (g ^ (v // per) % n_group), g * n_voc + v)
            for v in range(n_voc)
            for g in range(n_group)
        ]
        taken.append(lax.ppermute(sent, ("group", "vocab"), moves))

    up = [hidden, lax.ppermute(hidden, "vocab", ahead)]
    down = [hidden, lax.ppermute(hidden, "vocab", behind)]
    low, *taken = lax.optimization_barrier((make_load(depth, entries)(head), *taken))
    base, base_rows, high = make_base(r, depth, entries)(up[1], down[1], head, low)
    for hop in range(2, half):
        up.append(lax.ppermute(up[-1], "vocab", ahead))
        down.append(lax.ppermute(down[-1], "vocab", behind))
        if hop == 2:
            up[2], down[2], base = lax.optimization_barrier((up[2], down[2], base))
    ends = [
        lax.ppermute(up[-1][0], "vocab", ahead),
        lax.ppermute(down[-1][1], "vocab", behind),
    ]
    packs = {0: jnp.concatenate(taken, axis=1)}
    bit = n_group // 2
    while bit:
        for k in list(packs):
            packs[k ^ bit] = trade(packs[k], "group", n_group, bit)
        bit //= 2
    full_u, full_v, want = make_assemble(
        n_group, n_voc, u_rows, v_rows, rank, r, entries
    )(sampled, *[packs[k] for k in range(n_group)])

    stats = []
    for hop in range(2, half + 1):
        pieces = [up[hop], down[hop]] if hop < half else [hidden] + ends
        extra = [base, base_rows] if hop == 2 else stats if hop == half else []
        chunk = make_chunk(hop, len(pieces), r, depth, entries, rank, n_voc)
        out = chunk(*pieces, low, high, full_u, full_v, want, *extra)
        stats += [out[1], out[0]] if hop == 2 else [out]
    part = stats[-1]
    low = 1
    while low < n_voc:
        count = 2 if low == 1 else min(4, n_voc // low)
        bits = low * (count - 1)
        others = [trade(part, "vocab", n_voc, low * k) for k in range(1, count)]
        part = make_combine(bits, r, n_voc, low * count == n_voc)(part, *others)
        low *= count
    return part


def solution(mesh):
    in_specs = (
        P(None, ("group", "vocab"), None),
        P("vocab", None),
        P(("group", "vocab"), None),
        P("vocab", None),
        P(None, "group"),
    )
    out_specs = (P(None, "group"), P(None, "group"))
    return jax.shard_map(body, mesh=mesh, in_specs=in_specs, out_specs=out_specs, check_vma=False)
```

```python
import jax
import jax.numpy as jnp
from jax import lax
from jax.experimental import pallas as pl
from jax.experimental.pallas import tpu as pltpu
from jax.sharding import PartitionSpec as P

MIB = 1024 * 1024
LANES = 128
WHOLE = pl.BlockSpec(memory_space=pltpu.VMEM)


def ring_order(n):
    return [2 * i for i in range(n // 2)] + [2 * i + 1 for i in reversed(range(n // 2))]


def ring_position(device, n):
    return jnp.where(device % 2 == 0, device // 2, n - 1 - device // 2)


def ring_device(position, n):
    position = lax.rem(position + n, n)
    return jnp.where(position < n // 2, 2 * position, 2 * (n - 1 - position) + 1)


def tile_rows(entries):
    for rows in (512, 256, 128, 64, 32, 16):
        if entries % (2 * rows) == 0:
            return rows
    raise ValueError(entries)


def padded(size):
    return -(-size // LANES) * LANES


def make_assemble(n_group, n_voc, u_rows, v_rows, rank, r, entries):
    per = n_voc // n_group
    wide = padded(v_rows)

    def kernel(sampled_ref, *refs):
        packs = refs[:n_group]
        u_out, v_out, want_out, v_wide = refs[n_group:]
        group = lax.axis_index("group")
        voc = lax.axis_index("vocab")
        for k in range(n_group):
            member = group ^ k
            block = member ^ lax.rem(voc // per, n_group)
            start = pl.multiple_of(block * u_rows, u_rows)
            u_out[pl.ds(start, u_rows), :] = packs[k][:, :u_rows].T
            for t in range(per):
                shard = member * per + (lax.rem(voc, per) ^ t)
                at = u_rows + t * wide
                rows = packs[k][:, at : at + wide].astype(jnp.float32).T
                v_wide[pl.ds(pl.multiple_of(shard * v_rows, 8), v_rows), :] = rows[:v_rows]
        v_out[...] = v_wide[...].T.astype(jnp.bfloat16)
        for k in range(n_voc):
            for s in range(2):
                want_out[k, :, s * r : (s + 1) * r] = (
                    sampled_ref[s : s + 1, k * r : (k + 1) * r] - voc * entries
                )

    return pl.pallas_call(
        kernel,
        out_shape=(
            jax.ShapeDtypeStruct((n_group * u_rows, rank), jnp.bfloat16),
            jax.ShapeDtypeStruct((rank, n_voc * v_rows), jnp.bfloat16),
            jax.ShapeDtypeStruct((n_voc, 1, 2 * r), jnp.int32),
        ),
        in_specs=[WHOLE] * (1 + n_group),
        out_specs=(WHOLE,) * 3,
        scratch_shapes=[pltpu.VMEM((n_voc * v_rows, rank), jnp.float32)],
        compiler_params=pltpu.CompilerParams(vmem_limit_bytes=4 * MIB),
        name="assemble",
    )


def sources_of(hop, n_voc):
    position = ring_position(lax.axis_index("vocab"), n_voc)
    if hop < n_voc // 2:
        return ring_device(position - hop, n_voc), ring_device(position + hop, n_voc)
    return ring_device(position, n_voc), ring_device(position + hop, n_voc)


def load_rows(rows, pieces):
    at = 0
    for ref in pieces:
        block = ref[...].reshape(-1, ref.shape[-1])
        rows[:, at : at + block.shape[0]] = block.T
        at += block.shape[0]


def make_load(depth, entries):
    parts = 16 if entries % 4096 == 0 else 1
    part = entries // parts

    def kernel(head_ref, held, sems):
        spans = [pl.ds(t * part, part) for t in range(parts)]
        copies = [
            pltpu.make_async_copy(head_ref.at[span, :], held.at[span, :], sems.at[t])
            for t, span in enumerate(spans)
        ]
        for t, copy in enumerate(copies):
            copy.start(priority=t % 2)
        for copy in copies:
            copy.wait()

    return pl.pallas_call(
        kernel,
        out_shape=jax.ShapeDtypeStruct((entries, depth), jnp.bfloat16),
        in_specs=[pl.BlockSpec(memory_space=pltpu.HBM)],
        out_specs=WHOLE,
        scratch_shapes=[pltpu.SemaphoreType.DMA((parts,))],
        compiler_params=pltpu.CompilerParams(vmem_limit_bytes=32 * MIB),
        cost_estimate=pl.CostEstimate(
            flops=0, bytes_accessed=2 * depth * entries, transcendentals=0
        ),
        name="load",
    )


def make_base(r, depth, entries):
    n = 4 * r
    tile = tile_rows(entries)

    def kernel(up_ref, down_ref, head_ref, base_ref, rows):
        load_rows(rows, (up_ref, down_ref))

        @pl.loop(0, entries // tile)
        def _(i):
            span = pl.ds(pl.multiple_of(i * tile, tile), tile)
            base_ref[span, :] = jnp.dot(
                head_ref[span, :], rows[...], preferred_element_type=jnp.float32
            )

    return pl.pallas_call(
        kernel,
        out_shape=(
            jax.ShapeDtypeStruct((entries, n), jnp.float32),
            jax.ShapeDtypeStruct((depth, n), jnp.bfloat16),
        ),
        in_specs=[WHOLE] * 3,
        out_specs=(WHOLE,) * 2,
        compiler_params=pltpu.CompilerParams(vmem_limit_bytes=8 * MIB),
        cost_estimate=pl.CostEstimate(
            flops=2 * n * entries * depth,
            bytes_accessed=2 * entries * depth,
            transcendentals=0,
        ),
        name="base",
    )


def make_chunk(hop, pieces, r, depth, entries, rank, n_voc):
    tile = tile_rows(entries)
    tiles = entries // tile
    n = 4 * r
    carry, last = hop == 2, hop == n_voc // 2
    earlier = hop - 1 if last else 0

    def kernel(*refs):
        piece, refs = refs[:pieces], refs[pieces:]
        head_ref, u_ref, v_ref, want_ref, *refs = refs
        if carry:
            base_ref, base_rows, *refs = refs
        before, refs = refs[:earlier], refs[earlier:]
        out_ref, *refs = refs
        if carry:
            base_out, *refs = refs
        rows, even, odd, proj, top, total, pick, *refs = refs
        if carry:
            base_proj, base_top, base_total, base_pick = refs
            base_state = base_top, base_total, base_pick
        state = top, total, pick

        def project(source, into):
            into[...] = jnp.dot(
                v_ref[...], source[...], preferred_element_type=jnp.float32
            ).astype(jnp.bfloat16)

        def clear(top, total, pick):
            top[...] = jnp.full(top.shape, -1e30, jnp.float32)
            total[...] = jnp.zeros(total.shape, jnp.float32)
            pick[...] = jnp.zeros(pick.shape, jnp.float32)

        def wanted(k):
            left, right = sources_of(k, n_voc)
            return jnp.concatenate([want_ref[left], want_ref[right]], axis=1)

        load_rows(rows, piece)
        project(rows, proj)
        clear(*state)
        odd[...] = jnp.full(odd.shape, -1e30, jnp.float32)
        want = wanted(hop)
        if carry:
            project(base_rows, base_proj)
            clear(*base_state)
            base_want = wanted(1)

        def multiply(t, into):
            span = pl.ds(pl.multiple_of(t * tile, tile), tile)
            into[...] = jnp.dot(
                head_ref[span, :], rows[...], preferred_element_type=jnp.float32
            ) + jnp.dot(u_ref[span, :], proj[...], preferred_element_type=jnp.float32)

        def reduce(x, want, top, total, pick):
            entry = lax.broadcasted_iota(jnp.int32, (tile, n), 0)
            hit = jnp.where(entry == want, x, 0.0)
            x3 = x.reshape(tile // 8, 8, n)
            new = jnp.maximum(top[...], jnp.max(x3, axis=0))
            total[...] = total[...] * jnp.exp(top[...] - new) + jnp.sum(
                jnp.exp(x3 - new[None]), axis=0
            )
            pick[...] = pick[...] + jnp.sum(hit.reshape(tile // 8, 8, n), axis=0)
            top[...] = new

        def finish_base(t):
            if carry:
                span = pl.ds(pl.multiple_of(t * tile, tile), tile)
                x = base_ref[span, :] + jnp.dot(
                    u_ref[span, :], base_proj[...], preferred_element_type=jnp.float32
                )
                reduce(x, base_want - t * tile, *base_state)

        @pl.loop(0, tiles // 2)
        def _(i):
            multiply(2 * i, even)
            reduce(odd[...], want - jnp.where(i == 0, 1 << 29, (2 * i - 1) * tile), *state)
            finish_base(2 * i)
            multiply(2 * i + 1, odd)
            reduce(even[...], want - 2 * i * tile, *state)
            finish_base(2 * i + 1)

        reduce(odd[...], want - (entries - tile), *state)

        def results(top, total, pick):
            best = jnp.max(top[...], axis=0, keepdims=True)
            sums = jnp.sum(total[...] * jnp.exp(top[...] - best), axis=0, keepdims=True)
            return best, sums, jnp.sum(pick[...], axis=0, keepdims=True)

        if carry:
            for q, value in enumerate(results(*base_state)):
                base_out[q : q + 1, :] = value
        for q, value in enumerate(results(*state)):
            if not last:
                out_ref[q : q + 1, :] = value
                continue
            for k, lanes in [(hop, value)] + [
                (k, before[k - 1][q : q + 1, :]) for k in range(1, hop)
            ]:
                left, right = sources_of(k, n_voc)
                out_ref[q, pl.ds(left, 1), :] = lanes[:, : 2 * r]
                out_ref[q, pl.ds(right, 1), :] = lanes[:, 2 * r :]

    out_shape = jax.ShapeDtypeStruct((3, n_voc, 2 * r) if last else (3, n), jnp.float32)
    small = [pltpu.VMEM((rank, n), jnp.bfloat16)] + [pltpu.VMEM((8, n), jnp.float32)] * 3
    return pl.pallas_call(
        kernel,
        out_shape=(out_shape, out_shape) if carry else out_shape,
        in_specs=[WHOLE] * (pieces + 4 + 2 * carry + earlier),
        out_specs=(WHOLE, WHOLE) if carry else WHOLE,
        scratch_shapes=[
            pltpu.VMEM((depth, n), jnp.bfloat16),
            pltpu.VMEM((tile, n), jnp.float32),
            pltpu.VMEM((tile, n), jnp.float32),
        ]
        + small * (1 + carry),
        compiler_params=pltpu.CompilerParams(vmem_limit_bytes=8 * MIB),
        cost_estimate=pl.CostEstimate(
            flops=2 * n * entries * (depth + 256),
            bytes_accessed=2 * entries * (depth + LANES),
            transcendentals=n * entries,
        ),
        name="chunk",
    )


def make_combine(bits, r, n_voc, finish):
    low = bits & -bits
    count = bits // low + 1

    def kernel(*refs):
        parts, outs, held = refs[:count], refs[count:-1], refs[-1]
        slot = lax.rem(lax.axis_index("vocab") // low, count)
        for k in range(count):
            held[slot ^ k] = parts[k][...]
        top = held[0, 0]
        for k in range(1, count):
            top = jnp.maximum(top, held[k, 0])
        total = held[0, 1] * jnp.exp(held[0, 0] - top)
        pick = held[0, 2]
        for k in range(1, count):
            total = total + held[k, 1] * jnp.exp(held[k, 0] - top)
            pick = pick + held[k, 2]
        if not finish:
            for q, value in enumerate((top, total, pick)):
                outs[0][q] = value
            return
        log_total = top + jnp.log(total)
        for ref, value in zip(outs, (pick - log_total, log_total)):
            for k in range(n_voc):
                for s in range(2):
                    ref[s : s + 1, k * r : (k + 1) * r] = value[k : k + 1, s * r : (s + 1) * r]

    if finish:
        shape = (jax.ShapeDtypeStruct((2, n_voc * r), jnp.float32),) * 2
        specs = (WHOLE, WHOLE)
    else:
        shape, specs = jax.ShapeDtypeStruct((3, n_voc, 2 * r), jnp.float32), WHOLE
    return pl.pallas_call(
        kernel,
        out_shape=shape,
        in_specs=[WHOLE] * count,
        out_specs=specs,
        scratch_shapes=[pltpu.VMEM((count, 3, n_voc, 2 * r), jnp.float32)],
        compiler_params=pltpu.CompilerParams(vmem_limit_bytes=MIB),
        name="combine",
    )


def body(hidden, head, factor_u, factor_v, sampled):
    n_group = lax.axis_size("group")
    n_voc = lax.axis_size("vocab")
    _, r, depth = hidden.shape
    entries = head.shape[0]
    rank = factor_u.shape[1]
    per = n_voc // n_group
    half = n_voc // 2

    order = ring_order(n_voc)
    ahead = [(order[i], order[(i + 1) % n_voc]) for i in range(n_voc)]
    behind = [(b, a) for a, b in ahead]

    def trade(x, axis, size, bit):
        return lax.ppermute(x, axis, [(i, i ^ bit) for i in range(size)])

    u_rows, v_rows = factor_u.shape[0], factor_v.shape[0]
    everyone = [(g, v) for g in range(n_group) for v in range(n_voc)]
    moves = [
        (v * n_group + (g ^ (v // per) % n_group), g * n_voc + v) for g, v in everyone
    ]
    block = lax.ppermute(factor_u.T, ("group", "vocab"), moves)
    shards = []
    for t in range(per):
        moves = [
            ((v // per) % n_group * n_voc + g * per + (v % per ^ t), g * n_voc + v)
            for g, v in everyone
        ]
        shards.append(lax.ppermute(factor_v.T, ("group", "vocab"), moves))

    hidden, *shards = lax.optimization_barrier((hidden, *shards))
    up = [hidden, lax.ppermute(hidden, "vocab", ahead)]
    down = [hidden, lax.ppermute(hidden, "vocab", behind)]
    head, block = lax.optimization_barrier((make_load(depth, entries)(head), block))
    base, base_rows = make_base(r, depth, entries)(up[1], down[1], head)
    for hop in range(2, half):
        up.append(lax.ppermute(up[-1], "vocab", ahead))
        down.append(lax.ppermute(down[-1], "vocab", behind))
        if hop == 2:
            up[2], down[2], base = lax.optimization_barrier((up[2], down[2], base))
    ends = [
        lax.ppermute(up[-1][0], "vocab", ahead),
        lax.ppermute(down[-1][1], "vocab", behind),
    ]
    gap = ((0, 0), (0, padded(v_rows) - v_rows))
    packs = {0: jnp.concatenate([block] + [jnp.pad(x, gap) for x in shards], axis=1)}
    bit = n_group // 2
    while bit:
        for k in list(packs):
            packs[k ^ bit] = trade(packs[k], "group", n_group, bit)
        bit //= 2
    full_u, full_v, want = make_assemble(
        n_group, n_voc, u_rows, v_rows, rank, r, entries
    )(sampled, *[packs[k] for k in range(n_group)])

    stats = []
    for hop in range(2, half + 1):
        pieces = [up[hop], down[hop]] if hop < half else [hidden] + ends
        extra = [base, base_rows] if hop == 2 else stats if hop == half else []
        chunk = make_chunk(hop, len(pieces), r, depth, entries, rank, n_voc)
        out = chunk(*pieces, head, full_u, full_v, want, *extra)
        stats += [out[1], out[0]] if hop == 2 else [out]
    part = stats[-1]
    low = 1
    while low < n_voc:
        count = 2 if low == 1 else min(4, n_voc // low)
        bits = low * (count - 1)
        others = [trade(part, "vocab", n_voc, low * k) for k in range(1, count)]
        part = make_combine(bits, r, n_voc, low * count == n_voc)(part, *others)
        low *= count
    return part


def solution(mesh):
    in_specs = (
        P(None, ("group", "vocab"), None),
        P("vocab", None),
        P(("group", "vocab"), None),
        P("vocab", None),
        P(None, "group"),
    )
    out_specs = (P(None, "group"), P(None, "group"))
    return jax.shard_map(body, mesh=mesh, in_specs=in_specs, out_specs=out_specs, check_vma=False)
```

```python
import jax
import jax.numpy as jnp
from jax import lax
from jax.experimental import pallas as pl
from jax.experimental.pallas import tpu as pltpu
from jax.sharding import PartitionSpec as P

MIB = 1024 * 1024
LANES = 128
WHOLE = pl.BlockSpec(memory_space=pltpu.VMEM)


def ring_order(n):
    return [2 * i for i in range(n // 2)] + [2 * i + 1 for i in reversed(range(n // 2))]


def ring_position(device, n):
    return jnp.where(device % 2 == 0, device // 2, n - 1 - device // 2)


def ring_device(position, n):
    position = lax.rem(position + n, n)
    return jnp.where(position < n // 2, 2 * position, 2 * (n - 1 - position) + 1)


def tile_rows(entries):
    for rows in (512, 256, 128, 64, 32, 16):
        if entries % (2 * rows) == 0:
            return rows
    raise ValueError(entries)


def padded(size):
    return -(-size // LANES) * LANES


def make_assemble(n_group, n_voc, u_rows, v_rows, rank, r, entries):
    per = n_voc // n_group
    wide = padded(v_rows)

    def kernel(sampled_ref, *refs):
        packs = refs[:n_group]
        u_out, v_out, want_out, v_wide = refs[n_group:]
        group = lax.axis_index("group")
        voc = lax.axis_index("vocab")
        for k in range(n_group):
            member = group ^ k
            block = member ^ lax.rem(voc // per, n_group)
            start = pl.multiple_of(block * u_rows, u_rows)
            u_out[pl.ds(start, u_rows), :] = packs[k][:, :u_rows].T
            for t in range(per):
                shard = member * per + (lax.rem(voc, per) ^ t)
                at = u_rows + t * wide
                rows = packs[k][:, at : at + wide].astype(jnp.float32).T
                v_wide[pl.ds(pl.multiple_of(shard * v_rows, 8), v_rows), :] = rows[:v_rows]
        v_out[...] = v_wide[...].T.astype(jnp.bfloat16)
        for k in range(n_voc):
            for s in range(2):
                want_out[k, :, s * r : (s + 1) * r] = (
                    sampled_ref[s : s + 1, k * r : (k + 1) * r] - voc * entries
                )

    return pl.pallas_call(
        kernel,
        out_shape=(
            jax.ShapeDtypeStruct((n_group * u_rows, rank), jnp.bfloat16),
            jax.ShapeDtypeStruct((rank, n_voc * v_rows), jnp.bfloat16),
            jax.ShapeDtypeStruct((n_voc, 1, 2 * r), jnp.int32),
        ),
        in_specs=[WHOLE] * (1 + n_group),
        out_specs=(WHOLE,) * 3,
        scratch_shapes=[pltpu.VMEM((n_voc * v_rows, rank), jnp.float32)],
        compiler_params=pltpu.CompilerParams(vmem_limit_bytes=4 * MIB),
        name="assemble",
    )


def sources_of(hop, n_voc):
    position = ring_position(lax.axis_index("vocab"), n_voc)
    if hop < n_voc // 2:
        return ring_device(position - hop, n_voc), ring_device(position + hop, n_voc)
    return ring_device(position, n_voc), ring_device(position + hop, n_voc)


def load_rows(rows, pieces):
    at = 0
    for ref in pieces:
        block = ref[...].reshape(-1, ref.shape[-1])
        rows[:, at : at + block.shape[0]] = block.T
        at += block.shape[0]


def make_load(depth, entries):
    parts = 16 if entries % 4096 == 0 else 1
    part = entries // parts

    def kernel(head_ref, held, sems):
        spans = [pl.ds(t * part, part) for t in range(parts)]
        copies = [
            pltpu.make_async_copy(head_ref.at[span, :], held.at[span, :], sems.at[t])
            for t, span in enumerate(spans)
        ]
        for t, copy in enumerate(copies):
            copy.start(priority=t % 2)
        for copy in copies:
            copy.wait()

    return pl.pallas_call(
        kernel,
        out_shape=jax.ShapeDtypeStruct((entries, depth), jnp.bfloat16),
        in_specs=[pl.BlockSpec(memory_space=pltpu.HBM)],
        out_specs=WHOLE,
        scratch_shapes=[pltpu.SemaphoreType.DMA((parts,))],
        compiler_params=pltpu.CompilerParams(vmem_limit_bytes=32 * MIB),
        cost_estimate=pl.CostEstimate(
            flops=0, bytes_accessed=2 * depth * entries, transcendentals=0
        ),
        name="load",
    )


def make_base(r, depth, entries):
    n = 4 * r
    tile = tile_rows(entries)

    def kernel(up_ref, down_ref, head_ref, base_ref, rows):
        load_rows(rows, (up_ref, down_ref))

        @pl.loop(0, entries // tile)
        def _(i):
            span = pl.ds(pl.multiple_of(i * tile, tile), tile)
            base_ref[span, :] = jnp.dot(
                head_ref[span, :], rows[...], preferred_element_type=jnp.float32
            )

    return pl.pallas_call(
        kernel,
        out_shape=(
            jax.ShapeDtypeStruct((entries, n), jnp.float32),
            jax.ShapeDtypeStruct((depth, n), jnp.bfloat16),
        ),
        in_specs=[WHOLE] * 3,
        out_specs=(WHOLE,) * 2,
        compiler_params=pltpu.CompilerParams(vmem_limit_bytes=8 * MIB),
        cost_estimate=pl.CostEstimate(
            flops=2 * n * entries * depth,
            bytes_accessed=2 * entries * depth,
            transcendentals=0,
        ),
        name="base",
    )


def make_chunk(hop, pieces, r, depth, entries, rank, n_voc):
    tile = tile_rows(entries)
    tiles = entries // tile
    n = 4 * r
    carry, last = hop == 2, hop == n_voc // 2
    earlier = hop - 1 if last else 0

    def kernel(*refs):
        piece, refs = refs[:pieces], refs[pieces:]
        head_ref, u_ref, v_ref, want_ref, *refs = refs
        if carry:
            base_ref, base_rows, *refs = refs
        before, refs = refs[:earlier], refs[earlier:]
        out_ref, *refs = refs
        if carry:
            base_out, *refs = refs
        rows, even, odd, proj, top, total, pick, *refs = refs
        if carry:
            base_proj, base_top, base_total, base_pick = refs
            base_state = base_top, base_total, base_pick
        state = top, total, pick

        def project(source, into):
            into[...] = jnp.dot(
                v_ref[...], source[...], preferred_element_type=jnp.float32
            ).astype(jnp.bfloat16)

        def clear(top, total, pick):
            top[...] = jnp.full(top.shape, -1e30, jnp.float32)
            total[...] = jnp.zeros(total.shape, jnp.float32)
            pick[...] = jnp.zeros(pick.shape, jnp.float32)

        def wanted(k):
            left, right = sources_of(k, n_voc)
            return jnp.concatenate([want_ref[left], want_ref[right]], axis=1)

        load_rows(rows, piece)
        project(rows, proj)
        clear(*state)
        odd[...] = jnp.full(odd.shape, -1e30, jnp.float32)
        want = wanted(hop)
        if carry:
            project(base_rows, base_proj)
            clear(*base_state)
            base_want = wanted(1)

        def multiply(t, into):
            span = pl.ds(pl.multiple_of(t * tile, tile), tile)
            into[...] = jnp.dot(
                head_ref[span, :], rows[...], preferred_element_type=jnp.float32
            ) + jnp.dot(u_ref[span, :], proj[...], preferred_element_type=jnp.float32)

        def reduce(x, want, top, total, pick):
            entry = lax.broadcasted_iota(jnp.int32, (tile, n), 0)
            hit = jnp.where(entry == want, x, 0.0)
            x3 = x.reshape(tile // 8, 8, n)
            new = jnp.maximum(top[...], jnp.max(x3, axis=0))
            total[...] = total[...] * jnp.exp(top[...] - new) + jnp.sum(
                jnp.exp(x3 - new[None]), axis=0
            )
            pick[...] = pick[...] + jnp.sum(hit.reshape(tile // 8, 8, n), axis=0)
            top[...] = new

        def finish_base(t):
            if carry:
                span = pl.ds(pl.multiple_of(t * tile, tile), tile)
                x = base_ref[span, :] + jnp.dot(
                    u_ref[span, :], base_proj[...], preferred_element_type=jnp.float32
                )
                reduce(x, base_want - t * tile, *base_state)

        @pl.loop(0, tiles // 2)
        def _(i):
            multiply(2 * i, even)
            reduce(odd[...], want - jnp.where(i == 0, 1 << 29, (2 * i - 1) * tile), *state)
            finish_base(2 * i)
            multiply(2 * i + 1, odd)
            reduce(even[...], want - 2 * i * tile, *state)
            finish_base(2 * i + 1)

        reduce(odd[...], want - (entries - tile), *state)

        def results(top, total, pick):
            best = jnp.max(top[...], axis=0, keepdims=True)
            sums = jnp.sum(total[...] * jnp.exp(top[...] - best), axis=0, keepdims=True)
            return best, sums, jnp.sum(pick[...], axis=0, keepdims=True)

        if carry:
            for q, value in enumerate(results(*base_state)):
                base_out[q : q + 1, :] = value
        for q, value in enumerate(results(*state)):
            if not last:
                out_ref[q : q + 1, :] = value
                continue
            for k, lanes in [(hop, value)] + [
                (k, before[k - 1][q : q + 1, :]) for k in range(1, hop)
            ]:
                left, right = sources_of(k, n_voc)
                out_ref[q, pl.ds(left, 1), :] = lanes[:, : 2 * r]
                out_ref[q, pl.ds(right, 1), :] = lanes[:, 2 * r :]

    out_shape = jax.ShapeDtypeStruct((3, n_voc, 2 * r) if last else (3, n), jnp.float32)
    small = [pltpu.VMEM((rank, n), jnp.bfloat16)] + [pltpu.VMEM((8, n), jnp.float32)] * 3
    return pl.pallas_call(
        kernel,
        out_shape=(out_shape, out_shape) if carry else out_shape,
        in_specs=[WHOLE] * (pieces + 4 + 2 * carry + earlier),
        out_specs=(WHOLE, WHOLE) if carry else WHOLE,
        scratch_shapes=[
            pltpu.VMEM((depth, n), jnp.bfloat16),
            pltpu.VMEM((tile, n), jnp.float32),
            pltpu.VMEM((tile, n), jnp.float32),
        ]
        + small * (1 + carry),
        compiler_params=pltpu.CompilerParams(vmem_limit_bytes=8 * MIB),
        cost_estimate=pl.CostEstimate(
            flops=2 * n * entries * (depth + 256),
            bytes_accessed=2 * entries * (depth + LANES),
            transcendentals=n * entries,
        ),
        name="chunk",
    )


def make_combine(bits, r, n_voc, finish):
    low = bits & -bits
    count = bits // low + 1

    def kernel(*refs):
        parts, outs, held = refs[:count], refs[count:-1], refs[-1]
        slot = lax.rem(lax.axis_index("vocab") // low, count)
        for k in range(count):
            held[slot ^ k] = parts[k][...]
        top = held[0, 0]
        for k in range(1, count):
            top = jnp.maximum(top, held[k, 0])
        total = held[0, 1] * jnp.exp(held[0, 0] - top)
        pick = held[0, 2]
        for k in range(1, count):
            total = total + held[k, 1] * jnp.exp(held[k, 0] - top)
            pick = pick + held[k, 2]
        if not finish:
            for q, value in enumerate((top, total, pick)):
                outs[0][q] = value
            return
        log_total = top + jnp.log(total)
        for ref, value in zip(outs, (pick - log_total, log_total)):
            for k in range(n_voc):
                for s in range(2):
                    ref[s : s + 1, k * r : (k + 1) * r] = value[k : k + 1, s * r : (s + 1) * r]

    if finish:
        shape = (jax.ShapeDtypeStruct((2, n_voc * r), jnp.float32),) * 2
        specs = (WHOLE, WHOLE)
    else:
        shape, specs = jax.ShapeDtypeStruct((3, n_voc, 2 * r), jnp.float32), WHOLE
    return pl.pallas_call(
        kernel,
        out_shape=shape,
        in_specs=[WHOLE] * count,
        out_specs=specs,
        scratch_shapes=[pltpu.VMEM((count, 3, n_voc, 2 * r), jnp.float32)],
        compiler_params=pltpu.CompilerParams(vmem_limit_bytes=MIB),
        name="combine",
    )


def body(hidden, head, factor_u, factor_v, sampled):
    n_group = lax.axis_size("group")
    n_voc = lax.axis_size("vocab")
    _, r, depth = hidden.shape
    entries = head.shape[0]
    rank = factor_u.shape[1]
    per = n_voc // n_group
    half = n_voc // 2

    order = ring_order(n_voc)
    ahead = [(order[i], order[(i + 1) % n_voc]) for i in range(n_voc)]
    behind = [(b, a) for a, b in ahead]

    def trade(x, axis, size, bit):
        return lax.ppermute(x, axis, [(i, i ^ bit) for i in range(size)])

    u_rows, v_rows = factor_u.shape[0], factor_v.shape[0]
    everyone = [(g, v) for g in range(n_group) for v in range(n_voc)]
    moves = [
        (v * n_group + (g ^ (v // per) % n_group), g * n_voc + v) for g, v in everyone
    ]
    block = lax.ppermute(factor_u.T, ("group", "vocab"), moves)
    shards = []
    for t in range(per):
        moves = [
            ((v // per) % n_group * n_voc + g * per + (v % per ^ t), g * n_voc + v)
            for g, v in everyone
        ]
        shards.append(lax.ppermute(factor_v.T, ("group", "vocab"), moves))

    hidden, block, *shards = lax.optimization_barrier((hidden, block, *shards))
    up = [hidden, lax.ppermute(hidden, "vocab", ahead)]
    down = [hidden, lax.ppermute(hidden, "vocab", behind)]
    head, block = lax.optimization_barrier((make_load(depth, entries)(head), block))
    gap = ((0, 0), (0, padded(v_rows) - v_rows))
    packs = {0: jnp.concatenate([block] + [jnp.pad(x, gap) for x in shards], axis=1)}
    bit = n_group // 2
    while bit:
        for k in list(packs):
            packs[k ^ bit] = trade(packs[k], "group", n_group, bit)
        bit //= 2
    full_u, full_v, want = make_assemble(
        n_group, n_voc, u_rows, v_rows, rank, r, entries
    )(sampled, *[packs[k] for k in range(n_group)])
    base, base_rows = make_base(r, depth, entries)(up[1], down[1], head)
    for hop in range(2, half):
        up.append(lax.ppermute(up[-1], "vocab", ahead))
        down.append(lax.ppermute(down[-1], "vocab", behind))
        if hop == 2:
            up[2], down[2], base, full_u = lax.optimization_barrier(
                (up[2], down[2], base, full_u)
            )
    ends = [
        lax.ppermute(up[-1][0], "vocab", ahead),
        lax.ppermute(down[-1][1], "vocab", behind),
    ]
    stats = []
    for hop in range(2, half + 1):
        pieces = [up[hop], down[hop]] if hop < half else [hidden] + ends
        extra = [base, base_rows] if hop == 2 else stats if hop == half else []
        chunk = make_chunk(hop, len(pieces), r, depth, entries, rank, n_voc)
        out = chunk(*pieces, head, full_u, full_v, want, *extra)
        stats += [out[1], out[0]] if hop == 2 else [out]
    part = stats[-1]
    low = 1
    while low < n_voc:
        count = 2 if low == 1 else min(4, n_voc // low)
        bits = low * (count - 1)
        others = [trade(part, "vocab", n_voc, low * k) for k in range(1, count)]
        part = make_combine(bits, r, n_voc, low * count == n_voc)(part, *others)
        low *= count
    return part


def solution(mesh):
    in_specs = (
        P(None, ("group", "vocab"), None),
        P("vocab", None),
        P(("group", "vocab"), None),
        P("vocab", None),
        P(None, "group"),
    )
    out_specs = (P(None, "group"), P(None, "group"))
    return jax.shard_map(body, mesh=mesh, in_specs=in_specs, out_specs=out_specs, check_vma=False)
```

```python
import jax
import jax.numpy as jnp
from jax import lax
from jax.experimental import pallas as pl
from jax.experimental.pallas import tpu as pltpu
from jax.sharding import PartitionSpec as P

MIB = 1024 * 1024
LANES = 128
WHOLE = pl.BlockSpec(memory_space=pltpu.VMEM)


def ring_order(n):
    return [2 * i for i in range(n // 2)] + [2 * i + 1 for i in reversed(range(n // 2))]


def ring_position(device, n):
    return jnp.where(device % 2 == 0, device // 2, n - 1 - device // 2)


def ring_device(position, n):
    position = lax.rem(position + n, n)
    return jnp.where(position < n // 2, 2 * position, 2 * (n - 1 - position) + 1)


def tile_rows(entries):
    for rows in (512, 256, 128, 64, 32, 16):
        if entries % (2 * rows) == 0:
            return rows
    raise ValueError(entries)


def padded(size):
    return -(-size // LANES) * LANES


def make_assemble(n_group, n_voc, u_rows, v_rows, rank, r, entries):
    per = n_voc // n_group
    wide = padded(v_rows)

    def kernel(sampled_ref, *refs):
        packs = refs[:n_group]
        u_out, v_out, want_out, v_wide = refs[n_group:]
        group = lax.axis_index("group")
        voc = lax.axis_index("vocab")
        for k in range(n_group):
            member = group ^ k
            block = member ^ lax.rem(voc // per, n_group)
            start = pl.multiple_of(block * u_rows, u_rows)
            u_out[pl.ds(start, u_rows), :] = packs[k][:, :u_rows].T
            for t in range(per):
                shard = member * per + (lax.rem(voc, per) ^ t)
                at = u_rows + t * wide
                rows = packs[k][:, at : at + wide].astype(jnp.float32).T
                v_wide[pl.ds(pl.multiple_of(shard * v_rows, 8), v_rows), :] = rows[:v_rows]
        v_out[...] = v_wide[...].T.astype(jnp.bfloat16)
        for k in range(n_voc):
            for s in range(2):
                want_out[k, :, s * r : (s + 1) * r] = (
                    sampled_ref[s : s + 1, k * r : (k + 1) * r] - voc * entries
                )

    return pl.pallas_call(
        kernel,
        out_shape=(
            jax.ShapeDtypeStruct((n_group * u_rows, rank), jnp.bfloat16),
            jax.ShapeDtypeStruct((rank, n_voc * v_rows), jnp.bfloat16),
            jax.ShapeDtypeStruct((n_voc, 1, 2 * r), jnp.int32),
        ),
        in_specs=[WHOLE] * (1 + n_group),
        out_specs=(WHOLE,) * 3,
        scratch_shapes=[pltpu.VMEM((n_voc * v_rows, rank), jnp.float32)],
        compiler_params=pltpu.CompilerParams(vmem_limit_bytes=4 * MIB),
        name="assemble",
    )


def sources_of(hop, n_voc):
    position = ring_position(lax.axis_index("vocab"), n_voc)
    return ring_device(position + hop, n_voc), ring_device(position - hop + 1, n_voc)


def load_rows(rows, pieces):
    at = 0
    for ref in pieces:
        block = ref[...].reshape(-1, ref.shape[-1])
        rows[:, at : at + block.shape[0]] = block.T
        at += block.shape[0]


def make_load(depth, entries):
    parts = 16 if entries % 4096 == 0 else 1
    part = entries // parts

    def kernel(head_ref, held, sems):
        spans = [pl.ds(t * part, part) for t in range(parts)]
        copies = [
            pltpu.make_async_copy(head_ref.at[span, :], held.at[span, :], sems.at[t])
            for t, span in enumerate(spans)
        ]
        for t, copy in enumerate(copies):
            copy.start(priority=t % 2)
        for copy in copies:
            copy.wait()

    return pl.pallas_call(
        kernel,
        out_shape=jax.ShapeDtypeStruct((entries, depth), jnp.bfloat16),
        in_specs=[pl.BlockSpec(memory_space=pltpu.HBM)],
        out_specs=WHOLE,
        scratch_shapes=[pltpu.SemaphoreType.DMA((parts,))],
        compiler_params=pltpu.CompilerParams(vmem_limit_bytes=32 * MIB),
        cost_estimate=pl.CostEstimate(
            flops=0, bytes_accessed=2 * depth * entries, transcendentals=0
        ),
        name="load",
    )


def make_base(r, depth, entries):
    n = 4 * r
    tile = tile_rows(entries)

    def kernel(up_ref, down_ref, head_ref, base_ref, rows):
        load_rows(rows, (up_ref, down_ref))

        @pl.loop(0, entries // tile)
        def _(i):
            span = pl.ds(pl.multiple_of(i * tile, tile), tile)
            base_ref[span, :] = jnp.dot(
                head_ref[span, :], rows[...], preferred_element_type=jnp.float32
            )

    return pl.pallas_call(
        kernel,
        out_shape=(
            jax.ShapeDtypeStruct((entries, n), jnp.float32),
            jax.ShapeDtypeStruct((depth, n), jnp.bfloat16),
        ),
        in_specs=[WHOLE] * 3,
        out_specs=(WHOLE,) * 2,
        compiler_params=pltpu.CompilerParams(vmem_limit_bytes=8 * MIB),
        cost_estimate=pl.CostEstimate(
            flops=2 * n * entries * depth,
            bytes_accessed=2 * entries * depth,
            transcendentals=0,
        ),
        name="base",
    )


def make_chunk(hop, pieces, r, depth, entries, rank, n_voc):
    tile = tile_rows(entries)
    tiles = entries // tile
    n = 4 * r
    carry, last = hop == 2, hop == n_voc // 2
    earlier = hop - 1 if last else 0

    def kernel(*refs):
        piece, refs = refs[:pieces], refs[pieces:]
        head_ref, u_ref, v_ref, want_ref, *refs = refs
        if carry:
            base_ref, base_rows, *refs = refs
        before, refs = refs[:earlier], refs[earlier:]
        out_ref, *refs = refs
        if carry:
            base_out, *refs = refs
        rows, even, odd, proj, top, total, pick, *refs = refs
        if carry:
            base_proj, base_top, base_total, base_pick = refs
            base_state = base_top, base_total, base_pick
        state = top, total, pick

        def project(source, into):
            into[...] = jnp.dot(
                v_ref[...], source[...], preferred_element_type=jnp.float32
            ).astype(jnp.bfloat16)

        def clear(top, total, pick):
            top[...] = jnp.full(top.shape, -1e30, jnp.float32)
            total[...] = jnp.zeros(total.shape, jnp.float32)
            pick[...] = jnp.zeros(pick.shape, jnp.float32)

        def wanted(k):
            left, right = sources_of(k, n_voc)
            return jnp.concatenate([want_ref[left], want_ref[right]], axis=1)

        load_rows(rows, piece)
        project(rows, proj)
        clear(*state)
        odd[...] = jnp.full(odd.shape, -1e30, jnp.float32)
        want = wanted(hop)
        if carry:
            project(base_rows, base_proj)
            clear(*base_state)
            base_want = wanted(1)

        def multiply(t, into):
            span = pl.ds(pl.multiple_of(t * tile, tile), tile)
            into[...] = jnp.dot(
                head_ref[span, :], rows[...], preferred_element_type=jnp.float32
            ) + jnp.dot(u_ref[span, :], proj[...], preferred_element_type=jnp.float32)

        def reduce(x, want, top, total, pick):
            entry = lax.broadcasted_iota(jnp.int32, (tile, n), 0)
            hit = jnp.where(entry == want, x, 0.0)
            x3 = x.reshape(tile // 8, 8, n)
            new = jnp.maximum(top[...], jnp.max(x3, axis=0))
            total[...] = total[...] * jnp.exp(top[...] - new) + jnp.sum(
                jnp.exp(x3 - new[None]), axis=0
            )
            pick[...] = pick[...] + jnp.sum(hit.reshape(tile // 8, 8, n), axis=0)
            top[...] = new

        def finish_base(t):
            if carry:
                span = pl.ds(pl.multiple_of(t * tile, tile), tile)
                x = base_ref[span, :] + jnp.dot(
                    u_ref[span, :], base_proj[...], preferred_element_type=jnp.float32
                )
                reduce(x, base_want - t * tile, *base_state)

        @pl.loop(0, tiles // 2)
        def _(i):
            multiply(2 * i, even)
            reduce(odd[...], want - jnp.where(i == 0, 1 << 29, (2 * i - 1) * tile), *state)
            finish_base(2 * i)
            multiply(2 * i + 1, odd)
            reduce(even[...], want - 2 * i * tile, *state)
            finish_base(2 * i + 1)

        reduce(odd[...], want - (entries - tile), *state)

        def results(top, total, pick):
            best = jnp.max(top[...], axis=0, keepdims=True)
            sums = jnp.sum(total[...] * jnp.exp(top[...] - best), axis=0, keepdims=True)
            return best, sums, jnp.sum(pick[...], axis=0, keepdims=True)

        if carry:
            for q, value in enumerate(results(*base_state)):
                base_out[q : q + 1, :] = value
        for q, value in enumerate(results(*state)):
            if not last:
                out_ref[q : q + 1, :] = value
                continue
            for k, lanes in [(hop, value)] + [
                (k, before[k - 1][q : q + 1, :]) for k in range(1, hop)
            ]:
                left, right = sources_of(k, n_voc)
                out_ref[q, pl.ds(left, 1), :] = lanes[:, : 2 * r]
                out_ref[q, pl.ds(right, 1), :] = lanes[:, 2 * r :]

    out_shape = jax.ShapeDtypeStruct((3, n_voc, 2 * r) if last else (3, n), jnp.float32)
    small = [pltpu.VMEM((rank, n), jnp.bfloat16)] + [pltpu.VMEM((8, n), jnp.float32)] * 3
    return pl.pallas_call(
        kernel,
        out_shape=(out_shape, out_shape) if carry else out_shape,
        in_specs=[WHOLE] * (pieces + 4 + 2 * carry + earlier),
        out_specs=(WHOLE, WHOLE) if carry else WHOLE,
        scratch_shapes=[
            pltpu.VMEM((depth, n), jnp.bfloat16),
            pltpu.VMEM((tile, n), jnp.float32),
            pltpu.VMEM((tile, n), jnp.float32),
        ]
        + small * (1 + carry),
        compiler_params=pltpu.CompilerParams(vmem_limit_bytes=8 * MIB),
        cost_estimate=pl.CostEstimate(
            flops=2 * n * entries * (depth + 256),
            bytes_accessed=2 * entries * (depth + LANES),
            transcendentals=n * entries,
        ),
        name="chunk",
    )


def make_combine(bits, r, n_voc, finish):
    low = bits & -bits
    count = bits // low + 1

    def kernel(*refs):
        parts, outs, held = refs[:count], refs[count:-1], refs[-1]
        slot = lax.rem(lax.axis_index("vocab") // low, count)
        for k in range(count):
            held[slot ^ k] = parts[k][...]
        top = held[0, 0]
        for k in range(1, count):
            top = jnp.maximum(top, held[k, 0])
        total = held[0, 1] * jnp.exp(held[0, 0] - top)
        pick = held[0, 2]
        for k in range(1, count):
            total = total + held[k, 1] * jnp.exp(held[k, 0] - top)
            pick = pick + held[k, 2]
        if not finish:
            for q, value in enumerate((top, total, pick)):
                outs[0][q] = value
            return
        log_total = top + jnp.log(total)
        for ref, value in zip(outs, (pick - log_total, log_total)):
            for k in range(n_voc):
                for s in range(2):
                    ref[s : s + 1, k * r : (k + 1) * r] = value[k : k + 1, s * r : (s + 1) * r]

    if finish:
        shape = (jax.ShapeDtypeStruct((2, n_voc * r), jnp.float32),) * 2
        specs = (WHOLE, WHOLE)
    else:
        shape, specs = jax.ShapeDtypeStruct((3, n_voc, 2 * r), jnp.float32), WHOLE
    return pl.pallas_call(
        kernel,
        out_shape=shape,
        in_specs=[WHOLE] * count,
        out_specs=specs,
        scratch_shapes=[pltpu.VMEM((count, 3, n_voc, 2 * r), jnp.float32)],
        compiler_params=pltpu.CompilerParams(vmem_limit_bytes=MIB),
        name="combine",
    )


def body(hidden, head, factor_u, factor_v, sampled):
    n_group = lax.axis_size("group")
    n_voc = lax.axis_size("vocab")
    _, r, depth = hidden.shape
    entries = head.shape[0]
    rank = factor_u.shape[1]
    per = n_voc // n_group
    half = n_voc // 2

    order = ring_order(n_voc)
    ahead = [(order[i], order[(i + 1) % n_voc]) for i in range(n_voc)]
    behind = [(b, a) for a, b in ahead]

    def trade(x, axis, size, bit):
        return lax.ppermute(x, axis, [(i, i ^ bit) for i in range(size)])

    u_rows, v_rows = factor_u.shape[0], factor_v.shape[0]
    everyone = [(g, v) for g in range(n_group) for v in range(n_voc)]
    moves = [
        (v * n_group + (g ^ (v // per) % n_group), g * n_voc + v) for g, v in everyone
    ]
    block = lax.ppermute(factor_u.T, ("group", "vocab"), moves)
    shards = []
    for t in range(per):
        moves = [
            ((v // per) % n_group * n_voc + g * per + (v % per ^ t), g * n_voc + v)
            for g, v in everyone
        ]
        shards.append(lax.ppermute(factor_v.T, ("group", "vocab"), moves))

    up = [hidden, lax.ppermute(hidden, "vocab", behind)]
    head = make_load(depth, entries)(head)
    first, head, block, *shards = lax.optimization_barrier((hidden, head, block, *shards))
    down = [hidden, lax.ppermute(first, "vocab", ahead)]
    _, block, *shards = lax.optimization_barrier((up[1], block, *shards))
    gap = ((0, 0), (0, padded(v_rows) - v_rows))
    packs = {0: jnp.concatenate([block] + [jnp.pad(x, gap) for x in shards], axis=1)}
    bit = n_group // 2
    while bit:
        for k in list(packs):
            packs[k ^ bit] = trade(packs[k], "group", n_group, bit)
        bit //= 2
    full_u, full_v, want = make_assemble(
        n_group, n_voc, u_rows, v_rows, rank, r, entries
    )(sampled, *[packs[k] for k in range(n_group)])
    base, base_rows = make_base(r, depth, entries)(up[1], hidden, head)
    up.append(lax.ppermute(up[1], "vocab", behind))
    up[2], down[1], base, full_u = lax.optimization_barrier((up[2], down[1], base, full_u))
    stats = []
    for hop in range(2, half + 1):
        extra = [base, base_rows] if hop == 2 else stats if hop == half else []
        chunk = make_chunk(hop, 2, r, depth, entries, rank, n_voc)
        out = chunk(up[hop], down[hop - 1], head, full_u, full_v, want, *extra)
        stats += [out[1], out[0]] if hop == 2 else [out]
        if hop < half:
            up.append(lax.ppermute(up[-1], "vocab", behind))
            down.append(lax.ppermute(down[-1], "vocab", ahead))
            up[-1], down[-1], stats[-1] = lax.optimization_barrier((up[-1], down[-1], stats[-1]))
    part = stats[-1]
    low = 1
    while low < n_voc:
        count = 2 if low == 1 else min(4, n_voc // low)
        bits = low * (count - 1)
        others = [trade(part, "vocab", n_voc, low * k) for k in range(1, count)]
        part = make_combine(bits, r, n_voc, low * count == n_voc)(part, *others)
        low *= count
    return part


def solution(mesh):
    in_specs = (
        P(None, ("group", "vocab"), None),
        P("vocab", None),
        P(("group", "vocab"), None),
        P("vocab", None),
        P(None, "group"),
    )
    out_specs = (P(None, "group"), P(None, "group"))
    return jax.shard_map(body, mesh=mesh, in_specs=in_specs, out_specs=out_specs, check_vma=False)
```

```python
import jax
import jax.numpy as jnp
from jax import lax
from jax.experimental import pallas as pl
from jax.experimental.pallas import tpu as pltpu
from jax.sharding import PartitionSpec as P

MIB = 1024 * 1024
LANES = 128
WHOLE = pl.BlockSpec(memory_space=pltpu.VMEM)


def ring_order(n):
    return [2 * i for i in range(n // 2)] + [2 * i + 1 for i in reversed(range(n // 2))]


def ring_position(device, n):
    return jnp.where(device % 2 == 0, device // 2, n - 1 - device // 2)


def ring_device(position, n):
    position = lax.rem(position + n, n)
    return jnp.where(position < n // 2, 2 * position, 2 * (n - 1 - position) + 1)


def tile_rows(entries):
    for rows in (512, 256, 128, 64, 32, 16):
        if entries % (2 * rows) == 0:
            return rows
    raise ValueError(entries)


def padded(size):
    return -(-size // LANES) * LANES


def make_assemble(n_group, n_voc, u_rows, v_rows, rank, r, entries):
    per = n_voc // n_group
    wide = padded(v_rows)

    def kernel(sampled_ref, *refs):
        packs = refs[:n_group]
        u_out, v_out, want_out, v_wide = refs[n_group:]
        group = lax.axis_index("group")
        voc = lax.axis_index("vocab")
        for k in range(n_group):
            member = group ^ k
            block = member ^ lax.rem(voc // per, n_group)
            start = pl.multiple_of(block * u_rows, u_rows)
            u_out[pl.ds(start, u_rows), :] = packs[k][:, :u_rows].T
            for t in range(per):
                shard = member * per + (lax.rem(voc, per) ^ t)
                at = u_rows + t * wide
                rows = packs[k][:, at : at + wide].astype(jnp.float32).T
                v_wide[pl.ds(pl.multiple_of(shard * v_rows, 8), v_rows), :] = rows[:v_rows]
        v_out[...] = v_wide[...].T.astype(jnp.bfloat16)
        for k in range(n_voc):
            for s in range(2):
                want_out[k, :, s * r : (s + 1) * r] = (
                    sampled_ref[s : s + 1, k * r : (k + 1) * r] - voc * entries
                )

    return pl.pallas_call(
        kernel,
        out_shape=(
            jax.ShapeDtypeStruct((n_group * u_rows, rank), jnp.bfloat16),
            jax.ShapeDtypeStruct((rank, n_voc * v_rows), jnp.bfloat16),
            jax.ShapeDtypeStruct((n_voc, 1, 2 * r), jnp.int32),
        ),
        in_specs=[WHOLE] * (1 + n_group),
        out_specs=(WHOLE,) * 3,
        scratch_shapes=[pltpu.VMEM((n_voc * v_rows, rank), jnp.float32)],
        compiler_params=pltpu.CompilerParams(vmem_limit_bytes=4 * MIB),
        name="assemble",
    )


def sources_of(hop, n_voc):
    position = ring_position(lax.axis_index("vocab"), n_voc)
    return ring_device(position + hop, n_voc), ring_device(position - hop + 1, n_voc)


def load_rows(rows, pieces):
    at = 0
    for ref in pieces:
        block = ref[...].reshape(-1, ref.shape[-1])
        rows[:, at : at + block.shape[0]] = block.T
        at += block.shape[0]


def make_load(depth, entries):
    parts = 16 if entries % 4096 == 0 else 1
    part = entries // parts

    def kernel(head_ref, held, sems):
        spans = [pl.ds(t * part, part) for t in range(parts)]
        copies = [
            pltpu.make_async_copy(head_ref.at[span, :], held.at[span, :], sems.at[t])
            for t, span in enumerate(spans)
        ]
        for t, copy in enumerate(copies):
            copy.start(priority=t % 2)
        for copy in copies:
            copy.wait()

    return pl.pallas_call(
        kernel,
        out_shape=jax.ShapeDtypeStruct((entries, depth), jnp.bfloat16),
        in_specs=[pl.BlockSpec(memory_space=pltpu.HBM)],
        out_specs=WHOLE,
        scratch_shapes=[pltpu.SemaphoreType.DMA((parts,))],
        compiler_params=pltpu.CompilerParams(vmem_limit_bytes=32 * MIB),
        cost_estimate=pl.CostEstimate(
            flops=0, bytes_accessed=2 * depth * entries, transcendentals=0
        ),
        name="load",
    )


def make_base(r, depth, entries):
    n = 4 * r
    tile = tile_rows(entries)

    def kernel(up_ref, down_ref, head_ref, base_ref, rows):
        load_rows(rows, (up_ref, down_ref))

        @pl.loop(0, entries // tile)
        def _(i):
            span = pl.ds(pl.multiple_of(i * tile, tile), tile)
            base_ref[span, :] = jnp.dot(
                head_ref[span, :], rows[...], preferred_element_type=jnp.float32
            )

    return pl.pallas_call(
        kernel,
        out_shape=(
            jax.ShapeDtypeStruct((entries, n), jnp.float32),
            jax.ShapeDtypeStruct((depth, n), jnp.bfloat16),
        ),
        in_specs=[WHOLE] * 3,
        out_specs=(WHOLE,) * 2,
        compiler_params=pltpu.CompilerParams(vmem_limit_bytes=8 * MIB),
        cost_estimate=pl.CostEstimate(
            flops=2 * n * entries * depth,
            bytes_accessed=2 * entries * depth,
            transcendentals=0,
        ),
        name="base",
    )


def make_chunk(hop, r, depth, entries, rank, n_voc):
    tile = tile_rows(entries)
    tiles = entries // tile
    n = 4 * r
    carry, last = 2 * (hop == 3), hop == n_voc // 2
    earlier = hop - 1 if last else 0

    def kernel(*refs):
        piece, refs = refs[:2], refs[2:]
        head_ref, u_ref, v_ref, want_ref, *refs = refs
        bases, refs = refs[: 2 * carry], refs[2 * carry :]
        before, refs = refs[:earlier], refs[earlier:]
        (out_ref, *base_outs), refs = refs[: 1 + carry], refs[1 + carry :]
        rows, even, odd, *refs = refs
        (proj, *state), *base_scratch = [refs[4 * k : 4 * k + 4] for k in range(1 + carry)]

        def project(source, into):
            into[...] = jnp.dot(
                v_ref[...], source[...], preferred_element_type=jnp.float32
            ).astype(jnp.bfloat16)

        def clear(top, total, pick):
            top[...] = jnp.full(top.shape, -1e30, jnp.float32)
            total[...] = jnp.zeros(total.shape, jnp.float32)
            pick[...] = jnp.zeros(pick.shape, jnp.float32)

        def wanted(k):
            left, right = sources_of(k, n_voc)
            return jnp.concatenate([want_ref[left], want_ref[right]], axis=1)

        load_rows(rows, piece)
        project(rows, proj)
        clear(*state)
        odd[...] = jnp.full(odd.shape, -1e30, jnp.float32)
        want = wanted(hop)
        base_wants = []
        for k in range(carry):
            project(bases[2 * k + 1], base_scratch[k][0])
            clear(*base_scratch[k][1:])
            base_wants.append(wanted(k + 1))

        def multiply(t, into):
            span = pl.ds(pl.multiple_of(t * tile, tile), tile)
            into[...] = jnp.dot(
                head_ref[span, :], rows[...], preferred_element_type=jnp.float32
            ) + jnp.dot(u_ref[span, :], proj[...], preferred_element_type=jnp.float32)

        def reduce(x, want, top, total, pick):
            entry = lax.broadcasted_iota(jnp.int32, (tile, n), 0)
            hit = jnp.where(entry == want, x, 0.0)
            x3 = x.reshape(tile // 8, 8, n)
            new = jnp.maximum(top[...], jnp.max(x3, axis=0))
            total[...] = total[...] * jnp.exp(top[...] - new) + jnp.sum(
                jnp.exp(x3 - new[None]), axis=0
            )
            pick[...] = pick[...] + jnp.sum(hit.reshape(tile // 8, 8, n), axis=0)
            top[...] = new

        def finish_bases(t):
            span = pl.ds(pl.multiple_of(t * tile, tile), tile)
            for k in range(carry):
                base_proj, *base_state = base_scratch[k]
                x = bases[2 * k][span, :] + jnp.dot(
                    u_ref[span, :], base_proj[...], preferred_element_type=jnp.float32
                )
                reduce(x, base_wants[k] - t * tile, *base_state)

        @pl.loop(0, tiles // 2)
        def _(i):
            multiply(2 * i, even)
            reduce(odd[...], want - jnp.where(i == 0, 1 << 29, (2 * i - 1) * tile), *state)
            finish_bases(2 * i)
            multiply(2 * i + 1, odd)
            reduce(even[...], want - 2 * i * tile, *state)
            finish_bases(2 * i + 1)

        reduce(odd[...], want - (entries - tile), *state)

        def results(top, total, pick):
            best = jnp.max(top[...], axis=0, keepdims=True)
            sums = jnp.sum(total[...] * jnp.exp(top[...] - best), axis=0, keepdims=True)
            return best, sums, jnp.sum(pick[...], axis=0, keepdims=True)

        for k in range(carry):
            for q, value in enumerate(results(*base_scratch[k][1:])):
                base_outs[k][q : q + 1, :] = value
        for q, value in enumerate(results(*state)):
            if not last:
                out_ref[q : q + 1, :] = value
                continue
            for k, lanes in [(hop, value)] + [
                (k, before[k - 1][q : q + 1, :]) for k in range(1, hop)
            ]:
                left, right = sources_of(k, n_voc)
                out_ref[q, pl.ds(left, 1), :] = lanes[:, : 2 * r]
                out_ref[q, pl.ds(right, 1), :] = lanes[:, 2 * r :]

    out_shape = jax.ShapeDtypeStruct((3, n_voc, 2 * r) if last else (3, n), jnp.float32)
    small = [pltpu.VMEM((rank, n), jnp.bfloat16)] + [pltpu.VMEM((8, n), jnp.float32)] * 3
    return pl.pallas_call(
        kernel,
        out_shape=(out_shape,) * (1 + carry) if carry else out_shape,
        in_specs=[WHOLE] * (6 + 2 * carry + earlier),
        out_specs=(WHOLE,) * (1 + carry) if carry else WHOLE,
        scratch_shapes=[
            pltpu.VMEM((depth, n), jnp.bfloat16),
            pltpu.VMEM((tile, n), jnp.float32),
            pltpu.VMEM((tile, n), jnp.float32),
        ]
        + small * (1 + carry),
        compiler_params=pltpu.CompilerParams(vmem_limit_bytes=8 * MIB),
        cost_estimate=pl.CostEstimate(
            flops=2 * n * entries * (depth + 256),
            bytes_accessed=2 * entries * (depth + LANES),
            transcendentals=n * entries,
        ),
        name="chunk",
    )


def make_combine(bits, r, n_voc, finish):
    low = bits & -bits
    count = bits // low + 1

    def kernel(*refs):
        parts, outs, held = refs[:count], refs[count:-1], refs[-1]
        slot = lax.rem(lax.axis_index("vocab") // low, count)
        for k in range(count):
            held[slot ^ k] = parts[k][...]
        top = held[0, 0]
        for k in range(1, count):
            top = jnp.maximum(top, held[k, 0])
        total = held[0, 1] * jnp.exp(held[0, 0] - top)
        pick = held[0, 2]
        for k in range(1, count):
            total = total + held[k, 1] * jnp.exp(held[k, 0] - top)
            pick = pick + held[k, 2]
        if not finish:
            for q, value in enumerate((top, total, pick)):
                outs[0][q] = value
            return
        log_total = top + jnp.log(total)
        for ref, value in zip(outs, (pick - log_total, log_total)):
            for k in range(n_voc):
                for s in range(2):
                    ref[s : s + 1, k * r : (k + 1) * r] = value[k : k + 1, s * r : (s + 1) * r]

    if finish:
        shape = (jax.ShapeDtypeStruct((2, n_voc * r), jnp.float32),) * 2
        specs = (WHOLE, WHOLE)
    else:
        shape, specs = jax.ShapeDtypeStruct((3, n_voc, 2 * r), jnp.float32), WHOLE
    return pl.pallas_call(
        kernel,
        out_shape=shape,
        in_specs=[WHOLE] * count,
        out_specs=specs,
        scratch_shapes=[pltpu.VMEM((count, 3, n_voc, 2 * r), jnp.float32)],
        compiler_params=pltpu.CompilerParams(vmem_limit_bytes=MIB),
        name="combine",
    )


def body(hidden, head, factor_u, factor_v, sampled):
    n_group = lax.axis_size("group")
    n_voc = lax.axis_size("vocab")
    _, r, depth = hidden.shape
    entries = head.shape[0]
    rank = factor_u.shape[1]
    per = n_voc // n_group
    half = n_voc // 2

    order = ring_order(n_voc)
    ahead = [(order[i], order[(i + 1) % n_voc]) for i in range(n_voc)]
    behind = [(b, a) for a, b in ahead]

    def trade(x, axis, size, bit):
        return lax.ppermute(x, axis, [(i, i ^ bit) for i in range(size)])

    u_rows, v_rows = factor_u.shape[0], factor_v.shape[0]
    everyone = [(g, v) for g in range(n_group) for v in range(n_voc)]
    moves = [
        (v * n_group + (g ^ (v // per) % n_group), g * n_voc + v) for g, v in everyone
    ]
    block = lax.ppermute(factor_u.T, ("group", "vocab"), moves)
    shards = []
    for t in range(per):
        moves = [
            ((v // per) % n_group * n_voc + g * per + (v % per ^ t), g * n_voc + v)
            for g, v in everyone
        ]
        shards.append(lax.ppermute(factor_v.T, ("group", "vocab"), moves))

    head = make_load(depth, entries)(head)
    up = [hidden, lax.ppermute(hidden, "vocab", behind)]
    first, _ = lax.optimization_barrier((hidden, up[1]))
    down = [hidden, lax.ppermute(first, "vocab", ahead)]
    up.append(lax.ppermute(up[1], "vocab", behind))
    base, base_rows = make_base(r, depth, entries)(up[1], hidden, head)
    base, block, *shards = lax.optimization_barrier((base, block, *shards))
    held = [base, base_rows]
    gap = ((0, 0), (0, padded(v_rows) - v_rows))
    pack = jnp.concatenate([block] + [jnp.pad(x, gap) for x in shards], axis=1)
    up[2], down[1], held[0], pack = lax.optimization_barrier((up[2], down[1], held[0], pack))

    up.append(lax.ppermute(up[2], "vocab", behind))
    down.append(lax.ppermute(down[1], "vocab", ahead))
    packs = {0: pack}
    bit = n_group // 2
    while bit:
        for k in list(packs):
            packs[k ^ bit] = trade(packs[k], "group", n_group, bit)
        bit //= 2
    full_u, full_v, want = make_assemble(
        n_group, n_voc, u_rows, v_rows, rank, r, entries
    )(sampled, *[packs[k] for k in range(n_group)])
    held += make_base(r, depth, entries)(up[2], down[1], head)
    up[3], down[2], held[2], full_u = lax.optimization_barrier((up[3], down[2], held[2], full_u))

    stats = []
    for hop in range(3, half + 1):
        extra = held if hop == 3 else stats if hop == half else []
        chunk = make_chunk(hop, r, depth, entries, rank, n_voc)
        out = chunk(up[hop], down[hop - 1], head, full_u, full_v, want, *extra)
        stats += [out[1], out[2], out[0]] if hop == 3 else [out]
        if hop < half:
            up.append(lax.ppermute(up[-1], "vocab", behind))
            down.append(lax.ppermute(down[-1], "vocab", ahead))
            up[-1], down[-1], stats[-1] = lax.optimization_barrier((up[-1], down[-1], stats[-1]))
    part = stats[-1]
    low = 1
    while low < n_voc:
        count = 2 if low == 1 else min(4, n_voc // low)
        bits = low * (count - 1)
        others = [trade(part, "vocab", n_voc, low * k) for k in range(1, count)]
        part = make_combine(bits, r, n_voc, low * count == n_voc)(part, *others)
        low *= count
    return part


def solution(mesh):
    in_specs = (
        P(None, ("group", "vocab"), None),
        P("vocab", None),
        P(("group", "vocab"), None),
        P("vocab", None),
        P(None, "group"),
    )
    out_specs = (P(None, "group"), P(None, "group"))
    return jax.shard_map(body, mesh=mesh, in_specs=in_specs, out_specs=out_specs, check_vma=False)
```

```python
import jax
import jax.numpy as jnp
from jax import lax
from jax.experimental import pallas as pl
from jax.experimental.pallas import tpu as pltpu
from jax.sharding import PartitionSpec as P

MIB = 1024 * 1024
LANES = 128
WHOLE = pl.BlockSpec(memory_space=pltpu.VMEM)


def ring_order(n):
    return [2 * i for i in range(n // 2)] + [2 * i + 1 for i in reversed(range(n // 2))]


def ring_position(device, n):
    return jnp.where(device % 2 == 0, device // 2, n - 1 - device // 2)


def ring_device(position, n):
    position = lax.rem(position + n, n)
    return jnp.where(position < n // 2, 2 * position, 2 * (n - 1 - position) + 1)


def tile_rows(entries):
    for rows in (1024, 512, 256, 128, 64, 32, 16):
        if entries % (2 * rows) == 0:
            return rows
    raise ValueError(entries)


def padded(size):
    return -(-size // LANES) * LANES


def make_assemble(n_group, n_voc, u_rows, v_rows, rank, r, entries):
    per = n_voc // n_group
    wide = padded(v_rows)

    def kernel(sampled_ref, *refs):
        packs = refs[:n_group]
        u_out, v_out, want_out, v_wide = refs[n_group:]
        group = lax.axis_index("group")
        voc = lax.axis_index("vocab")
        for k in range(n_group):
            member = group ^ k
            block = member ^ lax.rem(voc // per, n_group)
            start = pl.multiple_of(block * u_rows, u_rows)
            u_out[pl.ds(start, u_rows), :] = packs[k][:, :u_rows].T
            for t in range(per):
                shard = member * per + (lax.rem(voc, per) ^ t)
                at = u_rows + t * wide
                rows = packs[k][:, at : at + wide].astype(jnp.float32).T
                v_wide[pl.ds(pl.multiple_of(shard * v_rows, 8), v_rows), :] = rows[:v_rows]
        v_out[...] = v_wide[...].T.astype(jnp.bfloat16)
        for k in range(n_voc):
            for s in range(2):
                want_out[k, :, s * r : (s + 1) * r] = (
                    sampled_ref[s : s + 1, k * r : (k + 1) * r] - voc * entries
                )

    return pl.pallas_call(
        kernel,
        out_shape=(
            jax.ShapeDtypeStruct((n_group * u_rows, rank), jnp.bfloat16),
            jax.ShapeDtypeStruct((rank, n_voc * v_rows), jnp.bfloat16),
            jax.ShapeDtypeStruct((n_voc, 1, 2 * r), jnp.int32),
        ),
        in_specs=[WHOLE] * (1 + n_group),
        out_specs=(WHOLE,) * 3,
        scratch_shapes=[pltpu.VMEM((n_voc * v_rows, rank), jnp.float32)],
        compiler_params=pltpu.CompilerParams(vmem_limit_bytes=4 * MIB),
        name="assemble",
    )


def sources_of(hop, n_voc):
    position = ring_position(lax.axis_index("vocab"), n_voc)
    return ring_device(position + hop, n_voc), ring_device(position - hop + 1, n_voc)


def load_rows(rows, pieces):
    at = 0
    for ref in pieces:
        block = ref[...].reshape(-1, ref.shape[-1])
        rows[:, at : at + block.shape[0]] = block.T
        at += block.shape[0]


def make_base(r, depth, entries, load):
    n = 4 * r
    tile = tile_rows(entries)
    tiles = entries // tile
    split = 2 if tile % 32 == 0 else 1
    part = tile // split

    def kernel(up_ref, down_ref, head_ref, base_ref, rows, *refs):
        held = head_ref
        if load:
            held, sems = refs

        def fetch(t):
            span = pl.ds(pl.multiple_of(t * part, part), part)
            return pltpu.make_async_copy(head_ref.at[span, :], held.at[span, :], sems.at[t])

        if load:
            for t in range(split * tiles):
                fetch(t).start(priority=t % 2)
        load_rows(rows, (up_ref, down_ref))

        @pl.loop(0, tiles)
        def _(i):
            if load:
                for k in range(split):
                    fetch(split * i + k).wait()
            span = pl.ds(pl.multiple_of(i * tile, tile), tile)
            base_ref[span, :] = jnp.dot(
                held[span, :], rows[...], preferred_element_type=jnp.float32
            )

    out_shape = [
        jax.ShapeDtypeStruct((entries, n), jnp.float32),
        jax.ShapeDtypeStruct((depth, n), jnp.bfloat16),
    ]
    if load:
        out_shape.append(jax.ShapeDtypeStruct((entries, depth), jnp.bfloat16))
    return pl.pallas_call(
        kernel,
        out_shape=tuple(out_shape),
        in_specs=[WHOLE, WHOLE, pl.BlockSpec(memory_space=pltpu.HBM) if load else WHOLE],
        out_specs=(WHOLE,) * len(out_shape),
        scratch_shapes=[pltpu.SemaphoreType.DMA((split * tiles,))] * load,
        compiler_params=pltpu.CompilerParams(vmem_limit_bytes=(23 if load else 8) * MIB),
        cost_estimate=pl.CostEstimate(
            flops=2 * n * entries * depth,
            bytes_accessed=2 * entries * depth,
            transcendentals=0,
        ),
        name="base",
    )


def make_chunk(hop, r, depth, entries, rank, n_voc):
    tile = tile_rows(entries)
    tiles = entries // tile
    n = 4 * r
    carry, last = 2 * (hop == 3), hop == n_voc // 2
    earlier = hop - 1 if last else 0

    def kernel(*refs):
        piece, refs = refs[:2], refs[2:]
        head_ref, u_ref, v_ref, want_ref, *refs = refs
        bases, refs = refs[: 2 * carry], refs[2 * carry :]
        before, refs = refs[:earlier], refs[earlier:]
        (out_ref, *base_outs), refs = refs[: 1 + carry], refs[1 + carry :]
        rows, even, odd, *refs = refs
        (proj, *state), *base_scratch = [refs[4 * k : 4 * k + 4] for k in range(1 + carry)]

        def project(source, into):
            into[...] = jnp.dot(
                v_ref[...], source[...], preferred_element_type=jnp.float32
            ).astype(jnp.bfloat16)

        def clear(top, total, pick):
            top[...] = jnp.full(top.shape, -1e30, jnp.float32)
            total[...] = jnp.zeros(total.shape, jnp.float32)
            pick[...] = jnp.zeros(pick.shape, jnp.float32)

        def wanted(k):
            left, right = sources_of(k, n_voc)
            return jnp.concatenate([want_ref[left], want_ref[right]], axis=1)

        load_rows(rows, piece)
        project(rows, proj)
        clear(*state)
        odd[...] = jnp.full(odd.shape, -1e30, jnp.float32)
        want = wanted(hop)
        base_wants = []
        for k in range(carry):
            project(bases[2 * k + 1], base_scratch[k][0])
            clear(*base_scratch[k][1:])
            base_wants.append(wanted(k + 1))

        def multiply(t, into):
            span = pl.ds(pl.multiple_of(t * tile, tile), tile)
            into[...] = jnp.dot(
                head_ref[span, :], rows[...], preferred_element_type=jnp.float32
            ) + jnp.dot(u_ref[span, :], proj[...], preferred_element_type=jnp.float32)

        def reduce(x, want, top, total, pick):
            entry = lax.broadcasted_iota(jnp.int32, (tile, n), 0)
            hit = jnp.where(entry == want, x, 0.0)
            x3 = x.reshape(tile // 8, 8, n)
            new = jnp.maximum(top[...], jnp.max(x3, axis=0))
            total[...] = total[...] * jnp.exp(top[...] - new) + jnp.sum(
                jnp.exp(x3 - new[None]), axis=0
            )
            pick[...] = pick[...] + jnp.sum(hit.reshape(tile // 8, 8, n), axis=0)
            top[...] = new

        def finish_bases(t):
            span = pl.ds(pl.multiple_of(t * tile, tile), tile)
            for k in range(carry):
                base_proj, *base_state = base_scratch[k]
                x = bases[2 * k][span, :] + jnp.dot(
                    u_ref[span, :], base_proj[...], preferred_element_type=jnp.float32
                )
                reduce(x, base_wants[k] - t * tile, *base_state)

        @pl.loop(0, tiles // 2)
        def _(i):
            multiply(2 * i, even)
            reduce(odd[...], want - jnp.where(i == 0, 1 << 29, (2 * i - 1) * tile), *state)
            finish_bases(2 * i)
            multiply(2 * i + 1, odd)
            reduce(even[...], want - 2 * i * tile, *state)
            finish_bases(2 * i + 1)

        reduce(odd[...], want - (entries - tile), *state)

        def results(top, total, pick):
            best = jnp.max(top[...], axis=0, keepdims=True)
            sums = jnp.sum(total[...] * jnp.exp(top[...] - best), axis=0, keepdims=True)
            return best, sums, jnp.sum(pick[...], axis=0, keepdims=True)

        for k in range(carry):
            for q, value in enumerate(results(*base_scratch[k][1:])):
                base_outs[k][q : q + 1, :] = value
        for q, value in enumerate(results(*state)):
            if not last:
                out_ref[q : q + 1, :] = value
                continue
            for k, lanes in [(hop, value)] + [
                (k, before[k - 1][q : q + 1, :]) for k in range(1, hop)
            ]:
                left, right = sources_of(k, n_voc)
                out_ref[q, pl.ds(left, 1), :] = lanes[:, : 2 * r]
                out_ref[q, pl.ds(right, 1), :] = lanes[:, 2 * r :]

    out_shape = jax.ShapeDtypeStruct((3, n_voc, 2 * r) if last else (3, n), jnp.float32)
    small = [pltpu.VMEM((rank, n), jnp.bfloat16)] + [pltpu.VMEM((8, n), jnp.float32)] * 3
    return pl.pallas_call(
        kernel,
        out_shape=(out_shape,) * (1 + carry) if carry else out_shape,
        in_specs=[WHOLE] * (6 + 2 * carry + earlier),
        out_specs=(WHOLE,) * (1 + carry) if carry else WHOLE,
        scratch_shapes=[
            pltpu.VMEM((depth, n), jnp.bfloat16),
            pltpu.VMEM((tile, n), jnp.float32),
            pltpu.VMEM((tile, n), jnp.float32),
        ]
        + small * (1 + carry),
        compiler_params=pltpu.CompilerParams(vmem_limit_bytes=8 * MIB),
        cost_estimate=pl.CostEstimate(
            flops=2 * n * entries * (depth + 256),
            bytes_accessed=2 * entries * (depth + LANES),
            transcendentals=n * entries,
        ),
        name="chunk",
    )


def make_combine(bits, r, n_voc, finish):
    low = bits & -bits
    count = bits // low + 1

    def kernel(*refs):
        parts, outs, held = refs[:count], refs[count:-1], refs[-1]
        slot = lax.rem(lax.axis_index("vocab") // low, count)
        for k in range(count):
            held[slot ^ k] = parts[k][...]
        top = held[0, 0]
        for k in range(1, count):
            top = jnp.maximum(top, held[k, 0])
        total = held[0, 1] * jnp.exp(held[0, 0] - top)
        pick = held[0, 2]
        for k in range(1, count):
            total = total + held[k, 1] * jnp.exp(held[k, 0] - top)
            pick = pick + held[k, 2]
        if not finish:
            for q, value in enumerate((top, total, pick)):
                outs[0][q] = value
            return
        log_total = top + jnp.log(total)
        for ref, value in zip(outs, (pick - log_total, log_total)):
            for k in range(n_voc):
                for s in range(2):
                    ref[s : s + 1, k * r : (k + 1) * r] = value[k : k + 1, s * r : (s + 1) * r]

    if finish:
        shape = (jax.ShapeDtypeStruct((2, n_voc * r), jnp.float32),) * 2
        specs = (WHOLE, WHOLE)
    else:
        shape, specs = jax.ShapeDtypeStruct((3, n_voc, 2 * r), jnp.float32), WHOLE
    return pl.pallas_call(
        kernel,
        out_shape=shape,
        in_specs=[WHOLE] * count,
        out_specs=specs,
        scratch_shapes=[pltpu.VMEM((count, 3, n_voc, 2 * r), jnp.float32)],
        compiler_params=pltpu.CompilerParams(vmem_limit_bytes=MIB),
        name="combine",
    )


def body(hidden, head, factor_u, factor_v, sampled):
    n_group = lax.axis_size("group")
    n_voc = lax.axis_size("vocab")
    _, r, depth = hidden.shape
    entries = head.shape[0]
    rank = factor_u.shape[1]
    per = n_voc // n_group
    half = n_voc // 2

    order = ring_order(n_voc)
    ahead = [(order[i], order[(i + 1) % n_voc]) for i in range(n_voc)]
    behind = [(b, a) for a, b in ahead]

    def trade(x, axis, size, bit):
        return lax.ppermute(x, axis, [(i, i ^ bit) for i in range(size)])

    u_rows, v_rows = factor_u.shape[0], factor_v.shape[0]
    everyone = [(g, v) for g in range(n_group) for v in range(n_voc)]
    moves = [
        (v * n_group + (g ^ (v // per) % n_group), g * n_voc + v) for g, v in everyone
    ]
    block = lax.ppermute(factor_u.T, ("group", "vocab"), moves)
    shards = []
    for t in range(per):
        moves = [
            ((v // per) % n_group * n_voc + g * per + (v % per ^ t), g * n_voc + v)
            for g, v in everyone
        ]
        shards.append(lax.ppermute(factor_v.T, ("group", "vocab"), moves))

    up = [hidden, lax.ppermute(hidden, "vocab", behind)]
    first, _ = lax.optimization_barrier((hidden, up[1]))
    down = [hidden, lax.ppermute(first, "vocab", ahead)]
    up.append(lax.ppermute(up[1], "vocab", behind))
    base, base_rows, head = make_base(r, depth, entries, True)(up[1], hidden, head)
    base, block, *shards = lax.optimization_barrier((base, block, *shards))
    held = [base, base_rows]
    gap = ((0, 0), (0, padded(v_rows) - v_rows))
    pack = jnp.concatenate([block] + [jnp.pad(x, gap) for x in shards], axis=1)
    up[2], down[1], held[0] = lax.optimization_barrier((up[2], down[1], held[0]))
    held += make_base(r, depth, entries, False)(up[2], down[1], head)
    held[2], pack = lax.optimization_barrier((held[2], pack))

    up.append(lax.ppermute(up[2], "vocab", behind))
    down.append(lax.ppermute(down[1], "vocab", ahead))
    packs = {0: pack}
    bit = n_group // 2
    while bit:
        for k in list(packs):
            packs[k ^ bit] = trade(packs[k], "group", n_group, bit)
        bit //= 2
    full_u, full_v, want = make_assemble(
        n_group, n_voc, u_rows, v_rows, rank, r, entries
    )(sampled, *[packs[k] for k in range(n_group)])
    up[3], down[2], held[2], full_u = lax.optimization_barrier((up[3], down[2], held[2], full_u))

    stats = []
    for hop in range(3, half + 1):
        extra = held if hop == 3 else stats if hop == half else []
        chunk = make_chunk(hop, r, depth, entries, rank, n_voc)
        out = chunk(up[hop], down[hop - 1], head, full_u, full_v, want, *extra)
        stats += [out[1], out[2], out[0]] if hop == 3 else [out]
        if hop < half:
            up.append(lax.ppermute(up[-1], "vocab", behind))
            down.append(lax.ppermute(down[-1], "vocab", ahead))
            up[-1], down[-1], stats[-1] = lax.optimization_barrier((up[-1], down[-1], stats[-1]))
    part = stats[-1]
    low = 1
    while low < n_voc:
        count = 2 if low == 1 else min(4, n_voc // low)
        bits = low * (count - 1)
        others = [trade(part, "vocab", n_voc, low * k) for k in range(1, count)]
        part = make_combine(bits, r, n_voc, low * count == n_voc)(part, *others)
        low *= count
    return part


def solution(mesh):
    in_specs = (
        P(None, ("group", "vocab"), None),
        P("vocab", None),
        P(("group", "vocab"), None),
        P("vocab", None),
        P(None, "group"),
    )
    out_specs = (P(None, "group"), P(None, "group"))
    return jax.shard_map(body, mesh=mesh, in_specs=in_specs, out_specs=out_specs, check_vma=False)
```

```python
import jax
import jax.numpy as jnp
from jax import lax
from jax.experimental import pallas as pl
from jax.experimental.pallas import tpu as pltpu
from jax.sharding import PartitionSpec as P

MIB = 1024 * 1024
LANES = 128
WHOLE = pl.BlockSpec(memory_space=pltpu.VMEM)


def ring_order(n):
    return [2 * i for i in range(n // 2)] + [2 * i + 1 for i in reversed(range(n // 2))]


def plane_of(member, n_group):
    return member // 2 + member % 2 * (n_group // 2)


def ring_position(device, n):
    return jnp.where(device % 2 == 0, device // 2, n - 1 - device // 2)


def ring_device(position, n):
    position = lax.rem(position + n, n)
    return jnp.where(position < n // 2, 2 * position, 2 * (n - 1 - position) + 1)


def tile_rows(entries):
    for rows in (1024, 512, 256, 128, 64, 32, 16):
        if entries % (2 * rows) == 0:
            return rows
    raise ValueError(entries)


def padded(size):
    return -(-size // LANES) * LANES


def make_assemble(n_group, n_voc, u_rows, v_rows, rank, r, entries):
    per = n_voc // n_group
    wide = padded(v_rows)

    def kernel(sampled_ref, *refs):
        packs = refs[:n_group]
        u_out, v_out, want_out, v_wide = refs[n_group:]
        group = lax.axis_index("group")
        voc = lax.axis_index("vocab")
        for k in range(n_group):
            member = group ^ k
            plane = lax.div(member, 2) + lax.rem(member, 2) * (n_group // 2)
            block = member ^ lax.rem(voc // per, n_group)
            start = pl.multiple_of(block * u_rows, u_rows)
            u_out[pl.ds(start, u_rows), :] = packs[k][:, :u_rows].T
            for t in range(per):
                shard = plane * per + (lax.rem(voc, per) ^ t)
                at = u_rows + t * wide
                rows = packs[k][:, at : at + wide].astype(jnp.float32).T
                v_wide[pl.ds(pl.multiple_of(shard * v_rows, 8), v_rows), :] = rows[:v_rows]
        v_out[...] = v_wide[...].T.astype(jnp.bfloat16)
        for k in range(n_voc):
            for s in range(2):
                want_out[k, :, s * r : (s + 1) * r] = (
                    sampled_ref[s : s + 1, k * r : (k + 1) * r] - voc * entries
                )

    return pl.pallas_call(
        kernel,
        out_shape=(
            jax.ShapeDtypeStruct((n_group * u_rows, rank), jnp.bfloat16),
            jax.ShapeDtypeStruct((rank, n_voc * v_rows), jnp.bfloat16),
            jax.ShapeDtypeStruct((n_voc, 1, 2 * r), jnp.int32),
        ),
        in_specs=[WHOLE] * (1 + n_group),
        out_specs=(WHOLE,) * 3,
        scratch_shapes=[pltpu.VMEM((n_voc * v_rows, rank), jnp.float32)],
        compiler_params=pltpu.CompilerParams(vmem_limit_bytes=4 * MIB),
        name="assemble",
    )


def sources_of(hop, n_voc):
    position = ring_position(lax.axis_index("vocab"), n_voc)
    return ring_device(position + hop, n_voc), ring_device(position - hop + 1, n_voc)


def load_rows(rows, pieces):
    at = 0
    for ref in pieces:
        block = ref[...].reshape(-1, ref.shape[-1])
        rows[:, at : at + block.shape[0]] = block.T
        at += block.shape[0]


def make_base(r, depth, entries, load):
    n = 4 * r
    tile = tile_rows(entries)
    tiles = entries // tile
    split = 2 if tile % 32 == 0 else 1
    part = tile // split

    def kernel(up_ref, down_ref, head_ref, base_ref, rows, *refs):
        held = head_ref
        if load:
            held, sems = refs

        def fetch(t):
            span = pl.ds(pl.multiple_of(t * part, part), part)
            return pltpu.make_async_copy(head_ref.at[span, :], held.at[span, :], sems.at[t])

        if load:
            for t in range(split * tiles):
                fetch(t).start(priority=t % 2)
        load_rows(rows, (up_ref, down_ref))

        @pl.loop(0, tiles)
        def _(i):
            if load:
                for k in range(split):
                    fetch(split * i + k).wait()
            span = pl.ds(pl.multiple_of(i * tile, tile), tile)
            base_ref[span, :] = jnp.dot(
                held[span, :], rows[...], preferred_element_type=jnp.float32
            )

    out_shape = [
        jax.ShapeDtypeStruct((entries, n), jnp.float32),
        jax.ShapeDtypeStruct((depth, n), jnp.bfloat16),
    ]
    if load:
        out_shape.append(jax.ShapeDtypeStruct((entries, depth), jnp.bfloat16))
    return pl.pallas_call(
        kernel,
        out_shape=tuple(out_shape),
        in_specs=[WHOLE, WHOLE, pl.BlockSpec(memory_space=pltpu.HBM) if load else WHOLE],
        out_specs=(WHOLE,) * len(out_shape),
        scratch_shapes=[pltpu.SemaphoreType.DMA((split * tiles,))] * load,
        compiler_params=pltpu.CompilerParams(vmem_limit_bytes=(23 if load else 8) * MIB),
        cost_estimate=pl.CostEstimate(
            flops=2 * n * entries * depth,
            bytes_accessed=2 * entries * depth,
            transcendentals=0,
        ),
        name="base",
    )


def make_chunk(hop, r, depth, entries, rank, n_voc):
    tile = tile_rows(entries)
    sizes = [tile] * (entries // tile - 1) + [tile // 2] * 2
    n = 4 * r
    carry, last = 2 * (hop == 3), hop == n_voc // 2
    earlier = hop - 1 if last else 0

    def kernel(*refs):
        piece, refs = refs[:2], refs[2:]
        head_ref, u_ref, v_ref, want_ref, *refs = refs
        bases, refs = refs[: 2 * carry], refs[2 * carry :]
        before, refs = refs[:earlier], refs[earlier:]
        (out_ref, *base_outs), refs = refs[: 1 + carry], refs[1 + carry :]
        rows, even, odd, *refs = refs
        (proj, *state), *base_scratch = [refs[4 * k : 4 * k + 4] for k in range(1 + carry)]

        def project(source, into):
            into[...] = jnp.dot(
                v_ref[...], source[...], preferred_element_type=jnp.float32
            ).astype(jnp.bfloat16)

        def clear(top, total, pick):
            top[...] = jnp.full(top.shape, -1e30, jnp.float32)
            total[...] = jnp.zeros(total.shape, jnp.float32)
            pick[...] = jnp.zeros(pick.shape, jnp.float32)

        def wanted(k):
            left, right = sources_of(k, n_voc)
            return jnp.concatenate([want_ref[left], want_ref[right]], axis=1)

        load_rows(rows, piece)
        project(rows, proj)
        clear(*state)
        want = wanted(hop)
        base_wants = []
        for k in range(carry):
            project(bases[2 * k + 1], base_scratch[k][0])
            clear(*base_scratch[k][1:])
            base_wants.append(wanted(k + 1))

        def multiply(start, size, into):
            span = slice(start, start + size)
            into[:size, :] = jnp.dot(
                head_ref[span, :], rows[...], preferred_element_type=jnp.float32
            ) + jnp.dot(u_ref[span, :], proj[...], preferred_element_type=jnp.float32)

        def reduce(x, want, top, total, pick):
            size = x.shape[0]
            entry = lax.broadcasted_iota(jnp.int32, (size, n), 0)
            hit = jnp.where(entry == want, x, 0.0)
            x3 = x.reshape(size // 8, 8, n)
            new = jnp.maximum(top[...], jnp.max(x3, axis=0))
            total[...] = total[...] * jnp.exp(top[...] - new) + jnp.sum(
                jnp.exp(x3 - new[None]), axis=0
            )
            pick[...] = pick[...] + jnp.sum(hit.reshape(size // 8, 8, n), axis=0)
            top[...] = new

        def finish_bases(start, size):
            span = slice(start, start + size)
            for k in range(carry):
                base_proj, *base_state = base_scratch[k]
                x = bases[2 * k][span, :] + jnp.dot(
                    u_ref[span, :], base_proj[...], preferred_element_type=jnp.float32
                )
                reduce(x, base_wants[k] - start, *base_state)

        start = 0
        for i, size in enumerate(sizes):
            multiply(start, size, (even, odd)[i % 2])
            if i:
                ahead = sizes[i - 1]
                reduce((even, odd)[(i - 1) % 2][:ahead, :], want - (start - ahead), *state)
            finish_bases(start, size)
            start += size
        reduce((even, odd)[(len(sizes) - 1) % 2][:size, :], want - (start - size), *state)

        def results(top, total, pick):
            best = jnp.max(top[...], axis=0, keepdims=True)
            sums = jnp.sum(total[...] * jnp.exp(top[...] - best), axis=0, keepdims=True)
            return best, sums, jnp.sum(pick[...], axis=0, keepdims=True)

        for k in range(carry):
            for q, value in enumerate(results(*base_scratch[k][1:])):
                base_outs[k][q : q + 1, :] = value
        for q, value in enumerate(results(*state)):
            if not last:
                out_ref[q : q + 1, :] = value
                continue
            for k, lanes in [(hop, value)] + [
                (k, before[k - 1][q : q + 1, :]) for k in range(1, hop)
            ]:
                left, right = sources_of(k, n_voc)
                out_ref[q, pl.ds(left, 1), :] = lanes[:, : 2 * r]
                out_ref[q, pl.ds(right, 1), :] = lanes[:, 2 * r :]

    out_shape = jax.ShapeDtypeStruct((3, n_voc, 2 * r) if last else (3, n), jnp.float32)
    small = [pltpu.VMEM((rank, n), jnp.bfloat16)] + [pltpu.VMEM((8, n), jnp.float32)] * 3
    return pl.pallas_call(
        kernel,
        out_shape=(out_shape,) * (1 + carry) if carry else out_shape,
        in_specs=[WHOLE] * (6 + 2 * carry + earlier),
        out_specs=(WHOLE,) * (1 + carry) if carry else WHOLE,
        scratch_shapes=[
            pltpu.VMEM((depth, n), jnp.bfloat16),
            pltpu.VMEM((tile, n), jnp.float32),
            pltpu.VMEM((tile, n), jnp.float32),
        ]
        + small * (1 + carry),
        compiler_params=pltpu.CompilerParams(vmem_limit_bytes=8 * MIB),
        cost_estimate=pl.CostEstimate(
            flops=2 * n * entries * (depth + 256),
            bytes_accessed=2 * entries * (depth + LANES),
            transcendentals=n * entries,
        ),
        name="chunk",
    )


def make_combine(bits, r, n_voc, finish):
    low = bits & -bits
    count = bits // low + 1

    def kernel(*refs):
        parts, outs, held = refs[:count], refs[count:-1], refs[-1]
        slot = lax.rem(lax.axis_index("vocab") // low, count)
        for k in range(count):
            held[slot ^ k] = parts[k][...]
        top = held[0, 0]
        for k in range(1, count):
            top = jnp.maximum(top, held[k, 0])
        total = held[0, 1] * jnp.exp(held[0, 0] - top)
        pick = held[0, 2]
        for k in range(1, count):
            total = total + held[k, 1] * jnp.exp(held[k, 0] - top)
            pick = pick + held[k, 2]
        if not finish:
            for q, value in enumerate((top, total, pick)):
                outs[0][q] = value
            return
        log_total = top + jnp.log(total)
        for ref, value in zip(outs, (pick - log_total, log_total)):
            for k in range(n_voc):
                for s in range(2):
                    ref[s : s + 1, k * r : (k + 1) * r] = value[k : k + 1, s * r : (s + 1) * r]

    if finish:
        shape = (jax.ShapeDtypeStruct((2, n_voc * r), jnp.float32),) * 2
        specs = (WHOLE, WHOLE)
    else:
        shape, specs = jax.ShapeDtypeStruct((3, n_voc, 2 * r), jnp.float32), WHOLE
    return pl.pallas_call(
        kernel,
        out_shape=shape,
        in_specs=[WHOLE] * count,
        out_specs=specs,
        scratch_shapes=[pltpu.VMEM((count, 3, n_voc, 2 * r), jnp.float32)],
        compiler_params=pltpu.CompilerParams(vmem_limit_bytes=MIB),
        name="combine",
    )


def body(hidden, head, factor_u, factor_v, sampled):
    n_group = lax.axis_size("group")
    n_voc = lax.axis_size("vocab")
    _, r, depth = hidden.shape
    entries = head.shape[0]
    rank = factor_u.shape[1]
    per = n_voc // n_group
    half = n_voc // 2

    order = ring_order(n_voc)
    ahead = [(order[i], order[(i + 1) % n_voc]) for i in range(n_voc)]
    behind = [(b, a) for a, b in ahead]

    def trade(x, axis, size, bit):
        return lax.ppermute(x, axis, [(i, i ^ bit) for i in range(size)])

    u_rows, v_rows = factor_u.shape[0], factor_v.shape[0]
    everyone = [(g, v) for g in range(n_group) for v in range(n_voc)]
    moves = [
        (v * n_group + (g ^ (v // per) % n_group), g * n_voc + v) for g, v in everyone
    ]
    block = lax.ppermute(factor_u.T, ("group", "vocab"), moves)
    shards = []
    for t in range(per):
        moves = [
            ((v // per) % n_group * n_voc + plane_of(g, n_group) * per + (v % per ^ t), g * n_voc + v)
            for g, v in everyone
        ]
        shards.append(lax.ppermute(factor_v.T.reshape(16, -1), ("group", "vocab"), moves))

    up = [hidden, lax.ppermute(hidden, "vocab", behind)]
    first, _ = lax.optimization_barrier((hidden, up[1]))
    down = [hidden, lax.ppermute(first, "vocab", ahead)]
    up.append(lax.ppermute(up[1], "vocab", behind))
    base, base_rows, head = make_base(r, depth, entries, True)(up[1], hidden, head)
    base, block, *shards = lax.optimization_barrier((base, block, *shards))
    held = [base, base_rows]
    gap = ((0, 0), (0, padded(v_rows) - v_rows))
    pack = jnp.concatenate([block] + [jnp.pad(x.reshape(rank, -1), gap) for x in shards], axis=1)
    up[2], held[0] = lax.optimization_barrier((up[2], held[0]))
    down[1], held[0] = lax.optimization_barrier((down[1], held[0]))
    held += make_base(r, depth, entries, False)(up[2], down[1], head)
    held[2], pack = lax.optimization_barrier((held[2], pack))

    up.append(lax.ppermute(up[2], "vocab", behind))
    down.append(lax.ppermute(down[1], "vocab", ahead))
    packs = {0: pack}
    bit = n_group // 2
    while bit:
        for k in list(packs):
            packs[k ^ bit] = trade(packs[k], "group", n_group, bit)
        bit //= 2
    full_u, full_v, want = make_assemble(
        n_group, n_voc, u_rows, v_rows, rank, r, entries
    )(sampled, *[packs[k] for k in range(n_group)])
    up[3], held[2], full_u = lax.optimization_barrier((up[3], held[2], full_u))
    down[2], full_u = lax.optimization_barrier((down[2], full_u))

    stats = []
    for hop in range(3, half + 1):
        extra = held if hop == 3 else stats if hop == half else []
        chunk = make_chunk(hop, r, depth, entries, rank, n_voc)
        out = chunk(up[hop], down[hop - 1], head, full_u, full_v, want, *extra)
        stats += [out[1], out[2], out[0]] if hop == 3 else [out]
        if hop < half:
            up.append(lax.ppermute(up[-1], "vocab", behind))
            down.append(lax.ppermute(down[-1], "vocab", ahead))
            up[-1], stats[-1] = lax.optimization_barrier((up[-1], stats[-1]))
            down[-1], stats[-1] = lax.optimization_barrier((down[-1], stats[-1]))
    part = stats[-1]
    low = 1
    while low < n_voc:
        count = 2 if low == 1 else min(4, n_voc // low)
        bits = low * (count - 1)
        others = [trade(part, "vocab", n_voc, low * k) for k in range(1, count)]
        part = make_combine(bits, r, n_voc, low * count == n_voc)(part, *others)
        low *= count
    return part


def solution(mesh):
    in_specs = (
        P(None, ("group", "vocab"), None),
        P("vocab", None),
        P(("group", "vocab"), None),
        P("vocab", None),
        P(None, "group"),
    )
    out_specs = (P(None, "group"), P(None, "group"))
    return jax.shard_map(body, mesh=mesh, in_specs=in_specs, out_specs=out_specs, check_vma=False)
```

```python
import jax
import jax.numpy as jnp
from jax import lax
from jax.experimental import pallas as pl
from jax.experimental.pallas import tpu as pltpu
from jax.sharding import PartitionSpec as P

MIB = 1024 * 1024
LANES = 128
WHOLE = pl.BlockSpec(memory_space=pltpu.VMEM)


def ring_order(n):
    return [2 * i for i in range(n // 2)] + [2 * i + 1 for i in reversed(range(n // 2))]


def swapped(member, n_group):
    return member // 2 + member % 2 * (n_group // 2)


def ring_position(device, n):
    return jnp.where(device % 2 == 0, device // 2, n - 1 - device // 2)


def ring_device(position, n):
    position = lax.rem(position + n, n)
    return jnp.where(position < n // 2, 2 * position, 2 * (n - 1 - position) + 1)


def tile_rows(entries):
    for rows in (1024, 512, 256, 128, 64, 32, 16):
        if entries % (2 * rows) == 0:
            return rows
    raise ValueError(entries)


def padded(size):
    return -(-size // LANES) * LANES


def make_assemble(n_group, n_voc, u_rows, v_rows, rank, r, entries):
    per = n_voc // n_group
    wide = padded(v_rows)

    def kernel(sampled_ref, *refs):
        packs = refs[:n_group]
        u_out, v_out, want_out, v_wide = refs[n_group:]
        group = lax.axis_index("group")
        voc = lax.axis_index("vocab")
        for k in range(n_group):
            member = group ^ k
            plane = member ^ swapped(voc // per, n_group)
            block = swapped(member, n_group)
            start = pl.multiple_of(block * u_rows, u_rows)
            u_out[pl.ds(start, u_rows), :] = packs[k][:, :u_rows].T
            for t in range(per):
                shard = plane * per + (lax.rem(voc, per) ^ t)
                at = u_rows + t * wide
                rows = packs[k][:, at : at + wide].astype(jnp.float32).T
                v_wide[pl.ds(pl.multiple_of(shard * v_rows, 8), v_rows), :] = rows[:v_rows]
        v_out[...] = v_wide[...].T.astype(jnp.bfloat16)
        for k in range(n_voc):
            for s in range(2):
                want_out[k, :, s * r : (s + 1) * r] = (
                    sampled_ref[s : s + 1, k * r : (k + 1) * r] - voc * entries
                )

    return pl.pallas_call(
        kernel,
        out_shape=(
            jax.ShapeDtypeStruct((n_group * u_rows, rank), jnp.bfloat16),
            jax.ShapeDtypeStruct((rank, n_voc * v_rows), jnp.bfloat16),
            jax.ShapeDtypeStruct((n_voc, 1, 2 * r), jnp.int32),
        ),
        in_specs=[WHOLE] * (1 + n_group),
        out_specs=(WHOLE,) * 3,
        scratch_shapes=[pltpu.VMEM((n_voc * v_rows, rank), jnp.float32)],
        compiler_params=pltpu.CompilerParams(vmem_limit_bytes=4 * MIB),
        name="assemble",
    )


def sources_of(hop, n_voc):
    position = ring_position(lax.axis_index("vocab"), n_voc)
    return ring_device(position + hop, n_voc), ring_device(position - hop + 1, n_voc)


def load_rows(rows, pieces):
    at = 0
    for ref in pieces:
        block = ref[...].reshape(-1, ref.shape[-1])
        rows[:, at : at + block.shape[0]] = block.T
        at += block.shape[0]


def make_base(r, depth, entries, load):
    n = 4 * r
    tile = tile_rows(entries)
    tiles = entries // tile
    split = 2 if tile % 32 == 0 else 1
    part = tile // split

    def kernel(up_ref, down_ref, head_ref, base_ref, rows, *refs):
        held = head_ref
        if load:
            held, sems = refs

        def fetch(t):
            span = pl.ds(pl.multiple_of(t * part, part), part)
            return pltpu.make_async_copy(head_ref.at[span, :], held.at[span, :], sems.at[t])

        if load:
            for t in range(split * tiles):
                fetch(t).start(priority=t % 2)
        load_rows(rows, (up_ref, down_ref))

        @pl.loop(0, tiles)
        def _(i):
            if load:
                for k in range(split):
                    fetch(split * i + k).wait()
            span = pl.ds(pl.multiple_of(i * tile, tile), tile)
            base_ref[span, :] = jnp.dot(
                held[span, :], rows[...], preferred_element_type=jnp.float32
            )

    out_shape = [
        jax.ShapeDtypeStruct((entries, n), jnp.float32),
        jax.ShapeDtypeStruct((depth, n), jnp.bfloat16),
    ]
    if load:
        out_shape.append(jax.ShapeDtypeStruct((entries, depth), jnp.bfloat16))
    return pl.pallas_call(
        kernel,
        out_shape=tuple(out_shape),
        in_specs=[WHOLE, WHOLE, pl.BlockSpec(memory_space=pltpu.HBM) if load else WHOLE],
        out_specs=(WHOLE,) * len(out_shape),
        scratch_shapes=[pltpu.SemaphoreType.DMA((split * tiles,))] * load,
        compiler_params=pltpu.CompilerParams(vmem_limit_bytes=(23 if load else 8) * MIB),
        cost_estimate=pl.CostEstimate(
            flops=2 * n * entries * depth,
            bytes_accessed=2 * entries * depth,
            transcendentals=0,
        ),
        name="base",
    )


def make_chunk(hop, r, depth, entries, rank, n_voc):
    tile = tile_rows(entries)
    sizes = [tile] * (entries // tile - 1) + [tile // 2] * 2
    n = 4 * r
    carry, last = 2 * (hop == 3), hop == n_voc // 2
    earlier = hop - 1 if last else 0

    def kernel(*refs):
        piece, refs = refs[:2], refs[2:]
        head_ref, u_ref, v_ref, want_ref, *refs = refs
        bases, refs = refs[: 2 * carry], refs[2 * carry :]
        before, refs = refs[:earlier], refs[earlier:]
        (out_ref, *base_outs), refs = refs[: 1 + carry], refs[1 + carry :]
        rows, even, odd, *refs = refs
        (proj, *state), *base_scratch = [refs[4 * k : 4 * k + 4] for k in range(1 + carry)]

        def project(source, into):
            into[...] = jnp.dot(
                v_ref[...], source[...], preferred_element_type=jnp.float32
            ).astype(jnp.bfloat16)

        def clear(top, total, pick):
            top[...] = jnp.full(top.shape, -1e30, jnp.float32)
            total[...] = jnp.zeros(total.shape, jnp.float32)
            pick[...] = jnp.zeros(pick.shape, jnp.float32)

        def wanted(k):
            left, right = sources_of(k, n_voc)
            return jnp.concatenate([want_ref[left], want_ref[right]], axis=1)

        load_rows(rows, piece)
        project(rows, proj)
        clear(*state)
        want = wanted(hop)
        base_wants = []
        for k in range(carry):
            project(bases[2 * k + 1], base_scratch[k][0])
            clear(*base_scratch[k][1:])
            base_wants.append(wanted(k + 1))

        def multiply(start, size, into):
            span = slice(start, start + size)
            into[:size, :] = jnp.dot(
                head_ref[span, :], rows[...], preferred_element_type=jnp.float32
            ) + jnp.dot(u_ref[span, :], proj[...], preferred_element_type=jnp.float32)

        def reduce(x, want, top, total, pick):
            size = x.shape[0]
            entry = lax.broadcasted_iota(jnp.int32, (size, n), 0)
            hit = jnp.where(entry == want, x, 0.0)
            x3 = x.reshape(size // 8, 8, n)
            new = jnp.maximum(top[...], jnp.max(x3, axis=0))
            total[...] = total[...] * jnp.exp(top[...] - new) + jnp.sum(
                jnp.exp(x3 - new[None]), axis=0
            )
            pick[...] = pick[...] + jnp.sum(hit.reshape(size // 8, 8, n), axis=0)
            top[...] = new

        def finish_bases(start, size):
            span = slice(start, start + size)
            for k in range(carry):
                base_proj, *base_state = base_scratch[k]
                x = bases[2 * k][span, :] + jnp.dot(
                    u_ref[span, :], base_proj[...], preferred_element_type=jnp.float32
                )
                reduce(x, base_wants[k] - start, *base_state)

        start = 0
        for i, size in enumerate(sizes):
            multiply(start, size, (even, odd)[i % 2])
            if i:
                ahead = sizes[i - 1]
                reduce((even, odd)[(i - 1) % 2][:ahead, :], want - (start - ahead), *state)
            finish_bases(start, size)
            start += size
        reduce((even, odd)[(len(sizes) - 1) % 2][:size, :], want - (start - size), *state)

        def results(top, total, pick):
            best = jnp.max(top[...], axis=0, keepdims=True)
            sums = jnp.sum(total[...] * jnp.exp(top[...] - best), axis=0, keepdims=True)
            return best, sums, jnp.sum(pick[...], axis=0, keepdims=True)

        for k in range(carry):
            for q, value in enumerate(results(*base_scratch[k][1:])):
                base_outs[k][q : q + 1, :] = value
        for q, value in enumerate(results(*state)):
            if not last:
                out_ref[q : q + 1, :] = value
                continue
            for k, lanes in [(hop, value)] + [
                (k, before[k - 1][q : q + 1, :]) for k in range(1, hop)
            ]:
                left, right = sources_of(k, n_voc)
                out_ref[q, pl.ds(left, 1), :] = lanes[:, : 2 * r]
                out_ref[q, pl.ds(right, 1), :] = lanes[:, 2 * r :]

    out_shape = jax.ShapeDtypeStruct((3, n_voc, 2 * r) if last else (3, n), jnp.float32)
    small = [pltpu.VMEM((rank, n), jnp.bfloat16)] + [pltpu.VMEM((8, n), jnp.float32)] * 3
    return pl.pallas_call(
        kernel,
        out_shape=(out_shape,) * (1 + carry) if carry else out_shape,
        in_specs=[WHOLE] * (6 + 2 * carry + earlier),
        out_specs=(WHOLE,) * (1 + carry) if carry else WHOLE,
        scratch_shapes=[
            pltpu.VMEM((depth, n), jnp.bfloat16),
            pltpu.VMEM((tile, n), jnp.float32),
            pltpu.VMEM((tile, n), jnp.float32),
        ]
        + small * (1 + carry),
        compiler_params=pltpu.CompilerParams(vmem_limit_bytes=8 * MIB),
        cost_estimate=pl.CostEstimate(
            flops=2 * n * entries * (depth + 256),
            bytes_accessed=2 * entries * (depth + LANES),
            transcendentals=n * entries,
        ),
        name="chunk",
    )


def make_combine(bits, r, n_voc, finish):
    low = bits & -bits
    count = bits // low + 1

    def kernel(*refs):
        parts, outs, held = refs[:count], refs[count:-1], refs[-1]
        slot = lax.rem(lax.axis_index("vocab") // low, count)
        for k in range(count):
            held[slot ^ k] = parts[k][...]
        top = held[0, 0]
        for k in range(1, count):
            top = jnp.maximum(top, held[k, 0])
        total = held[0, 1] * jnp.exp(held[0, 0] - top)
        pick = held[0, 2]
        for k in range(1, count):
            total = total + held[k, 1] * jnp.exp(held[k, 0] - top)
            pick = pick + held[k, 2]
        if not finish:
            for q, value in enumerate((top, total, pick)):
                outs[0][q] = value
            return
        log_total = top + jnp.log(total)
        for ref, value in zip(outs, (pick - log_total, log_total)):
            for k in range(n_voc):
                for s in range(2):
                    ref[s : s + 1, k * r : (k + 1) * r] = value[k : k + 1, s * r : (s + 1) * r]

    if finish:
        shape = (jax.ShapeDtypeStruct((2, n_voc * r), jnp.float32),) * 2
        specs = (WHOLE, WHOLE)
    else:
        shape, specs = jax.ShapeDtypeStruct((3, n_voc, 2 * r), jnp.float32), WHOLE
    return pl.pallas_call(
        kernel,
        out_shape=shape,
        in_specs=[WHOLE] * count,
        out_specs=specs,
        scratch_shapes=[pltpu.VMEM((count, 3, n_voc, 2 * r), jnp.float32)],
        compiler_params=pltpu.CompilerParams(vmem_limit_bytes=MIB),
        name="combine",
    )


def body(hidden, head, factor_u, factor_v, sampled):
    n_group = lax.axis_size("group")
    n_voc = lax.axis_size("vocab")
    _, r, depth = hidden.shape
    entries = head.shape[0]
    rank = factor_u.shape[1]
    per = n_voc // n_group
    half = n_voc // 2

    order = ring_order(n_voc)
    ahead = [(order[i], order[(i + 1) % n_voc]) for i in range(n_voc)]
    behind = [(b, a) for a, b in ahead]

    def trade(x, axis, size, bit):
        return lax.ppermute(x, axis, [(i, i ^ bit) for i in range(size)])

    u_rows, v_rows = factor_u.shape[0], factor_v.shape[0]
    everyone = [(g, v) for g in range(n_group) for v in range(n_voc)]
    moves = [
        (v * n_group + swapped(g, n_group), g * n_voc + v) for g, v in everyone
    ]
    block = lax.ppermute(factor_u.T, ("group", "vocab"), moves)
    shards = []
    for t in range(per):
        moves = []
        for g, v in everyone:
            z = v // per
            plane = g ^ swapped(z, n_group)
            moves.append((z * n_voc + plane * per + (v % per ^ t), g * n_voc + v))
        shards.append(lax.ppermute(factor_v.T, ("group", "vocab"), moves))

    up = [hidden, lax.ppermute(hidden, "vocab", behind)]
    down = [hidden, lax.ppermute(hidden, "vocab", ahead)]
    up.append(lax.ppermute(up[1], "vocab", behind))
    base, base_rows, head = make_base(r, depth, entries, True)(up[1], hidden, head)
    base, block, *shards = lax.optimization_barrier((base, block, *shards))
    held = [base, base_rows]
    gap = ((0, 0), (0, padded(v_rows) - v_rows))
    pack = jnp.concatenate([block] + [jnp.pad(x, gap) for x in shards], axis=1)
    down[1], held[0] = lax.optimization_barrier((down[1], held[0]))
    up[2], held[0] = lax.optimization_barrier((up[2], held[0]))
    held += make_base(r, depth, entries, False)(up[2], down[1], head)
    held[2], pack = lax.optimization_barrier((held[2], pack))

    up.append(lax.ppermute(up[2], "vocab", behind))
    down.append(lax.ppermute(down[1], "vocab", ahead))
    packs = {0: pack}
    bit = n_group // 2
    while bit:
        for k in list(packs):
            packs[k ^ bit] = trade(packs[k], "group", n_group, bit)
        bit //= 2
    full_u, full_v, want = make_assemble(
        n_group, n_voc, u_rows, v_rows, rank, r, entries
    )(sampled, *[packs[k] for k in range(n_group)])
    down[2], full_u = lax.optimization_barrier((down[2], full_u))
    up[3], held[2], full_u = lax.optimization_barrier((up[3], held[2], full_u))

    stats = []
    for hop in range(3, half + 1):
        extra = held if hop == 3 else stats if hop == half else []
        chunk = make_chunk(hop, r, depth, entries, rank, n_voc)
        out = chunk(up[hop], down[hop - 1], head, full_u, full_v, want, *extra)
        stats += [out[1], out[2], out[0]] if hop == 3 else [out]
        if hop < half:
            up.append(lax.ppermute(up[-1], "vocab", behind))
            down.append(lax.ppermute(down[-1], "vocab", ahead))
            down[-1], stats[-1] = lax.optimization_barrier((down[-1], stats[-1]))
            up[-1], stats[-1] = lax.optimization_barrier((up[-1], stats[-1]))
    part = stats[-1]
    low = 1
    while low < n_voc:
        count = 2 if low == 1 else min(4, n_voc // low)
        bits = low * (count - 1)
        others = [trade(part, "vocab", n_voc, low * k) for k in range(1, count)]
        part = make_combine(bits, r, n_voc, low * count == n_voc)(part, *others)
        low *= count
    return part


def solution(mesh):
    in_specs = (
        P(None, ("group", "vocab"), None),
        P("vocab", None),
        P(("group", "vocab"), None),
        P("vocab", None),
        P(None, "group"),
    )
    out_specs = (P(None, "group"), P(None, "group"))
    return jax.shard_map(body, mesh=mesh, in_specs=in_specs, out_specs=out_specs, check_vma=False)
```

```python
import jax
import jax.numpy as jnp
from jax import lax
from jax.experimental import pallas as pl
from jax.experimental.pallas import tpu as pltpu
from jax.sharding import PartitionSpec as P

MIB = 1024 * 1024
LANES = 128
WHOLE = pl.BlockSpec(memory_space=pltpu.VMEM)


def ring_order(n):
    return [2 * i for i in range(n // 2)] + [2 * i + 1 for i in reversed(range(n // 2))]


def swapped(member, n_group):
    return member // 2 + member % 2 * (n_group // 2)


def ring_position(device, n):
    return jnp.where(device % 2 == 0, device // 2, n - 1 - device // 2)


def ring_device(position, n):
    position = lax.rem(position + n, n)
    return jnp.where(position < n // 2, 2 * position, 2 * (n - 1 - position) + 1)


def tile_rows(entries):
    for rows in (1024, 512, 256, 128, 64, 32, 16):
        if entries % (2 * rows) == 0:
            return rows
    raise ValueError(entries)


def padded(size):
    return -(-size // LANES) * LANES


def make_assemble(n_group, n_voc, u_rows, v_rows, rank, r, entries):
    per = n_voc // n_group
    wide = padded(v_rows)

    def kernel(sampled_ref, *refs):
        packs = refs[:n_group]
        u_out, v_out, want_out, v_wide = refs[n_group:]
        group = lax.axis_index("group")
        voc = lax.axis_index("vocab")
        for k in range(n_group):
            member = group ^ k
            plane = member ^ swapped(voc // per, n_group)
            block = swapped(member, n_group)
            start = pl.multiple_of(block * u_rows, u_rows)
            u_out[pl.ds(start, u_rows), :] = packs[k][:, :u_rows].T
            for t in range(per):
                shard = plane * per + (lax.rem(voc, per) ^ t)
                at = u_rows + t * wide
                rows = packs[k][:, at : at + wide].astype(jnp.float32).T
                v_wide[pl.ds(pl.multiple_of(shard * v_rows, 8), v_rows), :] = rows[:v_rows]
        v_out[...] = v_wide[...].T.astype(jnp.bfloat16)
        for k in range(n_voc):
            for s in range(2):
                want_out[k, :, s * r : (s + 1) * r] = (
                    sampled_ref[s : s + 1, k * r : (k + 1) * r] - voc * entries
                )

    return pl.pallas_call(
        kernel,
        out_shape=(
            jax.ShapeDtypeStruct((n_group * u_rows, rank), jnp.bfloat16),
            jax.ShapeDtypeStruct((rank, n_voc * v_rows), jnp.bfloat16),
            jax.ShapeDtypeStruct((n_voc, 1, 2 * r), jnp.int32),
        ),
        in_specs=[WHOLE] * (1 + n_group),
        out_specs=(WHOLE,) * 3,
        scratch_shapes=[pltpu.VMEM((n_voc * v_rows, rank), jnp.float32)],
        compiler_params=pltpu.CompilerParams(vmem_limit_bytes=4 * MIB),
        name="assemble",
    )


def sources_of(hop, n_voc):
    position = ring_position(lax.axis_index("vocab"), n_voc)
    return ring_device(position + hop, n_voc), ring_device(position - hop + 1, n_voc)


def load_rows(rows, pieces):
    at = 0
    for ref in pieces:
        block = ref[...].reshape(-1, ref.shape[-1])
        rows[:, at : at + block.shape[0]] = block.T
        at += block.shape[0]


def make_base(r, depth, entries, load):
    n = 4 * r
    tile = tile_rows(entries)
    tiles = entries // tile
    split = 2 if tile % 32 == 0 else 1
    part = tile // split

    def kernel(up_ref, down_ref, head_ref, base_ref, rows, *refs):
        held = head_ref
        if load:
            held, sems = refs

        def fetch(t):
            span = pl.ds(pl.multiple_of(t * part, part), part)
            return pltpu.make_async_copy(head_ref.at[span, :], held.at[span, :], sems.at[t])

        if load:
            for t in range(split * tiles):
                fetch(t).start(priority=t % 2)
        load_rows(rows, (up_ref, down_ref))

        @pl.loop(0, tiles)
        def _(i):
            if load:
                for k in range(split):
                    fetch(split * i + k).wait()
            span = pl.ds(pl.multiple_of(i * tile, tile), tile)
            base_ref[span, :] = jnp.dot(
                held[span, :], rows[...], preferred_element_type=jnp.float32
            )

    out_shape = [
        jax.ShapeDtypeStruct((entries, n), jnp.float32),
        jax.ShapeDtypeStruct((depth, n), jnp.bfloat16),
    ]
    if load:
        out_shape.append(jax.ShapeDtypeStruct((entries, depth), jnp.bfloat16))
    return pl.pallas_call(
        kernel,
        out_shape=tuple(out_shape),
        in_specs=[WHOLE, WHOLE, pl.BlockSpec(memory_space=pltpu.HBM) if load else WHOLE],
        out_specs=(WHOLE,) * len(out_shape),
        scratch_shapes=[pltpu.SemaphoreType.DMA((split * tiles,))] * load,
        compiler_params=pltpu.CompilerParams(vmem_limit_bytes=(23 if load else 8) * MIB),
        cost_estimate=pl.CostEstimate(
            flops=2 * n * entries * depth,
            bytes_accessed=2 * entries * depth,
            transcendentals=0,
        ),
        name="base",
    )


def make_chunk(hop, r, depth, entries, rank, n_voc):
    tile = tile_rows(entries)
    sizes = [tile] * (entries // tile - 1) + [tile // 2] * 2
    n = 4 * r
    carry, last = 2 * (hop == 3), hop == n_voc // 2
    earlier = hop - 1 if last else 0

    def kernel(*refs):
        piece, refs = refs[:2], refs[2:]
        head_ref, u_ref, v_ref, want_ref, *refs = refs
        bases, refs = refs[: 2 * carry], refs[2 * carry :]
        before, refs = refs[:earlier], refs[earlier:]
        (out_ref, *base_outs), refs = refs[: 1 + carry], refs[1 + carry :]
        rows, even, odd, *refs = refs
        (proj, *state), *base_scratch = [refs[4 * k : 4 * k + 4] for k in range(1 + carry)]

        def project(source, into):
            into[...] = jnp.dot(
                v_ref[...], source[...], preferred_element_type=jnp.float32
            ).astype(jnp.bfloat16)

        def clear(top, total, pick):
            top[...] = jnp.full(top.shape, -1e30, jnp.float32)
            total[...] = jnp.zeros(total.shape, jnp.float32)
            pick[...] = jnp.zeros(pick.shape, jnp.float32)

        def wanted(k):
            left, right = sources_of(k, n_voc)
            return jnp.concatenate([want_ref[left], want_ref[right]], axis=1)

        load_rows(rows, piece)
        project(rows, proj)
        clear(*state)
        want = wanted(hop)
        base_wants = []
        for k in range(carry):
            project(bases[2 * k + 1], base_scratch[k][0])
            clear(*base_scratch[k][1:])
            base_wants.append(wanted(k + 1))

        def multiply(start, size, into):
            span = slice(start, start + size)
            into[:size, :] = jnp.dot(
                head_ref[span, :], rows[...], preferred_element_type=jnp.float32
            ) + jnp.dot(u_ref[span, :], proj[...], preferred_element_type=jnp.float32)

        def reduce(x, want, top, total, pick):
            size = x.shape[0]
            entry = lax.broadcasted_iota(jnp.int32, (size, n), 0)
            hit = jnp.where(entry == want, x, 0.0)
            x3 = x.reshape(size // 8, 8, n)
            new = jnp.maximum(top[...], jnp.max(x3, axis=0))
            total[...] = total[...] * jnp.exp(top[...] - new) + jnp.sum(
                jnp.exp(x3 - new[None]), axis=0
            )
            pick[...] = pick[...] + jnp.sum(hit.reshape(size // 8, 8, n), axis=0)
            top[...] = new

        def finish_bases(start, size):
            span = slice(start, start + size)
            for k in range(carry):
                base_proj, *base_state = base_scratch[k]
                x = bases[2 * k][span, :] + jnp.dot(
                    u_ref[span, :], base_proj[...], preferred_element_type=jnp.float32
                )
                reduce(x, base_wants[k] - start, *base_state)

        start = 0
        for i, size in enumerate(sizes):
            multiply(start, size, (even, odd)[i % 2])
            if i:
                ahead = sizes[i - 1]
                reduce((even, odd)[(i - 1) % 2][:ahead, :], want - (start - ahead), *state)
            finish_bases(start, size)
            start += size
        reduce((even, odd)[(len(sizes) - 1) % 2][:size, :], want - (start - size), *state)

        def results(top, total, pick):
            best = jnp.max(top[...], axis=0, keepdims=True)
            sums = jnp.sum(total[...] * jnp.exp(top[...] - best), axis=0, keepdims=True)
            return best, sums, jnp.sum(pick[...], axis=0, keepdims=True)

        for k in range(carry):
            for q, value in enumerate(results(*base_scratch[k][1:])):
                base_outs[k][q : q + 1, :] = value
        for q, value in enumerate(results(*state)):
            if not last:
                out_ref[q : q + 1, :] = value
                continue
            for k, lanes in [(hop, value)] + [
                (k, before[k - 1][q : q + 1, :]) for k in range(1, hop)
            ]:
                left, right = sources_of(k, n_voc)
                out_ref[q, pl.ds(left, 1), :] = lanes[:, : 2 * r]
                out_ref[q, pl.ds(right, 1), :] = lanes[:, 2 * r :]

    out_shape = jax.ShapeDtypeStruct((3, n_voc, 2 * r) if last else (3, n), jnp.float32)
    small = [pltpu.VMEM((rank, n), jnp.bfloat16)] + [pltpu.VMEM((8, n), jnp.float32)] * 3
    return pl.pallas_call(
        kernel,
        out_shape=(out_shape,) * (1 + carry) if carry else out_shape,
        in_specs=[WHOLE] * (6 + 2 * carry + earlier),
        out_specs=(WHOLE,) * (1 + carry) if carry else WHOLE,
        scratch_shapes=[
            pltpu.VMEM((depth, n), jnp.bfloat16),
            pltpu.VMEM((tile, n), jnp.float32),
            pltpu.VMEM((tile, n), jnp.float32),
        ]
        + small * (1 + carry),
        compiler_params=pltpu.CompilerParams(vmem_limit_bytes=8 * MIB),
        cost_estimate=pl.CostEstimate(
            flops=2 * n * entries * (depth + 256),
            bytes_accessed=2 * entries * (depth + LANES),
            transcendentals=n * entries,
        ),
        name="chunk",
    )


def make_combine(bits, r, n_voc, finish):
    low = bits & -bits
    count = bits // low + 1

    def kernel(*refs):
        parts, outs, held = refs[:count], refs[count:-1], refs[-1]
        slot = lax.rem(lax.axis_index("vocab") // low, count)
        for k in range(count):
            held[slot ^ k] = parts[k][...]
        top = held[0, 0]
        for k in range(1, count):
            top = jnp.maximum(top, held[k, 0])
        total = held[0, 1] * jnp.exp(held[0, 0] - top)
        pick = held[0, 2]
        for k in range(1, count):
            total = total + held[k, 1] * jnp.exp(held[k, 0] - top)
            pick = pick + held[k, 2]
        if not finish:
            for q, value in enumerate((top, total, pick)):
                outs[0][q] = value
            return
        log_total = top + jnp.log(total)
        for ref, value in zip(outs, (pick - log_total, log_total)):
            for k in range(n_voc):
                for s in range(2):
                    ref[s : s + 1, k * r : (k + 1) * r] = value[k : k + 1, s * r : (s + 1) * r]

    if finish:
        shape = (jax.ShapeDtypeStruct((2, n_voc * r), jnp.float32),) * 2
        specs = (WHOLE, WHOLE)
    else:
        shape, specs = jax.ShapeDtypeStruct((3, n_voc, 2 * r), jnp.float32), WHOLE
    return pl.pallas_call(
        kernel,
        out_shape=shape,
        in_specs=[WHOLE] * count,
        out_specs=specs,
        scratch_shapes=[pltpu.VMEM((count, 3, n_voc, 2 * r), jnp.float32)],
        compiler_params=pltpu.CompilerParams(vmem_limit_bytes=MIB),
        name="combine",
    )


def body(hidden, head, factor_u, factor_v, sampled):
    n_group = lax.axis_size("group")
    n_voc = lax.axis_size("vocab")
    _, r, depth = hidden.shape
    entries = head.shape[0]
    rank = factor_u.shape[1]
    per = n_voc // n_group
    half = n_voc // 2

    order = ring_order(n_voc)
    ahead = [(order[i], order[(i + 1) % n_voc]) for i in range(n_voc)]
    behind = [(b, a) for a, b in ahead]

    def trade(x, axis, size, bit):
        return lax.ppermute(x, axis, [(i, i ^ bit) for i in range(size)])

    u_rows, v_rows = factor_u.shape[0], factor_v.shape[0]
    everyone = [(g, v) for g in range(n_group) for v in range(n_voc)]
    moves = [
        (v * n_group + swapped(g, n_group), g * n_voc + v) for g, v in everyone
    ]
    block = lax.ppermute(factor_u.T, ("group", "vocab"), moves)
    shards = []
    for t in range(per):
        moves = []
        for g, v in everyone:
            z = v // per
            plane = g ^ swapped(z, n_group)
            moves.append((z * n_voc + plane * per + (v % per ^ t), g * n_voc + v))
        shards.append(lax.ppermute(factor_v.T, ("group", "vocab"), moves))

    up = [hidden, lax.ppermute(hidden, "vocab", behind)]
    down = [hidden, lax.ppermute(hidden, "vocab", ahead)]
    up.append(lax.ppermute(up[1], "vocab", behind))
    base, base_rows, head = make_base(r, depth, entries, True)(up[1], hidden, head)
    base, block, *shards = lax.optimization_barrier((base, block, *shards))
    held = [base, base_rows]
    gap = ((0, 0), (0, padded(v_rows) - v_rows))
    pack = jnp.concatenate([block] + [jnp.pad(x, gap) for x in shards], axis=1)
    packs = {0: pack}
    near = [1 << k for k in reversed(range(n_group.bit_length() - 1))]
    for bit in near:
        packs[bit] = trade(pack, "group", n_group, bit)
    down[1], held[0] = lax.optimization_barrier((down[1], held[0]))
    up[2], held[0] = lax.optimization_barrier((up[2], held[0]))
    held += make_base(r, depth, entries, False)(up[2], down[1], head)
    held[2], *crossed = lax.optimization_barrier((held[2], *[packs[bit] for bit in near]))
    packs.update(zip(near, crossed))

    up.append(lax.ppermute(up[2], "vocab", behind))
    down.append(lax.ppermute(down[1], "vocab", ahead))
    for k in range(n_group):
        if k not in packs:
            packs[k] = trade(packs[k & (k - 1)], "group", n_group, k & -k)
    full_u, full_v, want = make_assemble(
        n_group, n_voc, u_rows, v_rows, rank, r, entries
    )(sampled, *[packs[k] for k in range(n_group)])
    down[2], full_u = lax.optimization_barrier((down[2], full_u))
    up[3], held[2], full_u = lax.optimization_barrier((up[3], held[2], full_u))

    stats = []
    for hop in range(3, half + 1):
        extra = held if hop == 3 else stats if hop == half else []
        chunk = make_chunk(hop, r, depth, entries, rank, n_voc)
        out = chunk(up[hop], down[hop - 1], head, full_u, full_v, want, *extra)
        stats += [out[1], out[2], out[0]] if hop == 3 else [out]
        if hop < half:
            up.append(lax.ppermute(up[-1], "vocab", behind))
            down.append(lax.ppermute(down[-1], "vocab", ahead))
            down[-1], stats[-1] = lax.optimization_barrier((down[-1], stats[-1]))
            up[-1], stats[-1] = lax.optimization_barrier((up[-1], stats[-1]))
    part = stats[-1]
    low = 1
    while low < n_voc:
        count = 2 if low == 1 else min(4, n_voc // low)
        bits = low * (count - 1)
        others = [trade(part, "vocab", n_voc, low * k) for k in range(1, count)]
        part = make_combine(bits, r, n_voc, low * count == n_voc)(part, *others)
        low *= count
    return part


def solution(mesh):
    in_specs = (
        P(None, ("group", "vocab"), None),
        P("vocab", None),
        P(("group", "vocab"), None),
        P("vocab", None),
        P(None, "group"),
    )
    out_specs = (P(None, "group"), P(None, "group"))
    return jax.shard_map(body, mesh=mesh, in_specs=in_specs, out_specs=out_specs, check_vma=False)
```

```python
import jax
import jax.numpy as jnp
from jax import lax
from jax.experimental import pallas as pl
from jax.experimental.pallas import tpu as pltpu
from jax.sharding import PartitionSpec as P

MIB = 1024 * 1024
LANES = 128
WHOLE = pl.BlockSpec(memory_space=pltpu.VMEM)


def ring_order(n):
    return [2 * i for i in range(n // 2)] + [2 * i + 1 for i in reversed(range(n // 2))]


def swapped(member, n_group):
    return member // 2 + member % 2 * (n_group // 2)


def ring_position(device, n):
    return jnp.where(device % 2 == 0, device // 2, n - 1 - device // 2)


def ring_device(position, n):
    position = lax.rem(position + n, n)
    return jnp.where(position < n // 2, 2 * position, 2 * (n - 1 - position) + 1)


def tile_rows(entries):
    for rows in (1024, 512, 256, 128, 64, 32, 16):
        if entries % (2 * rows) == 0:
            return rows
    raise ValueError(entries)


def padded(size):
    return -(-size // LANES) * LANES


def make_assemble(n_group, n_voc, u_rows, v_rows, rank, r, entries):
    per = n_voc // n_group
    wide = padded(v_rows)

    def kernel(sampled_ref, *refs):
        packs = refs[:n_group]
        u_out, v_out, want_out, v_wide = refs[n_group:]
        group = lax.axis_index("group")
        voc = lax.axis_index("vocab")
        for k in range(n_group):
            member = group ^ k
            plane = member ^ swapped(voc // per, n_group)
            block = swapped(member, n_group)
            start = pl.multiple_of(block * u_rows, u_rows)
            u_out[pl.ds(start, u_rows), :] = packs[k][:, :u_rows].T
            for t in range(per):
                shard = plane * per + (lax.rem(voc, per) ^ t)
                at = u_rows + t * wide
                rows = packs[k][:, at : at + wide].astype(jnp.float32).T
                v_wide[pl.ds(pl.multiple_of(shard * v_rows, 8), v_rows), :] = rows[:v_rows]
        v_out[...] = v_wide[...].T.astype(jnp.bfloat16)
        for k in range(n_voc):
            for s in range(2):
                want_out[k, :, s * r : (s + 1) * r] = (
                    sampled_ref[s : s + 1, k * r : (k + 1) * r] - voc * entries
                )

    return pl.pallas_call(
        kernel,
        out_shape=(
            jax.ShapeDtypeStruct((n_group * u_rows, rank), jnp.bfloat16),
            jax.ShapeDtypeStruct((rank, n_voc * v_rows), jnp.bfloat16),
            jax.ShapeDtypeStruct((n_voc, 1, 2 * r), jnp.int32),
        ),
        in_specs=[WHOLE] * (1 + n_group),
        out_specs=(WHOLE,) * 3,
        scratch_shapes=[pltpu.VMEM((n_voc * v_rows, rank), jnp.float32)],
        compiler_params=pltpu.CompilerParams(vmem_limit_bytes=4 * MIB),
        name="assemble",
    )


def sources_of(hop, n_voc):
    position = ring_position(lax.axis_index("vocab"), n_voc)
    return ring_device(position + hop, n_voc), ring_device(position - hop + 1, n_voc)


def load_rows(rows, pieces):
    at = 0
    for ref in pieces:
        block = ref[...].reshape(-1, ref.shape[-1])
        rows[:, at : at + block.shape[0]] = block.T
        at += block.shape[0]


def make_base(r, depth, entries, load):
    n = 4 * r
    tile = tile_rows(entries)
    tiles = entries // tile
    split = 2 if tile % 32 == 0 else 1
    part = tile // split

    def kernel(up_ref, down_ref, head_ref, base_ref, rows, *refs):
        held = head_ref
        if load:
            held, sems = refs

        def fetch(t):
            span = pl.ds(pl.multiple_of(t * part, part), part)
            return pltpu.make_async_copy(head_ref.at[span, :], held.at[span, :], sems.at[t])

        if load:
            for t in range(split * tiles):
                fetch(t).start(priority=t % 2)
        load_rows(rows, (up_ref, down_ref))

        @pl.loop(0, tiles)
        def _(i):
            if load:
                for k in range(split):
                    fetch(split * i + k).wait()
            span = pl.ds(pl.multiple_of(i * tile, tile), tile)
            base_ref[span, :] = jnp.dot(
                held[span, :], rows[...], preferred_element_type=jnp.float32
            )

    out_shape = [
        jax.ShapeDtypeStruct((entries, n), jnp.float32),
        jax.ShapeDtypeStruct((depth, n), jnp.bfloat16),
    ]
    if load:
        out_shape.append(jax.ShapeDtypeStruct((entries, depth), jnp.bfloat16))
    return pl.pallas_call(
        kernel,
        out_shape=tuple(out_shape),
        in_specs=[WHOLE, WHOLE, pl.BlockSpec(memory_space=pltpu.HBM) if load else WHOLE],
        out_specs=(WHOLE,) * len(out_shape),
        scratch_shapes=[pltpu.SemaphoreType.DMA((split * tiles,))] * load,
        compiler_params=pltpu.CompilerParams(vmem_limit_bytes=(23 if load else 8) * MIB),
        cost_estimate=pl.CostEstimate(
            flops=2 * n * entries * depth,
            bytes_accessed=2 * entries * depth,
            transcendentals=0,
        ),
        name="base",
    )


def clear(top, total, pick):
    top[...] = jnp.full(top.shape, -1e30, jnp.float32)
    total[...] = jnp.zeros(total.shape, jnp.float32)
    pick[...] = jnp.zeros(pick.shape, jnp.float32)


def project(v_ref, source, into):
    into[...] = jnp.dot(v_ref[...], source[...], preferred_element_type=jnp.float32).astype(
        jnp.bfloat16
    )


def wanted(want_ref, hop, n_voc):
    left, right = sources_of(hop, n_voc)
    return jnp.concatenate([want_ref[left], want_ref[right]], axis=1)


def reduce(x, want, top, total, pick):
    size, n = x.shape
    entry = lax.broadcasted_iota(jnp.int32, (size, n), 0)
    hit = jnp.where(entry == want, x, 0.0)
    x3 = x.reshape(size // 8, 8, n)
    new = jnp.maximum(top[...], jnp.max(x3, axis=0))
    total[...] = total[...] * jnp.exp(top[...] - new) + jnp.sum(jnp.exp(x3 - new[None]), axis=0)
    pick[...] = pick[...] + jnp.sum(hit.reshape(size // 8, 8, n), axis=0)
    top[...] = new


def results(top, total, pick):
    best = jnp.max(top[...], axis=0, keepdims=True)
    sums = jnp.sum(total[...] * jnp.exp(top[...] - best), axis=0, keepdims=True)
    return best, sums, jnp.sum(pick[...], axis=0, keepdims=True)


def state_scratch(rank, n):
    return [pltpu.VMEM((rank, n), jnp.bfloat16)] + [pltpu.VMEM((8, n), jnp.float32)] * 3


def make_ends(r, depth, entries, rank, n_voc):
    tile = tile_rows(entries)
    n = 4 * r

    def kernel(base_a, rows_a, base_b, rows_b, u_ref, v_ref, want_ref, out_a, out_b, *scratch):
        bases = [
            (base_a, wanted(want_ref, 1, n_voc), scratch[:4]),
            (base_b, wanted(want_ref, 2, n_voc), scratch[4:]),
        ]
        for rows, (_, _, (proj, *state)) in zip((rows_a, rows_b), bases):
            project(v_ref, rows, proj)
            clear(*state)

        @pl.loop(0, entries // tile)
        def _(i):
            span = pl.ds(pl.multiple_of(i * tile, tile), tile)
            for base, want, (proj, *state) in bases:
                x = base[span, :] + jnp.dot(
                    u_ref[span, :], proj[...], preferred_element_type=jnp.float32
                )
                reduce(x, want - i * tile, *state)

        for out, (_, _, (proj, *state)) in zip((out_a, out_b), bases):
            for q, value in enumerate(results(*state)):
                out[q : q + 1, :] = value

    return pl.pallas_call(
        kernel,
        out_shape=(jax.ShapeDtypeStruct((3, n), jnp.float32),) * 2,
        in_specs=[WHOLE] * 7,
        out_specs=(WHOLE,) * 2,
        scratch_shapes=state_scratch(rank, n) * 2,
        compiler_params=pltpu.CompilerParams(vmem_limit_bytes=8 * MIB),
        cost_estimate=pl.CostEstimate(
            flops=4 * n * entries * 256,
            bytes_accessed=8 * entries * n,
            transcendentals=2 * n * entries,
        ),
        name="ends",
    )


def make_chunk(hop, pieces, r, depth, entries, rank, n_voc):
    tile = tile_rows(entries)
    sizes = [tile] * (entries // tile - 1) + [tile // 2] * 2
    n = 4 * r
    last = hop == n_voc // 2
    earlier = hop - 1 if last else 0

    def kernel(*refs):
        piece, refs = refs[:pieces], refs[pieces:]
        head_ref, u_ref, v_ref, want_ref, *refs = refs
        before, refs = refs[:earlier], refs[earlier:]
        out_ref, rows, even, odd, proj, *state = refs

        load_rows(rows, piece)
        project(v_ref, rows, proj)
        clear(*state)
        want = wanted(want_ref, hop, n_voc)

        def multiply(start, size, into):
            span = slice(start, start + size)
            into[:size, :] = jnp.dot(
                head_ref[span, :], rows[...], preferred_element_type=jnp.float32
            ) + jnp.dot(u_ref[span, :], proj[...], preferred_element_type=jnp.float32)

        start = 0
        for i, size in enumerate(sizes):
            multiply(start, size, (even, odd)[i % 2])
            if i:
                ahead = sizes[i - 1]
                reduce((even, odd)[(i - 1) % 2][:ahead, :], want - (start - ahead), *state)
            start += size
        reduce((even, odd)[(len(sizes) - 1) % 2][:size, :], want - (start - size), *state)

        for q, value in enumerate(results(*state)):
            if not last:
                out_ref[q : q + 1, :] = value
                continue
            for k, lanes in [(hop, value)] + [
                (k, before[k - 1][q : q + 1, :]) for k in range(1, hop)
            ]:
                left, right = sources_of(k, n_voc)
                out_ref[q, pl.ds(left, 1), :] = lanes[:, : 2 * r]
                out_ref[q, pl.ds(right, 1), :] = lanes[:, 2 * r :]

    return pl.pallas_call(
        kernel,
        out_shape=jax.ShapeDtypeStruct((3, n_voc, 2 * r) if last else (3, n), jnp.float32),
        in_specs=[WHOLE] * (pieces + 4 + earlier),
        out_specs=WHOLE,
        scratch_shapes=[
            pltpu.VMEM((depth, n), jnp.bfloat16),
            pltpu.VMEM((tile, n), jnp.float32),
            pltpu.VMEM((tile, n), jnp.float32),
        ]
        + state_scratch(rank, n),
        compiler_params=pltpu.CompilerParams(vmem_limit_bytes=8 * MIB),
        cost_estimate=pl.CostEstimate(
            flops=2 * n * entries * (depth + 256),
            bytes_accessed=2 * entries * (depth + LANES),
            transcendentals=n * entries,
        ),
        name="chunk",
    )


def make_combine(bits, r, n_voc, finish):
    low = bits & -bits
    count = bits // low + 1

    def kernel(*refs):
        parts, outs, held = refs[:count], refs[count:-1], refs[-1]
        slot = lax.rem(lax.axis_index("vocab") // low, count)
        for k in range(count):
            held[slot ^ k] = parts[k][...]
        top = held[0, 0]
        for k in range(1, count):
            top = jnp.maximum(top, held[k, 0])
        total = held[0, 1] * jnp.exp(held[0, 0] - top)
        pick = held[0, 2]
        for k in range(1, count):
            total = total + held[k, 1] * jnp.exp(held[k, 0] - top)
            pick = pick + held[k, 2]
        if not finish:
            for q, value in enumerate((top, total, pick)):
                outs[0][q] = value
            return
        log_total = top + jnp.log(total)
        for ref, value in zip(outs, (pick - log_total, log_total)):
            for k in range(n_voc):
                for s in range(2):
                    ref[s : s + 1, k * r : (k + 1) * r] = value[k : k + 1, s * r : (s + 1) * r]

    if finish:
        shape = (jax.ShapeDtypeStruct((2, n_voc * r), jnp.float32),) * 2
        specs = (WHOLE, WHOLE)
    else:
        shape, specs = jax.ShapeDtypeStruct((3, n_voc, 2 * r), jnp.float32), WHOLE
    return pl.pallas_call(
        kernel,
        out_shape=shape,
        in_specs=[WHOLE] * count,
        out_specs=specs,
        scratch_shapes=[pltpu.VMEM((count, 3, n_voc, 2 * r), jnp.float32)],
        compiler_params=pltpu.CompilerParams(vmem_limit_bytes=MIB),
        name="combine",
    )


def body(hidden, head, factor_u, factor_v, sampled):
    n_group = lax.axis_size("group")
    n_voc = lax.axis_size("vocab")
    _, r, depth = hidden.shape
    entries = head.shape[0]
    rank = factor_u.shape[1]
    per = n_voc // n_group
    half = n_voc // 2

    order = ring_order(n_voc)
    ahead = [(order[i], order[(i + 1) % n_voc]) for i in range(n_voc)]
    behind = [(b, a) for a, b in ahead]

    def trade(x, axis, size, bit):
        return lax.ppermute(x, axis, [(i, i ^ bit) for i in range(size)])

    u_rows, v_rows = factor_u.shape[0], factor_v.shape[0]
    everyone = [(g, v) for g in range(n_group) for v in range(n_voc)]
    moves = [
        (v * n_group + swapped(g, n_group), g * n_voc + v) for g, v in everyone
    ]
    block = lax.ppermute(factor_u.T, ("group", "vocab"), moves)
    shards = []
    for t in range(per):
        moves = []
        for g, v in everyone:
            z = v // per
            plane = g ^ swapped(z, n_group)
            moves.append((z * n_voc + plane * per + (v % per ^ t), g * n_voc + v))
        shards.append(lax.ppermute(factor_v.T, ("group", "vocab"), moves))

    up = [hidden, lax.ppermute(hidden, "vocab", behind)]
    down = [hidden, lax.ppermute(hidden, "vocab", ahead)]
    up.append(lax.ppermute(up[1], "vocab", behind))
    down.append(lax.ppermute(down[1], "vocab", ahead))
    base, base_rows, head = make_base(r, depth, entries, True)(up[1], hidden, head)
    base, block, *shards = lax.optimization_barrier((base, block, *shards))
    held = [base, base_rows]
    gap = ((0, 0), (0, padded(v_rows) - v_rows))
    pack = jnp.concatenate([block] + [jnp.pad(x, gap) for x in shards], axis=1)
    packs = {0: pack}
    near = [1 << k for k in reversed(range(n_group.bit_length() - 1))]
    for bit in near:
        packs[bit] = trade(pack, "group", n_group, bit)
    down[2], held[0] = lax.optimization_barrier((down[2], held[0]))
    up[2], held[0] = lax.optimization_barrier((up[2], held[0]))
    held += make_base(r, depth, entries, False)(up[2], down[1], head)
    held[2], *crossed = lax.optimization_barrier((held[2], *[packs[bit] for bit in near]))
    packs.update(zip(near, crossed))

    up.append(lax.ppermute(up[2], "vocab", behind))
    down.append(lax.ppermute(down[2], "vocab", ahead))
    for k in range(n_group):
        if k not in packs:
            packs[k] = trade(packs[k & (k - 1)], "group", n_group, k & -k)
    full_u, full_v, want = make_assemble(
        n_group, n_voc, u_rows, v_rows, rank, r, entries
    )(sampled, *[packs[k] for k in range(n_group)])
    stats = list(make_ends(r, depth, entries, rank, n_voc)(*held, full_u, full_v, want))
    down[3], stats[0] = lax.optimization_barrier((down[3], stats[0]))
    up[3], stats[0] = lax.optimization_barrier((up[3], stats[0]))

    for hop in range(3, half):
        if hop + 1 < half:
            up.append(lax.ppermute(up[hop], "vocab", behind))
            down.append(lax.ppermute(down[hop], "vocab", ahead))
        else:
            opposite = [
                lax.ppermute(up[hop][0], "vocab", behind),
                lax.ppermute(down[hop][1], "vocab", ahead),
            ]
        chunk = make_chunk(hop, 2, r, depth, entries, rank, n_voc)
        stats.append(chunk(up[hop], down[hop - 1], head, full_u, full_v, want))
        if hop + 1 < half:
            down[-1], stats[-1] = lax.optimization_barrier((down[-1], stats[-1]))
            up[-1], stats[-1] = lax.optimization_barrier((up[-1], stats[-1]))
    chunk = make_chunk(half, 3, r, depth, entries, rank, n_voc)
    stats.append(chunk(*opposite, down[half - 1], head, full_u, full_v, want, *stats))
    part = stats[-1]
    low = 1
    while low < n_voc:
        count = 2 if low == 1 else min(4, n_voc // low)
        bits = low * (count - 1)
        others = [trade(part, "vocab", n_voc, low * k) for k in range(1, count)]
        part = make_combine(bits, r, n_voc, low * count == n_voc)(part, *others)
        low *= count
    return part


def solution(mesh):
    in_specs = (
        P(None, ("group", "vocab"), None),
        P("vocab", None),
        P(("group", "vocab"), None),
        P("vocab", None),
        P(None, "group"),
    )
    out_specs = (P(None, "group"), P(None, "group"))
    return jax.shard_map(body, mesh=mesh, in_specs=in_specs, out_specs=out_specs, check_vma=False)
```

```python
import jax
import jax.numpy as jnp
from jax import lax
from jax.experimental import pallas as pl
from jax.experimental.pallas import tpu as pltpu
from jax.sharding import PartitionSpec as P

MIB = 1024 * 1024
LANES = 128
WHOLE = pl.BlockSpec(memory_space=pltpu.VMEM)


def ring_order(n):
    return [2 * i for i in range(n // 2)] + [2 * i + 1 for i in reversed(range(n // 2))]


def swapped(member, n_group):
    return member // 2 + member % 2 * (n_group // 2)


def ring_position(device, n):
    return jnp.where(device % 2 == 0, device // 2, n - 1 - device // 2)


def ring_device(position, n):
    position = lax.rem(position + n, n)
    return jnp.where(position < n // 2, 2 * position, 2 * (n - 1 - position) + 1)


def tile_rows(entries):
    for rows in (1024, 512, 256, 128, 64, 32, 16):
        if entries % (2 * rows) == 0:
            return rows
    raise ValueError(entries)


def padded(size):
    return -(-size // LANES) * LANES


def make_assemble(n_group, n_voc, u_rows, v_rows, rank, r, entries):
    per = n_voc // n_group
    wide = padded(v_rows)

    def kernel(sampled_ref, *refs):
        packs = refs[:n_group]
        u_out, v_out, want_out, v_wide = refs[n_group:]
        group = lax.axis_index("group")
        voc = lax.axis_index("vocab")
        for k in range(n_group):
            member = group ^ k
            plane = member ^ swapped(voc // per, n_group)
            block = swapped(member, n_group)
            start = pl.multiple_of(block * u_rows, u_rows)
            u_out[pl.ds(start, u_rows), :] = packs[k][:, :u_rows].T
            for t in range(per):
                shard = plane * per + (lax.rem(voc, per) ^ t)
                at = u_rows + t * wide
                rows = packs[k][:, at : at + wide].astype(jnp.float32).T
                v_wide[pl.ds(pl.multiple_of(shard * v_rows, 8), v_rows), :] = rows[:v_rows]
        v_out[...] = v_wide[...].T.astype(jnp.bfloat16)
        for k in range(n_voc):
            for s in range(2):
                want_out[k, :, s * r : (s + 1) * r] = (
                    sampled_ref[s : s + 1, k * r : (k + 1) * r] - voc * entries
                )

    return pl.pallas_call(
        kernel,
        out_shape=(
            jax.ShapeDtypeStruct((n_group * u_rows, rank), jnp.bfloat16),
            jax.ShapeDtypeStruct((rank, n_voc * v_rows), jnp.bfloat16),
            jax.ShapeDtypeStruct((n_voc, 1, 2 * r), jnp.int32),
        ),
        in_specs=[WHOLE] * (1 + n_group),
        out_specs=(WHOLE,) * 3,
        scratch_shapes=[pltpu.VMEM((n_voc * v_rows, rank), jnp.float32)],
        compiler_params=pltpu.CompilerParams(vmem_limit_bytes=4 * MIB),
        name="assemble",
    )


def sources_of(hop, n_voc):
    position = ring_position(lax.axis_index("vocab"), n_voc)
    return ring_device(position + hop, n_voc), ring_device(position - hop + 1, n_voc)


def load_rows(rows, pieces):
    blocks = [ref[...].reshape(-1, ref.shape[-1]) for ref in pieces]
    rows[...] = jnp.concatenate(blocks, axis=0).T


def make_base(r, depth, entries, load):
    n = 4 * r
    tile = tile_rows(entries)
    tiles = entries // tile
    split = 2 if tile % 32 == 0 else 1
    part = tile // split

    def kernel(up_ref, down_ref, head_ref, base_ref, rows, *refs):
        held = head_ref
        if load:
            held, sems = refs

        def fetch(t):
            span = pl.ds(pl.multiple_of(t * part, part), part)
            return pltpu.make_async_copy(head_ref.at[span, :], held.at[span, :], sems.at[t])

        if load:
            for t in range(split * tiles):
                fetch(t).start(priority=t % 2)
        load_rows(rows, (up_ref, down_ref))

        @pl.loop(0, tiles)
        def _(i):
            if load:
                for k in range(split):
                    fetch(split * i + k).wait()
            span = pl.ds(pl.multiple_of(i * tile, tile), tile)
            base_ref[span, :] = jnp.dot(
                held[span, :], rows[...], preferred_element_type=jnp.float32
            )

    out_shape = [
        jax.ShapeDtypeStruct((entries, n), jnp.float32),
        jax.ShapeDtypeStruct((depth, n), jnp.bfloat16),
    ]
    if load:
        out_shape.append(jax.ShapeDtypeStruct((entries, depth), jnp.bfloat16))
    return pl.pallas_call(
        kernel,
        out_shape=tuple(out_shape),
        in_specs=[WHOLE, WHOLE, pl.BlockSpec(memory_space=pltpu.HBM) if load else WHOLE],
        out_specs=(WHOLE,) * len(out_shape),
        scratch_shapes=[pltpu.SemaphoreType.DMA((split * tiles,))] * load,
        compiler_params=pltpu.CompilerParams(vmem_limit_bytes=(23 if load else 8) * MIB),
        cost_estimate=pl.CostEstimate(
            flops=2 * n * entries * depth,
            bytes_accessed=2 * entries * depth,
            transcendentals=0,
        ),
        name="base",
    )


def clear(top, total, pick):
    top[...] = jnp.full(top.shape, -1e30, jnp.float32)
    total[...] = jnp.zeros(total.shape, jnp.float32)
    pick[...] = jnp.zeros(pick.shape, jnp.float32)


def project(v_ref, source, into):
    into[...] = jnp.dot(v_ref[...], source[...], preferred_element_type=jnp.float32).astype(
        jnp.bfloat16
    )


def wanted(want_ref, hop, n_voc):
    left, right = sources_of(hop, n_voc)
    return jnp.concatenate([want_ref[left], want_ref[right]], axis=1)


def reduce(x, want, top, total, pick):
    size, n = x.shape
    entry = lax.broadcasted_iota(jnp.int32, (size, n), 0)
    hit = jnp.where(entry == want, x, 0.0)
    x3 = x.reshape(size // 8, 8, n)
    new = jnp.maximum(top[...], jnp.max(x3, axis=0))
    total[...] = total[...] * jnp.exp(top[...] - new) + jnp.sum(jnp.exp(x3 - new[None]), axis=0)
    pick[...] = pick[...] + jnp.sum(hit.reshape(size // 8, 8, n), axis=0)
    top[...] = new


def results(top, total, pick):
    best = jnp.max(top[...], axis=0, keepdims=True)
    sums = jnp.sum(total[...] * jnp.exp(top[...] - best), axis=0, keepdims=True)
    return best, sums, jnp.sum(pick[...], axis=0, keepdims=True)


def state_scratch(rank, n):
    return [pltpu.VMEM((rank, n), jnp.bfloat16)] + [pltpu.VMEM((8, n), jnp.float32)] * 3


def make_ends(r, depth, entries, rank, n_voc):
    tile = tile_rows(entries)
    n = 4 * r

    def kernel(base_a, rows_a, base_b, rows_b, u_ref, v_ref, want_ref, out_a, out_b, *scratch):
        bases = [
            (base_a, wanted(want_ref, 1, n_voc), scratch[:4]),
            (base_b, wanted(want_ref, 2, n_voc), scratch[4:]),
        ]
        for rows, (_, _, (proj, *state)) in zip((rows_a, rows_b), bases):
            project(v_ref, rows, proj)
            clear(*state)

        @pl.loop(0, entries // tile)
        def _(i):
            span = pl.ds(pl.multiple_of(i * tile, tile), tile)
            for base, want, (proj, *state) in bases:
                x = base[span, :] + jnp.dot(
                    u_ref[span, :], proj[...], preferred_element_type=jnp.float32
                )
                reduce(x, want - i * tile, *state)

        for out, (_, _, (proj, *state)) in zip((out_a, out_b), bases):
            for q, value in enumerate(results(*state)):
                out[q : q + 1, :] = value

    return pl.pallas_call(
        kernel,
        out_shape=(jax.ShapeDtypeStruct((3, n), jnp.float32),) * 2,
        in_specs=[WHOLE] * 7,
        out_specs=(WHOLE,) * 2,
        scratch_shapes=state_scratch(rank, n) * 2,
        compiler_params=pltpu.CompilerParams(vmem_limit_bytes=8 * MIB),
        cost_estimate=pl.CostEstimate(
            flops=4 * n * entries * 256,
            bytes_accessed=8 * entries * n,
            transcendentals=2 * n * entries,
        ),
        name="ends",
    )


def make_chunk(hop, pieces, r, depth, entries, rank, n_voc):
    tile = tile_rows(entries)
    sizes = [tile] * (entries // tile - 1) + [tile // 2] * 2
    n = 4 * r
    last = hop == n_voc // 2
    earlier = hop - 1 if last else 0

    def kernel(*refs):
        piece, refs = refs[:pieces], refs[pieces:]
        head_ref, u_ref, v_ref, want_ref, *refs = refs
        before, refs = refs[:earlier], refs[earlier:]
        out_ref, rows, even, odd, proj, *state = refs

        load_rows(rows, piece)
        project(v_ref, rows, proj)
        clear(*state)
        want = wanted(want_ref, hop, n_voc)

        def multiply(start, size, into):
            span = slice(start, start + size)
            into[:size, :] = jnp.dot(
                head_ref[span, :], rows[...], preferred_element_type=jnp.float32
            ) + jnp.dot(u_ref[span, :], proj[...], preferred_element_type=jnp.float32)

        start = 0
        for i, size in enumerate(sizes):
            multiply(start, size, (even, odd)[i % 2])
            if i:
                ahead = sizes[i - 1]
                reduce((even, odd)[(i - 1) % 2][:ahead, :], want - (start - ahead), *state)
            start += size
        reduce((even, odd)[(len(sizes) - 1) % 2][:size, :], want - (start - size), *state)

        for q, value in enumerate(results(*state)):
            if not last:
                out_ref[q : q + 1, :] = value
                continue
            for k, lanes in [(hop, value)] + [
                (k, before[k - 1][q : q + 1, :]) for k in range(1, hop)
            ]:
                left, right = sources_of(k, n_voc)
                out_ref[q, pl.ds(left, 1), :] = lanes[:, : 2 * r]
                out_ref[q, pl.ds(right, 1), :] = lanes[:, 2 * r :]

    return pl.pallas_call(
        kernel,
        out_shape=jax.ShapeDtypeStruct((3, n_voc, 2 * r) if last else (3, n), jnp.float32),
        in_specs=[WHOLE] * (pieces + 4 + earlier),
        out_specs=WHOLE,
        scratch_shapes=[
            pltpu.VMEM((depth, n), jnp.bfloat16),
            pltpu.VMEM((tile, n), jnp.float32),
            pltpu.VMEM((tile, n), jnp.float32),
        ]
        + state_scratch(rank, n),
        compiler_params=pltpu.CompilerParams(vmem_limit_bytes=8 * MIB),
        cost_estimate=pl.CostEstimate(
            flops=2 * n * entries * (depth + 256),
            bytes_accessed=2 * entries * (depth + LANES),
            transcendentals=n * entries,
        ),
        name="chunk",
    )


def make_combine(bits, r, n_voc, finish):
    low = bits & -bits
    count = bits // low + 1

    def kernel(*refs):
        parts, outs, held = refs[:count], refs[count:-1], refs[-1]
        slot = lax.rem(lax.axis_index("vocab") // low, count)
        for k in range(count):
            held[slot ^ k] = parts[k][...]
        top = held[0, 0]
        for k in range(1, count):
            top = jnp.maximum(top, held[k, 0])
        total = held[0, 1] * jnp.exp(held[0, 0] - top)
        pick = held[0, 2]
        for k in range(1, count):
            total = total + held[k, 1] * jnp.exp(held[k, 0] - top)
            pick = pick + held[k, 2]
        if not finish:
            for q, value in enumerate((top, total, pick)):
                outs[0][q] = value
            return
        log_total = top + jnp.log(total)
        for ref, value in zip(outs, (pick - log_total, log_total)):
            for k in range(n_voc):
                for s in range(2):
                    ref[s : s + 1, k * r : (k + 1) * r] = value[k : k + 1, s * r : (s + 1) * r]

    if finish:
        shape = (jax.ShapeDtypeStruct((2, n_voc * r), jnp.float32),) * 2
        specs = (WHOLE, WHOLE)
    else:
        shape, specs = jax.ShapeDtypeStruct((3, n_voc, 2 * r), jnp.float32), WHOLE
    return pl.pallas_call(
        kernel,
        out_shape=shape,
        in_specs=[WHOLE] * count,
        out_specs=specs,
        scratch_shapes=[pltpu.VMEM((count, 3, n_voc, 2 * r), jnp.float32)],
        compiler_params=pltpu.CompilerParams(vmem_limit_bytes=MIB),
        name="combine",
    )


def body(hidden, head, factor_u, factor_v, sampled):
    n_group = lax.axis_size("group")
    n_voc = lax.axis_size("vocab")
    _, r, depth = hidden.shape
    entries = head.shape[0]
    rank = factor_u.shape[1]
    per = n_voc // n_group
    half = n_voc // 2

    order = ring_order(n_voc)
    ahead = [(order[i], order[(i + 1) % n_voc]) for i in range(n_voc)]
    behind = [(b, a) for a, b in ahead]

    def trade(x, axis, size, bit):
        return lax.ppermute(x, axis, [(i, i ^ bit) for i in range(size)])

    u_rows, v_rows = factor_u.shape[0], factor_v.shape[0]
    everyone = [(g, v) for g in range(n_group) for v in range(n_voc)]
    moves = [
        (v * n_group + swapped(g, n_group), g * n_voc + v) for g, v in everyone
    ]
    block = lax.ppermute(factor_u.T, ("group", "vocab"), moves)
    shards = []
    for t in range(per):
        moves = []
        for g, v in everyone:
            z = v // per
            plane = g ^ swapped(z, n_group)
            moves.append((z * n_voc + plane * per + (v % per ^ t), g * n_voc + v))
        shards.append(lax.ppermute(factor_v.T, ("group", "vocab"), moves))

    up = [hidden, lax.ppermute(hidden, "vocab", behind)]
    down = [hidden, lax.ppermute(hidden, "vocab", ahead)]
    up.append(lax.ppermute(up[1], "vocab", behind))
    down.append(lax.ppermute(down[1], "vocab", ahead))
    base, base_rows, head = make_base(r, depth, entries, True)(up[1], hidden, head)
    base, block, *shards = lax.optimization_barrier((base, block, *shards))
    held = [base, base_rows]
    gap = ((0, 0), (0, padded(v_rows) - v_rows))
    pack = jnp.concatenate([block] + [jnp.pad(x, gap) for x in shards], axis=1)
    packs = {0: pack}
    near = [1 << k for k in reversed(range(n_group.bit_length() - 1))]
    for bit in near:
        packs[bit] = trade(pack, "group", n_group, bit)
    down[2], held[0] = lax.optimization_barrier((down[2], held[0]))
    up[2], held[0] = lax.optimization_barrier((up[2], held[0]))
    held += make_base(r, depth, entries, False)(up[2], down[1], head)
    held[2], *crossed = lax.optimization_barrier((held[2], *[packs[bit] for bit in near]))
    packs.update(zip(near, crossed))

    up.append(lax.ppermute(up[2], "vocab", behind))
    down.append(lax.ppermute(down[2], "vocab", ahead))
    for k in range(n_group):
        if k not in packs:
            packs[k] = trade(packs[k & (k - 1)], "group", n_group, k & -k)
    full_u, full_v, want = make_assemble(
        n_group, n_voc, u_rows, v_rows, rank, r, entries
    )(sampled, *[packs[k] for k in range(n_group)])
    stats = list(make_ends(r, depth, entries, rank, n_voc)(*held, full_u, full_v, want))
    down[3], stats[0] = lax.optimization_barrier((down[3], stats[0]))
    up[3], stats[0] = lax.optimization_barrier((up[3], stats[0]))

    for hop in range(3, half):
        if hop + 1 < half:
            up.append(lax.ppermute(up[hop], "vocab", behind))
            down.append(lax.ppermute(down[hop], "vocab", ahead))
        else:
            opposite = [
                lax.ppermute(up[hop][0], "vocab", behind),
                lax.ppermute(down[hop][1], "vocab", ahead),
            ]
        chunk = make_chunk(hop, 2, r, depth, entries, rank, n_voc)
        stats.append(chunk(up[hop], down[hop - 1], head, full_u, full_v, want))
        if hop + 1 < half:
            down[-1], stats[-1] = lax.optimization_barrier((down[-1], stats[-1]))
            up[-1], stats[-1] = lax.optimization_barrier((up[-1], stats[-1]))
    chunk = make_chunk(half, 3, r, depth, entries, rank, n_voc)
    stats.append(chunk(*opposite, down[half - 1], head, full_u, full_v, want, *stats))
    part = stats[-1]
    low = 1
    while low < n_voc:
        count = 2 if low == 1 else min(4, n_voc // low)
        bits = low * (count - 1)
        others = [trade(part, "vocab", n_voc, low * k) for k in range(1, count)]
        part = make_combine(bits, r, n_voc, low * count == n_voc)(part, *others)
        low *= count
    return part


def solution(mesh):
    in_specs = (
        P(None, ("group", "vocab"), None),
        P("vocab", None),
        P(("group", "vocab"), None),
        P("vocab", None),
        P(None, "group"),
    )
    out_specs = (P(None, "group"), P(None, "group"))
    return jax.shard_map(body, mesh=mesh, in_specs=in_specs, out_specs=out_specs, check_vma=False)
```

```python
import jax
import jax.numpy as jnp
from jax import lax
from jax.experimental import pallas as pl
from jax.experimental.pallas import tpu as pltpu
from jax.sharding import PartitionSpec as P

MIB = 1024 * 1024
LANES = 128
WHOLE = pl.BlockSpec(memory_space=pltpu.VMEM)


def ring_order(n):
    return [2 * i for i in range(n // 2)] + [2 * i + 1 for i in reversed(range(n // 2))]


def swapped(member, n_group):
    return member // 2 + member % 2 * (n_group // 2)


def ring_position(device, n):
    return jnp.where(device % 2 == 0, device // 2, n - 1 - device // 2)


def ring_device(position, n):
    position = lax.rem(position + n, n)
    return jnp.where(position < n // 2, 2 * position, 2 * (n - 1 - position) + 1)


def tile_rows(entries):
    for rows in (1024, 512, 256, 128, 64, 32, 16):
        if entries % (2 * rows) == 0:
            return rows
    raise ValueError(entries)


def padded(size):
    return -(-size // LANES) * LANES


def make_assemble(n_group, n_voc, u_rows, v_rows, rank, r, entries):
    per = n_voc // n_group
    wide = padded(v_rows)

    def kernel(sampled_ref, *refs):
        packs = refs[:n_group]
        u_out, v_out, want_out, v_wide = refs[n_group:]
        group = lax.axis_index("group")
        voc = lax.axis_index("vocab")
        for k in range(n_group):
            member = group ^ k
            plane = member ^ swapped(voc // per, n_group)
            block = swapped(member, n_group)
            start = pl.multiple_of(block * u_rows, u_rows)
            u_out[pl.ds(start, u_rows), :] = packs[k][:, :u_rows].T
            for t in range(per):
                shard = plane * per + (lax.rem(voc, per) ^ t)
                at = u_rows + t * wide
                rows = packs[k][:, at : at + wide].astype(jnp.float32).T
                v_wide[pl.ds(pl.multiple_of(shard * v_rows, 8), v_rows), :] = rows[:v_rows]
        v_out[...] = v_wide[...].T.astype(jnp.bfloat16)
        for k in range(n_voc):
            for s in range(2):
                want_out[k, :, s * r : (s + 1) * r] = (
                    sampled_ref[s : s + 1, k * r : (k + 1) * r] - voc * entries
                )

    return pl.pallas_call(
        kernel,
        out_shape=(
            jax.ShapeDtypeStruct((n_group * u_rows, rank), jnp.bfloat16),
            jax.ShapeDtypeStruct((rank, n_voc * v_rows), jnp.bfloat16),
            jax.ShapeDtypeStruct((n_voc, 1, 2 * r), jnp.int32),
        ),
        in_specs=[WHOLE] * (1 + n_group),
        out_specs=(WHOLE,) * 3,
        scratch_shapes=[pltpu.VMEM((n_voc * v_rows, rank), jnp.float32)],
        compiler_params=pltpu.CompilerParams(vmem_limit_bytes=4 * MIB),
        name="assemble",
    )


def sources_of(hop, n_voc):
    voc = lax.axis_index("vocab")
    if n_voc == 8:
        steps = {1: (0, -2, 0, 0), 2: (2, 0, 0, 1), 3: (-2, 4, 1, 0), 4: (4, 2, 1, 1)}[hop]
        return tuple(lax.rem(voc + steps[k] + n_voc, n_voc) ^ steps[2 + k] for k in range(2))
    position = ring_position(voc, n_voc)
    return ring_device(position + hop, n_voc), ring_device(position - hop + 1, n_voc)


def load_rows(rows, pieces):
    blocks = [ref[...].reshape(-1, ref.shape[-1]) for ref in pieces]
    rows[...] = jnp.concatenate(blocks, axis=0).T


def make_base(r, depth, entries, load):
    n = 4 * r
    tile = tile_rows(entries)
    tiles = entries // tile
    split = 2 if tile % 32 == 0 else 1
    part = tile // split

    def kernel(up_ref, down_ref, head_ref, base_ref, rows, *refs):
        held = head_ref
        if load:
            held, sems = refs

        def fetch(t):
            span = pl.ds(pl.multiple_of(t * part, part), part)
            return pltpu.make_async_copy(head_ref.at[span, :], held.at[span, :], sems.at[t])

        if load:
            for t in range(split * tiles):
                fetch(t).start(priority=t % 2)
        load_rows(rows, (up_ref, down_ref))

        @pl.loop(0, tiles)
        def _(i):
            if load:
                for k in range(split):
                    fetch(split * i + k).wait()
            span = pl.ds(pl.multiple_of(i * tile, tile), tile)
            base_ref[span, :] = jnp.dot(
                held[span, :], rows[...], preferred_element_type=jnp.float32
            )

    out_shape = [
        jax.ShapeDtypeStruct((entries, n), jnp.float32),
        jax.ShapeDtypeStruct((depth, n), jnp.bfloat16),
    ]
    if load:
        out_shape.append(jax.ShapeDtypeStruct((entries, depth), jnp.bfloat16))
    return pl.pallas_call(
        kernel,
        out_shape=tuple(out_shape),
        in_specs=[WHOLE, WHOLE, pl.BlockSpec(memory_space=pltpu.HBM) if load else WHOLE],
        out_specs=(WHOLE,) * len(out_shape),
        scratch_shapes=[pltpu.SemaphoreType.DMA((split * tiles,))] * load,
        compiler_params=pltpu.CompilerParams(vmem_limit_bytes=(23 if load else 8) * MIB),
        cost_estimate=pl.CostEstimate(
            flops=2 * n * entries * depth,
            bytes_accessed=2 * entries * depth,
            transcendentals=0,
        ),
        name="base",
    )


def clear(top, total, pick):
    top[...] = jnp.full(top.shape, -1e30, jnp.float32)
    total[...] = jnp.zeros(total.shape, jnp.float32)
    pick[...] = jnp.zeros(pick.shape, jnp.float32)


def project(v_ref, source, into):
    into[...] = jnp.dot(v_ref[...], source[...], preferred_element_type=jnp.float32).astype(
        jnp.bfloat16
    )


def wanted(want_ref, hop, n_voc):
    left, right = sources_of(hop, n_voc)
    return jnp.concatenate([want_ref[left], want_ref[right]], axis=1)


def reduce(x, want, top, total, pick):
    size, n = x.shape
    entry = lax.broadcasted_iota(jnp.int32, (size, n), 0)
    hit = jnp.where(entry == want, x, 0.0)
    x3 = x.reshape(size // 8, 8, n)
    new = jnp.maximum(top[...], jnp.max(x3, axis=0))
    total[...] = total[...] * jnp.exp(top[...] - new) + jnp.sum(jnp.exp(x3 - new[None]), axis=0)
    pick[...] = pick[...] + jnp.sum(hit.reshape(size // 8, 8, n), axis=0)
    top[...] = new


def results(top, total, pick):
    best = jnp.max(top[...], axis=0, keepdims=True)
    sums = jnp.sum(total[...] * jnp.exp(top[...] - best), axis=0, keepdims=True)
    return best, sums, jnp.sum(pick[...], axis=0, keepdims=True)


def state_scratch(rank, n):
    return [pltpu.VMEM((rank, n), jnp.bfloat16)] + [pltpu.VMEM((8, n), jnp.float32)] * 3


def make_ends(r, depth, entries, rank, n_voc):
    tile = tile_rows(entries)
    n = 4 * r

    def kernel(base_a, rows_a, base_b, rows_b, u_ref, v_ref, want_ref, out_a, out_b, *scratch):
        bases = [
            (base_a, wanted(want_ref, 1, n_voc), scratch[:4]),
            (base_b, wanted(want_ref, 2, n_voc), scratch[4:]),
        ]
        for rows, (_, _, (proj, *state)) in zip((rows_a, rows_b), bases):
            project(v_ref, rows, proj)
            clear(*state)

        @pl.loop(0, entries // tile)
        def _(i):
            span = pl.ds(pl.multiple_of(i * tile, tile), tile)
            for base, want, (proj, *state) in bases:
                x = base[span, :] + jnp.dot(
                    u_ref[span, :], proj[...], preferred_element_type=jnp.float32
                )
                reduce(x, want - i * tile, *state)

        for out, (_, _, (proj, *state)) in zip((out_a, out_b), bases):
            for q, value in enumerate(results(*state)):
                out[q : q + 1, :] = value

    return pl.pallas_call(
        kernel,
        out_shape=(jax.ShapeDtypeStruct((3, n), jnp.float32),) * 2,
        in_specs=[WHOLE] * 7,
        out_specs=(WHOLE,) * 2,
        scratch_shapes=state_scratch(rank, n) * 2,
        compiler_params=pltpu.CompilerParams(vmem_limit_bytes=8 * MIB),
        cost_estimate=pl.CostEstimate(
            flops=4 * n * entries * 256,
            bytes_accessed=8 * entries * n,
            transcendentals=2 * n * entries,
        ),
        name="ends",
    )


def make_chunk(hop, pieces, r, depth, entries, rank, n_voc):
    tile = tile_rows(entries)
    sizes = [tile] * (entries // tile - 1) + [tile // 2] * 2
    n = 4 * r
    last = hop == n_voc // 2
    earlier = hop - 1 if last else 0

    def kernel(*refs):
        piece, refs = refs[:pieces], refs[pieces:]
        head_ref, u_ref, v_ref, want_ref, *refs = refs
        before, refs = refs[:earlier], refs[earlier:]
        out_ref, rows, even, odd, proj, *state = refs

        load_rows(rows, piece)
        project(v_ref, rows, proj)
        clear(*state)
        want = wanted(want_ref, hop, n_voc)

        def multiply(start, size, into):
            span = slice(start, start + size)
            into[:size, :] = jnp.dot(
                head_ref[span, :], rows[...], preferred_element_type=jnp.float32
            ) + jnp.dot(u_ref[span, :], proj[...], preferred_element_type=jnp.float32)

        start = 0
        for i, size in enumerate(sizes):
            multiply(start, size, (even, odd)[i % 2])
            if i:
                ahead = sizes[i - 1]
                reduce((even, odd)[(i - 1) % 2][:ahead, :], want - (start - ahead), *state)
            start += size
        reduce((even, odd)[(len(sizes) - 1) % 2][:size, :], want - (start - size), *state)

        for q, value in enumerate(results(*state)):
            if not last:
                out_ref[q : q + 1, :] = value
                continue
            for k, lanes in [(hop, value)] + [
                (k, before[k - 1][q : q + 1, :]) for k in range(1, hop)
            ]:
                left, right = sources_of(k, n_voc)
                out_ref[q, pl.ds(left, 1), :] = lanes[:, : 2 * r]
                out_ref[q, pl.ds(right, 1), :] = lanes[:, 2 * r :]

    return pl.pallas_call(
        kernel,
        out_shape=jax.ShapeDtypeStruct((3, n_voc, 2 * r) if last else (3, n), jnp.float32),
        in_specs=[WHOLE] * (pieces + 4 + earlier),
        out_specs=WHOLE,
        scratch_shapes=[
            pltpu.VMEM((depth, n), jnp.bfloat16),
            pltpu.VMEM((tile, n), jnp.float32),
            pltpu.VMEM((tile, n), jnp.float32),
        ]
        + state_scratch(rank, n),
        compiler_params=pltpu.CompilerParams(vmem_limit_bytes=8 * MIB),
        cost_estimate=pl.CostEstimate(
            flops=2 * n * entries * (depth + 256),
            bytes_accessed=2 * entries * (depth + LANES),
            transcendentals=n * entries,
        ),
        name="chunk",
    )


def make_combine(bits, r, n_voc, finish):
    low = bits & -bits
    count = bits // low + 1

    def kernel(*refs):
        parts, outs, held = refs[:count], refs[count:-1], refs[-1]
        slot = lax.rem(lax.axis_index("vocab") // low, count)
        for k in range(count):
            held[slot ^ k] = parts[k][...]
        top = held[0, 0]
        for k in range(1, count):
            top = jnp.maximum(top, held[k, 0])
        total = held[0, 1] * jnp.exp(held[0, 0] - top)
        pick = held[0, 2]
        for k in range(1, count):
            total = total + held[k, 1] * jnp.exp(held[k, 0] - top)
            pick = pick + held[k, 2]
        if not finish:
            for q, value in enumerate((top, total, pick)):
                outs[0][q] = value
            return
        log_total = top + jnp.log(total)
        for ref, value in zip(outs, (pick - log_total, log_total)):
            for k in range(n_voc):
                for s in range(2):
                    ref[s : s + 1, k * r : (k + 1) * r] = value[k : k + 1, s * r : (s + 1) * r]

    if finish:
        shape = (jax.ShapeDtypeStruct((2, n_voc * r), jnp.float32),) * 2
        specs = (WHOLE, WHOLE)
    else:
        shape, specs = jax.ShapeDtypeStruct((3, n_voc, 2 * r), jnp.float32), WHOLE
    return pl.pallas_call(
        kernel,
        out_shape=shape,
        in_specs=[WHOLE] * count,
        out_specs=specs,
        scratch_shapes=[pltpu.VMEM((count, 3, n_voc, 2 * r), jnp.float32)],
        compiler_params=pltpu.CompilerParams(vmem_limit_bytes=MIB),
        name="combine",
    )


def body(hidden, head, factor_u, factor_v, sampled):
    n_group = lax.axis_size("group")
    n_voc = lax.axis_size("vocab")
    _, r, depth = hidden.shape
    entries = head.shape[0]
    rank = factor_u.shape[1]
    per = n_voc // n_group
    half = n_voc // 2

    order = ring_order(n_voc)
    ahead = [(order[i], order[(i + 1) % n_voc]) for i in range(n_voc)]
    behind = [(b, a) for a, b in ahead]

    def trade(x, axis, size, bit):
        return lax.ppermute(x, axis, [(i, i ^ bit) for i in range(size)])

    u_rows, v_rows = factor_u.shape[0], factor_v.shape[0]
    everyone = [(g, v) for g in range(n_group) for v in range(n_voc)]
    moves = [
        (v * n_group + swapped(g, n_group), g * n_voc + v) for g, v in everyone
    ]
    block = lax.ppermute(factor_u.T, ("group", "vocab"), moves)
    shards = []
    for t in range(per):
        moves = []
        for g, v in everyone:
            z = v // per
            plane = g ^ swapped(z, n_group)
            moves.append((z * n_voc + plane * per + (v % per ^ t), g * n_voc + v))
        shards.append(lax.ppermute(factor_v.T, ("group", "vocab"), moves))

    square = n_voc == 8
    if square:
        def before(x):
            return lax.ppermute(x, "vocab", [(v, (v + 2) % n_voc) for v in range(n_voc)])

        def after(x):
            return lax.ppermute(x, "vocab", [(v, (v - 2) % n_voc) for v in range(n_voc)])

        a, b, c = before(hidden), after(hidden), trade(hidden, "vocab", n_voc, 1)
        a, b, c = lax.optimization_barrier((a, b, c))
        a2, b2, c2 = before(c), after(b), trade(b, "vocab", n_voc, 1)
        first, second = (hidden, a), (b, c)
    else:
        up = [hidden, lax.ppermute(hidden, "vocab", behind)]
        down = [hidden, lax.ppermute(hidden, "vocab", ahead)]
        up.append(lax.ppermute(up[1], "vocab", behind))
        down.append(lax.ppermute(down[1], "vocab", ahead))
        first, second = (up[1], hidden), (up[2], down[1])
    base, base_rows, head = make_base(r, depth, entries, True)(*first, head)
    base, block, *shards = lax.optimization_barrier((base, block, *shards))
    held = [base, base_rows]
    gap = ((0, 0), (0, padded(v_rows) - v_rows))
    pack = jnp.concatenate([block] + [jnp.pad(x, gap) for x in shards], axis=1)
    packs = {0: pack}
    near = [1 << k for k in reversed(range(n_group.bit_length() - 1))]
    for bit in near:
        packs[bit] = trade(pack, "group", n_group, bit)
    if square:
        b, c, a2, b2, c2, held[0] = lax.optimization_barrier((b, c, a2, b2, c2, held[0]))
        second = b, c
        opposite = [after(c2[0]), before(a2[1])]
    else:
        down[2], held[0] = lax.optimization_barrier((down[2], held[0]))
        up[2], held[0] = lax.optimization_barrier((up[2], held[0]))
        second = (up[2], down[1])
    held += make_base(r, depth, entries, False)(*second, head)
    held[2], *crossed = lax.optimization_barrier((held[2], *[packs[bit] for bit in near]))
    packs.update(zip(near, crossed))

    if not square:
        up.append(lax.ppermute(up[2], "vocab", behind))
        down.append(lax.ppermute(down[2], "vocab", ahead))
    for k in range(n_group):
        if k not in packs:
            packs[k] = trade(packs[k & (k - 1)], "group", n_group, k & -k)
    full_u, full_v, want = make_assemble(
        n_group, n_voc, u_rows, v_rows, rank, r, entries
    )(sampled, *[packs[k] for k in range(n_group)])
    stats = list(make_ends(r, depth, entries, rank, n_voc)(*held, full_u, full_v, want))
    if square:
        chunk = make_chunk(3, 2, r, depth, entries, rank, n_voc)
        stats.append(chunk(a2, b2, head, full_u, full_v, want))
        final = c2
    else:
        down[3], stats[0] = lax.optimization_barrier((down[3], stats[0]))
        up[3], stats[0] = lax.optimization_barrier((up[3], stats[0]))
        for hop in range(3, half):
            if hop + 1 < half:
                up.append(lax.ppermute(up[hop], "vocab", behind))
                down.append(lax.ppermute(down[hop], "vocab", ahead))
            else:
                opposite = [
                    lax.ppermute(up[hop][0], "vocab", behind),
                    lax.ppermute(down[hop][1], "vocab", ahead),
                ]
            chunk = make_chunk(hop, 2, r, depth, entries, rank, n_voc)
            stats.append(chunk(up[hop], down[hop - 1], head, full_u, full_v, want))
            if hop + 1 < half:
                down[-1], stats[-1] = lax.optimization_barrier((down[-1], stats[-1]))
                up[-1], stats[-1] = lax.optimization_barrier((up[-1], stats[-1]))
        final = down[half - 1]
    chunk = make_chunk(half, 3, r, depth, entries, rank, n_voc)
    stats.append(chunk(*opposite, final, head, full_u, full_v, want, *stats))
    part = stats[-1]
    low = 1
    while low < n_voc:
        count = 2 if low == 1 else min(4, n_voc // low)
        bits = low * (count - 1)
        others = [trade(part, "vocab", n_voc, low * k) for k in range(1, count)]
        part = make_combine(bits, r, n_voc, low * count == n_voc)(part, *others)
        low *= count
    return part


def solution(mesh):
    in_specs = (
        P(None, ("group", "vocab"), None),
        P("vocab", None),
        P(("group", "vocab"), None),
        P("vocab", None),
        P(None, "group"),
    )
    out_specs = (P(None, "group"), P(None, "group"))
    return jax.shard_map(body, mesh=mesh, in_specs=in_specs, out_specs=out_specs, check_vma=False)
```

```python
import jax
import jax.numpy as jnp
from jax import lax
from jax.experimental import pallas as pl
from jax.experimental.pallas import tpu as pltpu
from jax.sharding import PartitionSpec as P

MIB = 1024 * 1024
LANES = 128
WHOLE = pl.BlockSpec(memory_space=pltpu.VMEM)


def ring_order(n):
    return [2 * i for i in range(n // 2)] + [2 * i + 1 for i in reversed(range(n // 2))]


def swapped(member, n_group):
    return member // 2 + member % 2 * (n_group // 2)


def ring_position(device, n):
    return jnp.where(device % 2 == 0, device // 2, n - 1 - device // 2)


def ring_device(position, n):
    position = lax.rem(position + n, n)
    return jnp.where(position < n // 2, 2 * position, 2 * (n - 1 - position) + 1)


def tile_rows(entries):
    for rows in (1024, 512, 256, 128, 64, 32, 16):
        if entries % (2 * rows) == 0:
            return rows
    raise ValueError(entries)


def padded(size):
    return -(-size // LANES) * LANES


def make_assemble(n_group, n_voc, u_rows, v_rows, rank, r, entries):
    per = n_voc // n_group
    wide = padded(v_rows)

    def kernel(sampled_ref, *refs):
        packs = refs[:n_group]
        u_out, v_out, want_out, v_wide = refs[n_group:]
        group = lax.axis_index("group")
        voc = lax.axis_index("vocab")
        for k in range(n_group):
            member = group ^ k
            plane = member ^ swapped(voc // per, n_group)
            block = swapped(member, n_group)
            start = pl.multiple_of(block * u_rows, u_rows)
            u_out[pl.ds(start, u_rows), :] = packs[k][:, :u_rows].T
            for t in range(per):
                shard = plane * per + (lax.rem(voc, per) ^ t)
                at = u_rows + t * wide
                rows = packs[k][:, at : at + wide].astype(jnp.float32).T
                v_wide[pl.ds(pl.multiple_of(shard * v_rows, 8), v_rows), :] = rows[:v_rows]
        v_out[...] = v_wide[...].T.astype(jnp.bfloat16)
        for k in range(n_voc):
            for s in range(2):
                want_out[k, :, s * r : (s + 1) * r] = (
                    sampled_ref[s : s + 1, k * r : (k + 1) * r] - voc * entries
                )

    return pl.pallas_call(
        kernel,
        out_shape=(
            jax.ShapeDtypeStruct((n_group * u_rows, rank), jnp.bfloat16),
            jax.ShapeDtypeStruct((rank, n_voc * v_rows), jnp.bfloat16),
            jax.ShapeDtypeStruct((n_voc, 1, 2 * r), jnp.int32),
        ),
        in_specs=[WHOLE] * (1 + n_group),
        out_specs=(WHOLE,) * 3,
        scratch_shapes=[pltpu.VMEM((n_voc * v_rows, rank), jnp.float32)],
        compiler_params=pltpu.CompilerParams(vmem_limit_bytes=4 * MIB),
        name="assemble",
    )


def sources_of(hop, n_voc):
    position = ring_position(lax.axis_index("vocab"), n_voc)
    return ring_device(position + hop, n_voc), ring_device(position - hop + 1, n_voc)


def load_rows(rows, pieces):
    blocks = [ref[...].reshape(-1, ref.shape[-1]) for ref in pieces]
    rows[...] = jnp.concatenate(blocks, axis=0).T


def make_base(r, depth, entries, load):
    n = 4 * r
    tile = tile_rows(entries)
    tiles = entries // tile
    split = 2 if tile % 32 == 0 else 1
    part = tile // split

    def kernel(up_ref, down_ref, head_ref, base_ref, rows, *refs):
        held = head_ref
        if load:
            held, sems = refs

        def fetch(t):
            span = pl.ds(pl.multiple_of(t * part, part), part)
            return pltpu.make_async_copy(head_ref.at[span, :], held.at[span, :], sems.at[t])

        if load:
            for t in range(split * tiles):
                fetch(t).start(priority=t % 2)
        load_rows(rows, (up_ref, down_ref))

        @pl.loop(0, tiles)
        def _(i):
            if load:
                for k in range(split):
                    fetch(split * i + k).wait()
            span = pl.ds(pl.multiple_of(i * tile, tile), tile)
            base_ref[span, :] = jnp.dot(
                held[span, :], rows[...], preferred_element_type=jnp.float32
            )

    out_shape = [
        jax.ShapeDtypeStruct((entries, n), jnp.float32),
        jax.ShapeDtypeStruct((depth, n), jnp.bfloat16),
    ]
    if load:
        out_shape.append(jax.ShapeDtypeStruct((entries, depth), jnp.bfloat16))
    return pl.pallas_call(
        kernel,
        out_shape=tuple(out_shape),
        in_specs=[WHOLE, WHOLE, pl.BlockSpec(memory_space=pltpu.HBM) if load else WHOLE],
        out_specs=(WHOLE,) * len(out_shape),
        scratch_shapes=[pltpu.SemaphoreType.DMA((split * tiles,))] * load,
        compiler_params=pltpu.CompilerParams(vmem_limit_bytes=(23 if load else 8) * MIB),
        cost_estimate=pl.CostEstimate(
            flops=2 * n * entries * depth,
            bytes_accessed=2 * entries * depth,
            transcendentals=0,
        ),
        name="base",
    )


def clear(top, total, pick):
    top[...] = jnp.full(top.shape, -1e30, jnp.float32)
    total[...] = jnp.zeros(total.shape, jnp.float32)
    pick[...] = jnp.zeros(pick.shape, jnp.float32)


def project(v_ref, source, into):
    into[...] = jnp.dot(v_ref[...], source[...], preferred_element_type=jnp.float32).astype(
        jnp.bfloat16
    )


def wanted(want_ref, hop, n_voc):
    left, right = sources_of(hop, n_voc)
    return jnp.concatenate([want_ref[left], want_ref[right]], axis=1)


def reduce(x, want, top, total, pick):
    size, n = x.shape
    entry = lax.broadcasted_iota(jnp.int32, (size, n), 0)
    hit = jnp.where(entry == want, x, 0.0)
    x3 = x.reshape(size // 8, 8, n)
    new = jnp.maximum(top[...], jnp.max(x3, axis=0))
    total[...] = total[...] * jnp.exp(top[...] - new) + jnp.sum(jnp.exp(x3 - new[None]), axis=0)
    pick[...] = pick[...] + jnp.sum(hit.reshape(size // 8, 8, n), axis=0)
    top[...] = new


def results(top, total, pick):
    best = jnp.max(top[...], axis=0, keepdims=True)
    sums = jnp.sum(total[...] * jnp.exp(top[...] - best), axis=0, keepdims=True)
    return best, sums, jnp.sum(pick[...], axis=0, keepdims=True)


def state_scratch(rank, n):
    return [pltpu.VMEM((rank, n), jnp.bfloat16)] + [pltpu.VMEM((8, n), jnp.float32)] * 3


def make_ends(r, depth, entries, rank, n_voc):
    tile = tile_rows(entries)
    n = 4 * r

    def kernel(base_a, rows_a, base_b, rows_b, u_ref, v_ref, want_ref, out_a, out_b, *scratch):
        bases = [
            (base_a, wanted(want_ref, 1, n_voc), scratch[:4]),
            (base_b, wanted(want_ref, 2, n_voc), scratch[4:]),
        ]
        for rows, (_, _, (proj, *state)) in zip((rows_a, rows_b), bases):
            project(v_ref, rows, proj)
            clear(*state)

        @pl.loop(0, entries // tile)
        def _(i):
            span = pl.ds(pl.multiple_of(i * tile, tile), tile)
            for base, want, (proj, *state) in bases:
                x = base[span, :] + jnp.dot(
                    u_ref[span, :], proj[...], preferred_element_type=jnp.float32
                )
                reduce(x, want - i * tile, *state)

        for out, (_, _, (proj, *state)) in zip((out_a, out_b), bases):
            for q, value in enumerate(results(*state)):
                out[q : q + 1, :] = value

    return pl.pallas_call(
        kernel,
        out_shape=(jax.ShapeDtypeStruct((3, n), jnp.float32),) * 2,
        in_specs=[WHOLE] * 7,
        out_specs=(WHOLE,) * 2,
        scratch_shapes=state_scratch(rank, n) * 2,
        compiler_params=pltpu.CompilerParams(vmem_limit_bytes=8 * MIB),
        cost_estimate=pl.CostEstimate(
            flops=4 * n * entries * 256,
            bytes_accessed=8 * entries * n,
            transcendentals=2 * n * entries,
        ),
        name="ends",
    )


def make_chunk(hop, pieces, r, depth, entries, rank, n_voc):
    tile = tile_rows(entries)
    sizes = [tile] * (entries // tile - 1) + [tile // 2, tile // 4, tile // 4]
    n = 4 * r
    last = hop == n_voc // 2
    earlier = hop - 1 if last else 0

    def kernel(*refs):
        piece, refs = refs[:pieces], refs[pieces:]
        head_ref, u_ref, v_ref, want_ref, *refs = refs
        before, refs = refs[:earlier], refs[earlier:]
        out_ref, rows, even, odd, proj, *state = refs

        load_rows(rows, piece)
        project(v_ref, rows, proj)
        clear(*state)
        want = wanted(want_ref, hop, n_voc)

        def multiply(start, size, into):
            span = slice(start, start + size)
            into[:size, :] = jnp.dot(
                head_ref[span, :], rows[...], preferred_element_type=jnp.float32
            ) + jnp.dot(u_ref[span, :], proj[...], preferred_element_type=jnp.float32)

        start = 0
        for i, size in enumerate(sizes):
            multiply(start, size, (even, odd)[i % 2])
            if i:
                ahead = sizes[i - 1]
                reduce((even, odd)[(i - 1) % 2][:ahead, :], want - (start - ahead), *state)
            start += size
        reduce((even, odd)[(len(sizes) - 1) % 2][:size, :], want - (start - size), *state)

        for q, value in enumerate(results(*state)):
            if not last:
                out_ref[q : q + 1, :] = value
                continue
            for k, lanes in [(hop, value)] + [
                (k, before[k - 1][q : q + 1, :]) for k in range(1, hop)
            ]:
                left, right = sources_of(k, n_voc)
                out_ref[q, pl.ds(left, 1), :] = lanes[:, : 2 * r]
                out_ref[q, pl.ds(right, 1), :] = lanes[:, 2 * r :]

    return pl.pallas_call(
        kernel,
        out_shape=jax.ShapeDtypeStruct((3, n_voc, 2 * r) if last else (3, n), jnp.float32),
        in_specs=[WHOLE] * (pieces + 4 + earlier),
        out_specs=WHOLE,
        scratch_shapes=[
            pltpu.VMEM((depth, n), jnp.bfloat16),
            pltpu.VMEM((tile, n), jnp.float32),
            pltpu.VMEM((tile, n), jnp.float32),
        ]
        + state_scratch(rank, n),
        compiler_params=pltpu.CompilerParams(vmem_limit_bytes=8 * MIB),
        cost_estimate=pl.CostEstimate(
            flops=2 * n * entries * (depth + 256),
            bytes_accessed=2 * entries * (depth + LANES),
            transcendentals=n * entries,
        ),
        name="chunk",
    )


def make_combine(bits, r, n_voc, finish):
    low = bits & -bits
    count = bits // low + 1

    def kernel(*refs):
        parts, outs, held = refs[:count], refs[count:-1], refs[-1]
        slot = lax.rem(lax.axis_index("vocab") // low, count)
        for k in range(count):
            held[slot ^ k] = parts[k][...]
        top = held[0, 0]
        for k in range(1, count):
            top = jnp.maximum(top, held[k, 0])
        total = held[0, 1] * jnp.exp(held[0, 0] - top)
        pick = held[0, 2]
        for k in range(1, count):
            total = total + held[k, 1] * jnp.exp(held[k, 0] - top)
            pick = pick + held[k, 2]
        if not finish:
            for q, value in enumerate((top, total, pick)):
                outs[0][q] = value
            return
        log_total = top + jnp.log(total)
        for ref, value in zip(outs, (pick - log_total, log_total)):
            for k in range(n_voc):
                for s in range(2):
                    ref[s : s + 1, k * r : (k + 1) * r] = value[k : k + 1, s * r : (s + 1) * r]

    if finish:
        shape = (jax.ShapeDtypeStruct((2, n_voc * r), jnp.float32),) * 2
        specs = (WHOLE, WHOLE)
    else:
        shape, specs = jax.ShapeDtypeStruct((3, n_voc, 2 * r), jnp.float32), WHOLE
    return pl.pallas_call(
        kernel,
        out_shape=shape,
        in_specs=[WHOLE] * count,
        out_specs=specs,
        scratch_shapes=[pltpu.VMEM((count, 3, n_voc, 2 * r), jnp.float32)],
        compiler_params=pltpu.CompilerParams(vmem_limit_bytes=MIB),
        name="combine",
    )


def body(hidden, head, factor_u, factor_v, sampled):
    n_group = lax.axis_size("group")
    n_voc = lax.axis_size("vocab")
    _, r, depth = hidden.shape
    entries = head.shape[0]
    rank = factor_u.shape[1]
    per = n_voc // n_group
    half = n_voc // 2

    order = ring_order(n_voc)
    ahead = [(order[i], order[(i + 1) % n_voc]) for i in range(n_voc)]
    behind = [(b, a) for a, b in ahead]

    def trade(x, axis, size, bit):
        return lax.ppermute(x, axis, [(i, i ^ bit) for i in range(size)])

    u_rows, v_rows = factor_u.shape[0], factor_v.shape[0]
    everyone = [(g, v) for g in range(n_group) for v in range(n_voc)]
    moves = [
        (v * n_group + swapped(g, n_group), g * n_voc + v) for g, v in everyone
    ]
    block = lax.ppermute(factor_u.T, ("group", "vocab"), moves)
    shards = []
    for t in range(per):
        moves = []
        for g, v in everyone:
            z = v // per
            plane = g ^ swapped(z, n_group)
            moves.append((z * n_voc + plane * per + (v % per ^ t), g * n_voc + v))
        shards.append(lax.ppermute(factor_v.T, ("group", "vocab"), moves))

    up = [hidden, lax.ppermute(hidden, "vocab", behind)]
    down = [hidden, lax.ppermute(hidden, "vocab", ahead)]
    up.append(lax.ppermute(up[1], "vocab", behind))
    down.append(lax.ppermute(down[1], "vocab", ahead))
    base, base_rows, head = make_base(r, depth, entries, True)(up[1], hidden, head)
    base, block, *shards = lax.optimization_barrier((base, block, *shards))
    held = [base, base_rows]
    gap = ((0, 0), (0, padded(v_rows) - v_rows))
    pack = jnp.concatenate([block] + [jnp.pad(x, gap) for x in shards], axis=1)
    packs = {0: pack}
    near = [1 << k for k in reversed(range(n_group.bit_length() - 1))]
    for bit in near:
        packs[bit] = trade(pack, "group", n_group, bit)
    down[2], held[0] = lax.optimization_barrier((down[2], held[0]))
    up[2], held[0] = lax.optimization_barrier((up[2], held[0]))
    held += make_base(r, depth, entries, False)(up[2], down[1], head)
    held[2], *crossed = lax.optimization_barrier((held[2], *[packs[bit] for bit in near]))
    packs.update(zip(near, crossed))

    up.append(lax.ppermute(up[2], "vocab", behind))
    down.append(lax.ppermute(down[2], "vocab", ahead))
    for k in range(n_group):
        if k not in packs:
            packs[k] = trade(packs[k & (k - 1)], "group", n_group, k & -k)
    full_u, full_v, want = make_assemble(
        n_group, n_voc, u_rows, v_rows, rank, r, entries
    )(sampled, *[packs[k] for k in range(n_group)])
    stats = list(make_ends(r, depth, entries, rank, n_voc)(*held, full_u, full_v, want))
    down[3], stats[0] = lax.optimization_barrier((down[3], stats[0]))
    up[3], stats[0] = lax.optimization_barrier((up[3], stats[0]))

    for hop in range(3, half):
        if hop + 1 < half:
            up.append(lax.ppermute(up[hop], "vocab", behind))
            down.append(lax.ppermute(down[hop], "vocab", ahead))
        else:
            opposite = [
                lax.ppermute(up[hop][0], "vocab", behind),
                lax.ppermute(down[hop][1], "vocab", ahead),
            ]
        chunk = make_chunk(hop, 2, r, depth, entries, rank, n_voc)
        stats.append(chunk(up[hop], down[hop - 1], head, full_u, full_v, want))
        if hop + 1 < half:
            down[-1], stats[-1] = lax.optimization_barrier((down[-1], stats[-1]))
            up[-1], stats[-1] = lax.optimization_barrier((up[-1], stats[-1]))
    chunk = make_chunk(half, 3, r, depth, entries, rank, n_voc)
    stats.append(chunk(*opposite, down[half - 1], head, full_u, full_v, want, *stats))
    part = stats[-1]
    low = 1
    while low < n_voc:
        count = 2 if low == 1 else min(4, n_voc // low)
        bits = low * (count - 1)
        others = [trade(part, "vocab", n_voc, low * k) for k in range(1, count)]
        part = make_combine(bits, r, n_voc, low * count == n_voc)(part, *others)
        low *= count
    return part


def solution(mesh):
    in_specs = (
        P(None, ("group", "vocab"), None),
        P("vocab", None),
        P(("group", "vocab"), None),
        P("vocab", None),
        P(None, "group"),
    )
    out_specs = (P(None, "group"), P(None, "group"))
    return jax.shard_map(body, mesh=mesh, in_specs=in_specs, out_specs=out_specs, check_vma=False)
```

```python
import jax
import jax.numpy as jnp
from jax import lax
from jax.experimental import pallas as pl
from jax.experimental.pallas import tpu as pltpu
from jax.sharding import PartitionSpec as P

MIB = 1024 * 1024
LANES = 128
WHOLE = pl.BlockSpec(memory_space=pltpu.VMEM)


def ring_order(n):
    return [2 * i for i in range(n // 2)] + [2 * i + 1 for i in reversed(range(n // 2))]


def swapped(member, n_group):
    return member // 2 + member % 2 * (n_group // 2)


def ring_position(device, n):
    return jnp.where(device % 2 == 0, device // 2, n - 1 - device // 2)


def ring_device(position, n):
    position = lax.rem(position + n, n)
    return jnp.where(position < n // 2, 2 * position, 2 * (n - 1 - position) + 1)


def tile_rows(entries):
    for rows in (1024, 512, 256, 128, 64, 32, 16):
        if entries % (2 * rows) == 0:
            return rows
    raise ValueError(entries)


def padded(size):
    return -(-size // LANES) * LANES


def make_assemble(n_group, n_voc, u_rows, v_rows, rank, r, entries):
    per = n_voc // n_group
    wide = padded(v_rows)

    def kernel(sampled_ref, *refs):
        packs = refs[:n_group]
        u_out, v_out, want_out, v_wide = refs[n_group:]
        group = lax.axis_index("group")
        voc = lax.axis_index("vocab")
        for k in range(n_group):
            member = group ^ k
            plane = member ^ swapped(voc // per, n_group)
            block = swapped(member, n_group)
            start = pl.multiple_of(block * u_rows, u_rows)
            u_out[pl.ds(start, u_rows), :] = packs[k][:, :u_rows].T
            for t in range(per):
                shard = plane * per + (lax.rem(voc, per) ^ t)
                at = u_rows + t * wide
                rows = packs[k][:, at : at + wide].astype(jnp.float32).T
                v_wide[pl.ds(pl.multiple_of(shard * v_rows, 8), v_rows), :] = rows[:v_rows]
        v_out[...] = v_wide[...].T.astype(jnp.bfloat16)
        for k in range(n_voc):
            for s in range(2):
                want_out[k, :, s * r : (s + 1) * r] = (
                    sampled_ref[s : s + 1, k * r : (k + 1) * r] - voc * entries
                )

    return pl.pallas_call(
        kernel,
        out_shape=(
            jax.ShapeDtypeStruct((n_group * u_rows, rank), jnp.bfloat16),
            jax.ShapeDtypeStruct((rank, n_voc * v_rows), jnp.bfloat16),
            jax.ShapeDtypeStruct((n_voc, 1, 2 * r), jnp.int32),
        ),
        in_specs=[WHOLE] * (1 + n_group),
        out_specs=(WHOLE,) * 3,
        scratch_shapes=[pltpu.VMEM((n_voc * v_rows, rank), jnp.float32)],
        compiler_params=pltpu.CompilerParams(vmem_limit_bytes=4 * MIB),
        name="assemble",
    )


def sources_of(hop, n_voc):
    position = ring_position(lax.axis_index("vocab"), n_voc)
    return ring_device(position + hop, n_voc), ring_device(position - hop + 1, n_voc)


def load_rows(rows, pieces):
    blocks = [ref[...].reshape(-1, ref.shape[-1]) for ref in pieces]
    rows[...] = jnp.concatenate(blocks, axis=0).T


def make_base(r, depth, entries, load):
    n = 4 * r
    tile = tile_rows(entries)
    tiles = entries // tile
    split = 2 if tile % 32 == 0 else 1
    part = tile // split

    def kernel(up_ref, down_ref, head_ref, base_ref, rows, *refs):
        held = head_ref
        if load:
            held, sems = refs

        def fetch(t):
            span = pl.ds(pl.multiple_of(t * part, part), part)
            return pltpu.make_async_copy(head_ref.at[span, :], held.at[span, :], sems.at[t])

        if load:
            for t in range(split * tiles):
                fetch(t).start(priority=t % 2)
        load_rows(rows, (up_ref, down_ref))

        @pl.loop(0, tiles)
        def _(i):
            if load:
                for k in range(split):
                    fetch(split * i + k).wait()
            span = pl.ds(pl.multiple_of(i * tile, tile), tile)
            base_ref[span, :] = jnp.dot(
                held[span, :], rows[...], preferred_element_type=jnp.float32
            )

    out_shape = [
        jax.ShapeDtypeStruct((entries, n), jnp.float32),
        jax.ShapeDtypeStruct((depth, n), jnp.bfloat16),
    ]
    if load:
        out_shape.append(jax.ShapeDtypeStruct((entries, depth), jnp.bfloat16))
    return pl.pallas_call(
        kernel,
        out_shape=tuple(out_shape),
        in_specs=[WHOLE, WHOLE, pl.BlockSpec(memory_space=pltpu.HBM) if load else WHOLE],
        out_specs=(WHOLE,) * len(out_shape),
        scratch_shapes=[pltpu.SemaphoreType.DMA((split * tiles,))] * load,
        compiler_params=pltpu.CompilerParams(vmem_limit_bytes=(23 if load else 8) * MIB),
        cost_estimate=pl.CostEstimate(
            flops=2 * n * entries * depth,
            bytes_accessed=2 * entries * depth,
            transcendentals=0,
        ),
        name="base",
    )


def clear(top, total, pick):
    top[...] = jnp.full(top.shape, -1e30, jnp.float32)
    total[...] = jnp.zeros(total.shape, jnp.float32)
    pick[...] = jnp.zeros(pick.shape, jnp.float32)


def project(v_ref, source, into):
    into[...] = jnp.dot(v_ref[...], source[...], preferred_element_type=jnp.float32).astype(
        jnp.bfloat16
    )


def wanted(want_ref, hop, n_voc):
    left, right = sources_of(hop, n_voc)
    return jnp.concatenate([want_ref[left], want_ref[right]], axis=1)


def reduce(x, want, top, total, pick):
    size, n = x.shape
    entry = lax.broadcasted_iota(jnp.int32, (size, n), 0)
    hit = jnp.where(entry == want, x, 0.0)
    x3 = x.reshape(size // 8, 8, n)
    new = jnp.maximum(top[...], jnp.max(x3, axis=0))
    total[...] = total[...] * jnp.exp(top[...] - new) + jnp.sum(jnp.exp(x3 - new[None]), axis=0)
    pick[...] = pick[...] + jnp.sum(hit.reshape(size // 8, 8, n), axis=0)
    top[...] = new


def results(top, total, pick):
    best = jnp.max(top[...], axis=0, keepdims=True)
    sums = jnp.sum(total[...] * jnp.exp(top[...] - best), axis=0, keepdims=True)
    return best, sums, jnp.sum(pick[...], axis=0, keepdims=True)


def state_scratch(rank, n):
    return [pltpu.VMEM((rank, n), jnp.bfloat16)] + [pltpu.VMEM((8, n), jnp.float32)] * 3


def make_ends(r, depth, entries, rank, n_voc):
    tile = tile_rows(entries)
    n = 4 * r

    def kernel(base_a, rows_a, base_b, rows_b, u_ref, v_ref, want_ref, out_a, out_b, *scratch):
        bases = [
            (base_a, wanted(want_ref, 1, n_voc), scratch[:4]),
            (base_b, wanted(want_ref, 2, n_voc), scratch[4:]),
        ]
        for rows, (_, _, (proj, *state)) in zip((rows_a, rows_b), bases):
            project(v_ref, rows, proj)
            clear(*state)

        @pl.loop(0, entries // tile)
        def _(i):
            span = pl.ds(pl.multiple_of(i * tile, tile), tile)
            for base, want, (proj, *state) in bases:
                x = base[span, :] + jnp.dot(
                    u_ref[span, :], proj[...], preferred_element_type=jnp.float32
                )
                reduce(x, want - i * tile, *state)

        for out, (_, _, (proj, *state)) in zip((out_a, out_b), bases):
            for q, value in enumerate(results(*state)):
                out[q : q + 1, :] = value

    return pl.pallas_call(
        kernel,
        out_shape=(jax.ShapeDtypeStruct((3, n), jnp.float32),) * 2,
        in_specs=[WHOLE] * 7,
        out_specs=(WHOLE,) * 2,
        scratch_shapes=state_scratch(rank, n) * 2,
        compiler_params=pltpu.CompilerParams(vmem_limit_bytes=8 * MIB),
        cost_estimate=pl.CostEstimate(
            flops=4 * n * entries * 256,
            bytes_accessed=8 * entries * n,
            transcendentals=2 * n * entries,
        ),
        name="ends",
    )


def make_chunk(hop, pieces, r, depth, entries, rank, n_voc):
    tile = tile_rows(entries)
    sizes = [tile] * (entries // tile - 1) + [tile // 2] * 2
    if len(sizes) > 3:
        sizes[:2] = [2 * tile]
    n = 4 * r
    last = hop == n_voc // 2
    earlier = hop - 1 if last else 0

    def kernel(*refs):
        piece, refs = refs[:pieces], refs[pieces:]
        head_ref, u_ref, v_ref, want_ref, *refs = refs
        before, refs = refs[:earlier], refs[earlier:]
        out_ref, rows, even, odd, proj, *state = refs

        load_rows(rows, piece)
        project(v_ref, rows, proj)
        clear(*state)
        want = wanted(want_ref, hop, n_voc)

        def multiply(start, size, into):
            span = slice(start, start + size)
            into[:size, :] = jnp.dot(
                head_ref[span, :], rows[...], preferred_element_type=jnp.float32
            ) + jnp.dot(u_ref[span, :], proj[...], preferred_element_type=jnp.float32)

        start = 0
        for i, size in enumerate(sizes):
            multiply(start, size, (even, odd)[i % 2])
            if i:
                ahead = sizes[i - 1]
                reduce((even, odd)[(i - 1) % 2][:ahead, :], want - (start - ahead), *state)
            start += size
        reduce((even, odd)[(len(sizes) - 1) % 2][:size, :], want - (start - size), *state)

        for q, value in enumerate(results(*state)):
            if not last:
                out_ref[q : q + 1, :] = value
                continue
            for k, lanes in [(hop, value)] + [
                (k, before[k - 1][q : q + 1, :]) for k in range(1, hop)
            ]:
                left, right = sources_of(k, n_voc)
                out_ref[q, pl.ds(left, 1), :] = lanes[:, : 2 * r]
                out_ref[q, pl.ds(right, 1), :] = lanes[:, 2 * r :]

    return pl.pallas_call(
        kernel,
        out_shape=jax.ShapeDtypeStruct((3, n_voc, 2 * r) if last else (3, n), jnp.float32),
        in_specs=[WHOLE] * (pieces + 4 + earlier),
        out_specs=WHOLE,
        scratch_shapes=[
            pltpu.VMEM((depth, n), jnp.bfloat16),
            pltpu.VMEM((max(sizes[::2]), n), jnp.float32),
            pltpu.VMEM((max(sizes[1::2]), n), jnp.float32),
        ]
        + state_scratch(rank, n),
        compiler_params=pltpu.CompilerParams(vmem_limit_bytes=12 * MIB),
        cost_estimate=pl.CostEstimate(
            flops=2 * n * entries * (depth + 256),
            bytes_accessed=2 * entries * (depth + LANES),
            transcendentals=n * entries,
        ),
        name="chunk",
    )


def make_combine(bits, r, n_voc, finish):
    low = bits & -bits
    count = bits // low + 1

    def kernel(*refs):
        parts, outs, held = refs[:count], refs[count:-1], refs[-1]
        slot = lax.rem(lax.axis_index("vocab") // low, count)
        for k in range(count):
            held[slot ^ k] = parts[k][...]
        top = held[0, 0]
        for k in range(1, count):
            top = jnp.maximum(top, held[k, 0])
        total = held[0, 1] * jnp.exp(held[0, 0] - top)
        pick = held[0, 2]
        for k in range(1, count):
            total = total + held[k, 1] * jnp.exp(held[k, 0] - top)
            pick = pick + held[k, 2]
        if not finish:
            for q, value in enumerate((top, total, pick)):
                outs[0][q] = value
            return
        log_total = top + jnp.log(total)
        for ref, value in zip(outs, (pick - log_total, log_total)):
            for k in range(n_voc):
                for s in range(2):
                    ref[s : s + 1, k * r : (k + 1) * r] = value[k : k + 1, s * r : (s + 1) * r]

    if finish:
        shape = (jax.ShapeDtypeStruct((2, n_voc * r), jnp.float32),) * 2
        specs = (WHOLE, WHOLE)
    else:
        shape, specs = jax.ShapeDtypeStruct((3, n_voc, 2 * r), jnp.float32), WHOLE
    return pl.pallas_call(
        kernel,
        out_shape=shape,
        in_specs=[WHOLE] * count,
        out_specs=specs,
        scratch_shapes=[pltpu.VMEM((count, 3, n_voc, 2 * r), jnp.float32)],
        compiler_params=pltpu.CompilerParams(vmem_limit_bytes=MIB),
        name="combine",
    )


def body(hidden, head, factor_u, factor_v, sampled):
    n_group = lax.axis_size("group")
    n_voc = lax.axis_size("vocab")
    _, r, depth = hidden.shape
    entries = head.shape[0]
    rank = factor_u.shape[1]
    per = n_voc // n_group
    half = n_voc // 2

    order = ring_order(n_voc)
    ahead = [(order[i], order[(i + 1) % n_voc]) for i in range(n_voc)]
    behind = [(b, a) for a, b in ahead]

    def trade(x, axis, size, bit):
        return lax.ppermute(x, axis, [(i, i ^ bit) for i in range(size)])

    u_rows, v_rows = factor_u.shape[0], factor_v.shape[0]
    everyone = [(g, v) for g in range(n_group) for v in range(n_voc)]
    moves = [
        (v * n_group + swapped(g, n_group), g * n_voc + v) for g, v in everyone
    ]
    block = lax.ppermute(factor_u.T, ("group", "vocab"), moves)
    shards = []
    for t in range(per):
        moves = []
        for g, v in everyone:
            z = v // per
            plane = g ^ swapped(z, n_group)
            moves.append((z * n_voc + plane * per + (v % per ^ t), g * n_voc + v))
        shards.append(lax.ppermute(factor_v.T, ("group", "vocab"), moves))

    up = [hidden, lax.ppermute(hidden, "vocab", behind)]
    down = [hidden, lax.ppermute(hidden, "vocab", ahead)]
    up.append(lax.ppermute(up[1], "vocab", behind))
    down.append(lax.ppermute(down[1], "vocab", ahead))
    base, base_rows, head = make_base(r, depth, entries, True)(up[1], hidden, head)
    base, block, *shards = lax.optimization_barrier((base, block, *shards))
    held = [base, base_rows]
    gap = ((0, 0), (0, padded(v_rows) - v_rows))
    pack = jnp.concatenate([block] + [jnp.pad(x, gap) for x in shards], axis=1)
    packs = {0: pack}
    near = [1 << k for k in reversed(range(n_group.bit_length() - 1))]
    for bit in near:
        packs[bit] = trade(pack, "group", n_group, bit)
    down[2], held[0] = lax.optimization_barrier((down[2], held[0]))
    up[2], held[0] = lax.optimization_barrier((up[2], held[0]))
    held += make_base(r, depth, entries, False)(up[2], down[1], head)
    held[2], *crossed = lax.optimization_barrier((held[2], *[packs[bit] for bit in near]))
    packs.update(zip(near, crossed))

    up.append(lax.ppermute(up[2], "vocab", behind))
    down.append(lax.ppermute(down[2], "vocab", ahead))
    for k in range(n_group):
        if k not in packs:
            packs[k] = trade(packs[k & (k - 1)], "group", n_group, k & -k)
    full_u, full_v, want = make_assemble(
        n_group, n_voc, u_rows, v_rows, rank, r, entries
    )(sampled, *[packs[k] for k in range(n_group)])
    stats = list(make_ends(r, depth, entries, rank, n_voc)(*held, full_u, full_v, want))
    down[3], stats[0] = lax.optimization_barrier((down[3], stats[0]))
    up[3], stats[0] = lax.optimization_barrier((up[3], stats[0]))

    for hop in range(3, half):
        if hop + 1 < half:
            up.append(lax.ppermute(up[hop], "vocab", behind))
            down.append(lax.ppermute(down[hop], "vocab", ahead))
        else:
            opposite = [
                lax.ppermute(up[hop][0], "vocab", behind),
                lax.ppermute(down[hop][1], "vocab", ahead),
            ]
        chunk = make_chunk(hop, 2, r, depth, entries, rank, n_voc)
        stats.append(chunk(up[hop], down[hop - 1], head, full_u, full_v, want))
        if hop + 1 < half:
            down[-1], stats[-1] = lax.optimization_barrier((down[-1], stats[-1]))
            up[-1], stats[-1] = lax.optimization_barrier((up[-1], stats[-1]))
    chunk = make_chunk(half, 3, r, depth, entries, rank, n_voc)
    stats.append(chunk(*opposite, down[half - 1], head, full_u, full_v, want, *stats))
    part = stats[-1]
    low = 1
    while low < n_voc:
        count = 2 if low == 1 else min(4, n_voc // low)
        bits = low * (count - 1)
        others = [trade(part, "vocab", n_voc, low * k) for k in range(1, count)]
        part = make_combine(bits, r, n_voc, low * count == n_voc)(part, *others)
        low *= count
    return part


def solution(mesh):
    in_specs = (
        P(None, ("group", "vocab"), None),
        P("vocab", None),
        P(("group", "vocab"), None),
        P("vocab", None),
        P(None, "group"),
    )
    out_specs = (P(None, "group"), P(None, "group"))
    return jax.shard_map(body, mesh=mesh, in_specs=in_specs, out_specs=out_specs, check_vma=False)
```
